32 devices in a mesh: groups: 2 (over y), ctx: 8 (over z, x), lane: 2 (over core).
Axes of the slice: x: 2, y: 2, z: 4, core: 2. Of those that a mesh axis runs over, the one named last changes fastest.
Arguments:
- pre_conv: bfloat16 [4, 1024, 2560], P(('groups', 'lane'), 'ctx'), parts along dimension 0, as said below
- step_size: float32 [4, 64, 1024], P(('groups', 'lane'), None, 'ctx'), parts along dimension 0, as said below
- lengths: int32 [4, 4], P(('groups', 'lane')), parts along dimension 0, may hold values from 1 to 4, 8 in all within a row
- conv_weight: bfloat16 [4, 2560], replicated, as said below
- conv_bias: bfloat16 [2560], replicated, as said below
- decay_rate: float32 [64], replicated, as said below
- skip_gain: float32 [64], replicated, may hold values from 0.5 to 1.5
Outputs:
- mamba_out: bfloat16 [4, 1024, 2048], P(('groups', 'lane'), 'ctx'), parts along dimension 0
The draws below stay inside these ranges and needn't reach their ends.
There are 2 independent parts, one for each index of `groups`. The reference program is written for one: setup_inputs(seed, part) draws one part's arguments, and reference() takes and returns one part's arrays. A program takes and returns all parts, laid end to end along the dimension named above; an argument that names none is the same for every part. Nothing has to cross between parts.
Inputs may be any that keep to these rules, and one draw needn't show every extreme that they name: Each lane's row of lengths sums to 8; every entry is at least 1. `step_size`: positive step sizes. `decay_rate`: positive rates. `pre_conv`: entries of order one. `conv_weight`: taps of order one. `conv_bias`: entries of order one.
All inputs are finite; a program needn't handle non-finite values.
Results may differ from the reference program's by a relative error of at most 0.0054.
Values may be sent and summed in bfloat16 or wider, within the bound.
No kernel may reach another device: no remote copies, remote signals or barrier semaphores. Data moves between devices by JAX's collectives and lax.ppermute only.
A program may use at most 256 MiB of HBM per device.

```python
import math
import jax
import jax.numpy as jnp
import numpy as np
from jax import lax

HEADS = 64
HEAD_DIM = 32
STATE = 64
BC_GROUPS = 4
KERNEL = 4
BLOCK = 128
PROMPT_LANES = 2
LANE_TOKENS = 1024
PROMPTS = 4
CONV_DIM = 2560
N_CTX = 8


def conv_taps(key):
    return jnp.clip(0.5 * jax.random.normal(key, (KERNEL, CONV_DIM), jnp.float32), -1.2, 1.2)


def draw_pre_conv(key, part):
    key = jax.random.fold_in(key, 3)
    entries = jnp.clip(jax.random.normal(key, (PROMPT_LANES, LANE_TOKENS, CONV_DIM), jnp.float32), -6.0, 6.0)
    return entries.astype(jnp.bfloat16)


def draw_conv_weight(key, part):
    taps = conv_taps(key)
    return taps.astype(jnp.bfloat16)


def draw_conv_bias(key, part):
    taps = conv_taps(key)
    key = jax.random.fold_in(key, 9)
    offset = jax.random.uniform(key, (CONV_DIM,), jnp.float32, -0.1, 0.1)
    return (-0.52 * jnp.sum(taps * taps, axis=0) + offset).astype(jnp.bfloat16)


def draw_step_size(key, part):
    key = jax.random.fold_in(key, 7)
    half_tokens = LANE_TOKENS // 2
    unit = jnp.exp(jax.random.uniform(key, (PROMPT_LANES, HEADS, LANE_TOKENS), jnp.float32, math.log(0.5), math.log(2.0)))
    return (0.65 / math.sqrt(half_tokens) * unit).astype(jnp.float32)


def draw_decay_rate(key, part):
    key = jax.random.fold_in(key, 11)
    key_class, key_rate = jax.random.split(key, 2)
    fast_cut = 8
    fast = jax.random.randint(key_class, (HEADS,), 0, 16) < fast_cut
    spread = jax.random.uniform(key_rate, (HEADS,), jnp.float32, 0.0, 1.0)
    root = math.sqrt(LANE_TOKENS // 2)
    slow_rate = 0.57 * jnp.exp(spread * math.log(3.0)) / root
    fast_rate = 0.028 * jnp.exp(spread * math.log(1.67)) * root
    return jnp.where(fast, fast_rate, slow_rate).astype(jnp.float32)


def length_profile(number_of, total, limit, skew):
    portions = [(1 << 20) // math.isqrt(grade ** skew) + 1 for grade in range(2, number_of + 1)]
    surplus, counts = total - limit - (number_of - 1), [1] * (number_of - 1)
    while surplus > 0:
        candidates = [i for i in range(number_of - 1) if counts[i] < limit]
        mass, budget = sum([portions[i] for i in candidates]), surplus
        for i in candidates:
            addition = min(limit - counts[i], max(1, budget * portions[i] // mass), surplus)
            counts[i] = counts[i] + addition
            surplus = surplus - addition
    return np.array([limit] + counts)


def ragged_sizes(key, count, total, limit, skew):
    if count == 2:
        one = jax.random.randint(key, (), max(1, total - limit), min(limit, total - 1) + 1)
        return jnp.stack([one, total - one])
    sizes = jnp.asarray(length_profile(count, total, limit, skew), jnp.int32)
    couples = (count - 1) // 2
    giver, taker = sizes[1:1 + 2 * couples:2], sizes[2:2 + 2 * couples:2]
    margin = jnp.minimum(giver - 1, limit - taker)
    shifted = jax.random.randint(jax.random.fold_in(key, 1), (couples,), 0, 1 << 20) % (margin + 1)
    sizes = sizes.at[1:1 + 2 * couples:2].set(giver - shifted).at[2:2 + 2 * couples:2].set(taker + shifted)
    return sizes[jax.random.permutation(jax.random.fold_in(key, 2), count)]


def setup_inputs(seed: int = 0, part: int = 0) -> dict:
    key_of = jax.random.split(jax.random.key(seed), 8)
    own_keys = jax.random.split(jax.random.fold_in(key_of[7], part), 8)
    return {
        "pre_conv": draw_pre_conv(jax.random.fold_in(jax.random.fold_in(key_of[7], part), 71), part),
        "step_size": draw_step_size(jax.random.fold_in(jax.random.fold_in(key_of[7], part), 71), part),
        "lengths": jax.vmap(lambda own: ragged_sizes(own, PROMPTS, N_CTX, N_CTX // 2, 2))(jax.random.split(own_keys[2], PROMPT_LANES)).reshape((PROMPT_LANES, PROMPTS)).astype(jnp.int32),
        "conv_weight": draw_conv_weight(jax.random.fold_in(key_of[7], 71), part),
        "conv_bias": draw_conv_bias(jax.random.fold_in(key_of[7], 71), part),
        "decay_rate": draw_decay_rate(jax.random.fold_in(key_of[7], 71), part),
        "skip_gain": jnp.clip(1.0 + 0.1 * jax.random.normal(key_of[6], (HEADS,), jnp.float32), 0.5, 1.5),
    }


def convolve(padded, conv_weight, conv_bias, count_rows):
    total = conv_bias.astype(jnp.float32)[None, :]
    for offset in range(conv_weight.shape[0]):
        total = total + padded[offset:offset + count_rows].astype(jnp.float32) * conv_weight[offset].astype(jnp.float32)[None, :]
    return jax.nn.silu(total).astype(jnp.bfloat16)


def group_terms(values, keys_in, queries, decay_rate, step_rows):
    heads_group = step_rows.shape[0]
    count_rows = step_rows.shape[1]
    values = values.reshape(count_rows, heads_group, -1)
    cumulative = jnp.cumsum(-step_rows * decay_rate[:, None], axis=1)
    scores = jnp.einsum("tn,sn->ts", queries.astype(jnp.float32), keys_in.astype(jnp.float32))
    later = lax.broadcasted_iota(jnp.int32, (count_rows, count_rows), 0)
    earlier = lax.broadcasted_iota(jnp.int32, (count_rows, count_rows), 1)
    spread = jnp.where((later >= earlier)[None], cumulative[:, :, None] - cumulative[:, None, :], -1e30)
    weights = (jnp.exp(spread) * scores[None]).astype(jnp.bfloat16)
    scaled = (values.astype(jnp.float32) * step_rows.T[:, :, None]).astype(jnp.bfloat16)
    diagonal_part = jnp.einsum("hts,shp->thp", weights.astype(jnp.float32), scaled.astype(jnp.float32))
    tail_weight = jnp.exp(cumulative[:, -1:] - cumulative)
    written = (values.astype(jnp.float32) * (step_rows * tail_weight).T[:, :, None]).astype(jnp.bfloat16)
    local_state = jnp.einsum("tn,thp->hpn", keys_in.astype(jnp.float32), written.astype(jnp.float32))
    return diagonal_part, local_state, jnp.exp(cumulative[:, -1]), jnp.exp(cumulative), values


def finish_group(diagonal_part, entry_decay, queries, incoming, values, skip_gain):
    incoming_rounded = lax.optimization_barrier(incoming.astype(jnp.bfloat16)).astype(jnp.float32)
    carried_part = jnp.einsum("tn,hpn->thp", queries.astype(jnp.float32), incoming_rounded)
    carried_part = carried_part * entry_decay.T[:, :, None]
    return diagonal_part + carried_part + skip_gain[None, :, None] * values.astype(jnp.float32)


def reference(pre_conv, step_size, lengths, conv_weight, conv_bias, decay_rate, skip_gain):
    heads_group = HEADS // BC_GROUPS
    block_ids = jnp.arange(N_CTX, dtype=jnp.int32)

    def block_step(carry, inputs):
        trailing_rows, state = carry
        own_rows, step_rows, fresh = inputs
        trailing_rows = jnp.where(fresh, jnp.zeros_like(trailing_rows), trailing_rows)
        incoming = jnp.where(fresh, jnp.zeros_like(state), state)
        convolved = convolve(jnp.concatenate([trailing_rows, own_rows], axis=0), conv_weight, conv_bias, BLOCK)
        values = convolved[:, :HEADS * HEAD_DIM]
        keys_all = convolved[:, HEADS * HEAD_DIM:HEADS * HEAD_DIM + BC_GROUPS * STATE]
        queries_all = convolved[:, HEADS * HEAD_DIM + BC_GROUPS * STATE:]
        results = []
        states = []
        for bc_group in range(BC_GROUPS):
            low = bc_group * heads_group
            high = low + heads_group
            keys_in = keys_all[:, bc_group * STATE:(bc_group + 1) * STATE]
            queries = queries_all[:, bc_group * STATE:(bc_group + 1) * STATE]
            diagonal_part, local_state, block_decay, entry_decay, grouped = group_terms(
                values[:, low * HEAD_DIM:high * HEAD_DIM], keys_in, queries, decay_rate[low:high], step_rows[low:high])
            results.append(finish_group(diagonal_part, entry_decay, queries, incoming[low:high], grouped, skip_gain[low:high]))
            states.append(block_decay[:, None, None] * incoming[low:high] + local_state)
        output = jnp.concatenate(results, axis=1).reshape(BLOCK, HEADS * HEAD_DIM).astype(jnp.bfloat16)
        return (own_rows[BLOCK - KERNEL + 1:], jnp.concatenate(states, axis=0)), output

    output_lanes = []
    for lane_index in range(PROMPT_LANES):
        rows_all = pre_conv[lane_index].reshape(N_CTX, BLOCK, CONV_DIM)
        steps_all = step_size[lane_index].reshape(HEADS, N_CTX, BLOCK).transpose(1, 0, 2)
        sizes_row = lengths[lane_index].astype(jnp.int32)
        starts = (jnp.cumsum(sizes_row) - sizes_row).astype(jnp.int32)
        fresh = jnp.any(starts[None, :] == block_ids[:, None], axis=1)
        initial = (jnp.zeros((KERNEL - 1, CONV_DIM), pre_conv.dtype), jnp.zeros((HEADS, HEAD_DIM, STATE), jnp.float32))
        final_carry, outputs = lax.scan(block_step, initial, (rows_all, steps_all, fresh))
        output_lanes.append(outputs.reshape(LANE_TOKENS, HEADS * HEAD_DIM))
    return jnp.stack(output_lanes, axis=0)
```

```python
import jax
import jax.numpy as jnp
from jax import lax
from jax.experimental import pallas as pl
from jax.experimental.pallas import tpu as pltpu
from jax.sharding import PartitionSpec as P

HEADS = 64
HEAD_DIM = 32
STATE = 64
BC_GROUPS = 4
HEADS_GROUP = HEADS // BC_GROUPS
VALUES = HEADS * HEAD_DIM
WIDE = HEADS_GROUP * HEAD_DIM
STATE_ROWS = BC_GROUPS * STATE
TAIL_AT = STATE_ROWS
HEAD_AT = TAIL_AT + 16
SCALE_AT = HEAD_AT + 16
FIRST_ROWS = SCALE_AT + 16
SECOND_ROWS = STATE_ROWS + 16
LOG2E = 1.4426950408889634
VMEM = pl.BlockSpec(memory_space=pltpu.VMEM)
SMEM = pl.BlockSpec(memory_space=pltpu.SMEM)
f32 = jnp.float32
bf16 = jnp.bfloat16


def iota(shape, dim):
    return lax.broadcasted_iota(jnp.int32, shape, dim)


def dot(a, b, contract=((1,), (0,)), precision=None):
    return lax.dot_general(
        a, b, (contract, ((), ())), preferred_element_type=f32, precision=precision
    )


def is_fresh(lengths_ref, position):
    found = jnp.int32(0)
    start = jnp.int32(0)
    for k in range(lengths_ref.shape[1]):
        found = jnp.where(start == position, jnp.int32(1), found)
        start = start + lengths_ref[0, k]
    return found


def halves(value):
    high = value.astype(bf16)
    return high, (value - high.astype(f32)).astype(bf16)


def cumulative_of(step, rate_row):
    eye = iota((HEADS, HEADS), 0) == iota((HEADS, HEADS), 1)
    rate = jnp.sum(jnp.where(eye, rate_row, 0.0), axis=1, keepdims=True)
    tokens = step.shape[1]
    upto = (iota((tokens, tokens), 0) <= iota((tokens, tokens), 1)).astype(f32)
    return dot(-step * rate, upto, precision=lax.Precision.HIGHEST)


def spread_matrix():
    rows, lanes = 2 * HEADS_GROUP, WIDE
    return (iota((rows, lanes), 0) % HEADS_GROUP == iota((rows, lanes), 1) // HEAD_DIM).astype(bf16)


def spread(per_head, group, matrix):
    part = per_head[group * HEADS_GROUP : (group + 1) * HEADS_GROUP]
    return dot(jnp.concatenate(halves(part), axis=0), matrix, ((0,), (0,)))


def half_silu(half):
    return half + half * jnp.tanh(half)


def to_rows(strip, first):
    rows = iota((8, WIDE), 0)
    top = jnp.zeros((8, WIDE), f32)
    low = jnp.zeros((8, WIDE), f32)
    for k in range(strip.shape[1] // WIDE):
        chunk = strip[:, k * WIDE : (k + 1) * WIDE]
        moved = pltpu.roll(chunk, (3 * k - first) % 8, 0)
        for base, at in ((0, "top"), (8, "low")):
            low_row, high_row = 3 * k - base, 3 * k + 2 - base
            if high_row < 0 or low_row > 7:
                continue
            mask = (rows >= low_row) & (rows <= high_row)
            if at == "top":
                top = jnp.where(mask, moved, top)
            else:
                low = jnp.where(mask, moved, low)
    return jnp.concatenate([top, low], axis=0)


def state_kernel(
    lengths_ref, x_ref, step_ref, weight_ref, bias_ref, rate_ref, conv_ref, cumulative_ref, sent_ref
):
    fresh = is_fresh(lengths_ref, lax.axis_index("ctx"))
    count = x_ref.shape[1]
    step = step_ref[0]
    cumulative = cumulative_of(step, rate_ref[...])
    cumulative_ref[...] = cumulative
    last = cumulative[:, count - 1 :]
    tail = step * jnp.exp(last - cumulative)
    lanes = iota((HEADS, count), 1)
    kept = jnp.where((lanes >= KERNEL_EDGE) | (fresh == 1), tail, 0.0)
    scales = jnp.where(lanes == KERNEL_EDGE, jnp.exp(last), tail)
    high, low = halves(scales)
    place = iota((HEADS, 128), 1) - iota((HEADS, 128), 0)
    picked = dot(high, (place == 0).astype(bf16), ((0,), (0,)))
    picked = picked + dot(low, (place == HEADS).astype(bf16), ((0,), (0,)))
    sent_ref[SCALE_AT : SCALE_AT + 16, :] = jnp.concatenate(
        [picked[:16], jnp.zeros((16, WIDE - 128), f32)], axis=1
    ).astype(bf16)
    sent_ref[TAIL_AT : TAIL_AT + 16, :] = to_rows(x_ref[0, count - 16 :, :].astype(f32)[8:], 5).astype(bf16)
    sent_ref[HEAD_AT : HEAD_AT + 16, :] = to_rows(x_ref[0, :16, :].astype(f32)[:8], 0).astype(bf16)

    matrix = spread_matrix()
    weight = weight_ref[...].astype(f32) * 0.5
    bias = bias_ref[...].astype(f32) * 0.5

    def conv_tile(j):
        cols = slice(j * 128, (j + 1) * 128)
        x = x_ref[0, :, cols].astype(f32)
        padded = jnp.concatenate([jnp.zeros((8, 128), f32), x], axis=0)
        total = bias[j : j + 1, :] + x * weight[3:4, cols]
        for back in range(1, 4):
            total = total + padded[8 - back : 8 - back + count] * weight[3 - back : 4 - back, cols]
        return half_silu(total)

    tiles = CONV_TILES
    keys = []
    for j in range(tiles - 4, tiles):
        tile = conv_tile(j).astype(bf16)
        conv_ref[:, j * 128 : (j + 1) * 128] = tile
        keys.append(tile)
    for group in range(BC_GROUPS):
        scale = spread(kept, group, matrix)
        parts = []
        for i in range(WIDE // 128):
            j = group * (WIDE // 128) + i
            tile = conv_tile(j)
            conv_ref[:, j * 128 : (j + 1) * 128] = tile.astype(bf16)
            parts.append((tile * scale[:, i * 128 : (i + 1) * 128]).astype(bf16))
        written = jnp.concatenate(parts, axis=1)
        key = keys[group // 2][:, (group % 2) * STATE : (group % 2 + 1) * STATE]
        local = dot(key, written, ((0,), (0,)))
        sent_ref[group * STATE : (group + 1) * STATE, :] = local.astype(bf16)


KERNEL_EDGE = 3
CONV_TILES = 20


def edge_rows(tail_block, head_block, weight, bias):
    rows = iota((16, WIDE), 0)
    third = rows % 3
    chunk = rows // 3

    def blocked(lines):
        out = jnp.zeros((16, WIDE), f32)
        for k in range(5):
            out = jnp.where(chunk == k, lines[k], out)
        return out

    taps = [
        blocked([weight[tap : tap + 1, k * WIDE : (k + 1) * WIDE] for k in range(5)])
        for tap in range(4)
    ]
    offset = blocked(
        [
            jnp.concatenate([bias[4 * k + i : 4 * k + i + 1, :] for i in range(4)], axis=1)
            for k in range(5)
        ]
    )
    back1 = jnp.where(third == 0, pltpu.roll(tail_block, 14, 0), pltpu.roll(head_block, 1, 0))
    back2 = jnp.where(third == 2, pltpu.roll(head_block, 2, 0), pltpu.roll(tail_block, 15, 0))
    total = offset + head_block * taps[3] + back1 * taps[2] + back2 * taps[1] + tail_block * taps[0]
    return half_silu(total)


def unblocked(block, k):
    return pltpu.roll(block, (16 - 3 * k) % 16, 0)[:8]


def edge_scales(scale_rows, group):
    lanes = iota((128, WIDE), 1) // HEAD_DIM + group * HEADS_GROUP
    matrix = (iota((128, WIDE), 0) % HEADS == lanes).astype(bf16)
    return dot(scale_rows, matrix)


def edge_state(values_rows, key_rows, scale, group):
    rows = iota((8, WIDE), 0)
    written = jnp.where(rows < KERNEL_EDGE, values_rows.astype(bf16).astype(f32) * scale, 0.0)
    return dot(key_rows.astype(bf16), written.astype(bf16), ((0,), (0,)))


def edge_keys(keys_rows, group):
    tile = keys_rows[:, (group // 2) * 128 : (group // 2 + 1) * 128]
    return tile[:, (group % 2) * STATE : (group % 2 + 1) * STATE]


def combine_kernel(lengths_ref, own_ref, got_ref, weight_ref, bias_ref, sent_ref, edge_ref):
    fresh = is_fresh(lengths_ref, lax.axis_index("ctx"))
    goes_on = (1 - fresh).astype(f32)
    weight = weight_ref[...].astype(f32) * 0.5
    bias = bias_ref[...].astype(f32) * 0.5
    tail_block = got_ref[TAIL_AT : TAIL_AT + 16, :].astype(f32)
    head_block = own_ref[HEAD_AT : HEAD_AT + 16, :].astype(f32)
    tail_block = jnp.where(fresh == 1, 0.0, tail_block)
    block = edge_rows(tail_block, head_block, weight, bias)
    chunks = [unblocked(block, k) for k in range(5)]
    for k in range(5):
        edge_ref[:, k * WIDE : (k + 1) * WIDE] = chunks[k]
    sent_ref[STATE_ROWS:, :] = own_ref[TAIL_AT : TAIL_AT + 16, :]
    scales = own_ref[SCALE_AT : SCALE_AT + 16, :128]
    for group in range(BC_GROUPS):
        at = slice(group * STATE, (group + 1) * STATE)
        scale = edge_scales(scales, group)[:8]
        extra = edge_state(chunks[group], edge_keys(chunks[4], group), scale * goes_on, group)
        decay = scale[KERNEL_EDGE : KERNEL_EDGE + 1] * goes_on
        total = own_ref[at, :].astype(f32) + extra + decay * got_ref[at, :].astype(f32)
        sent_ref[at, :] = total.astype(bf16)


def diagonal_kernel(
    skip_ref, conv_ref, edge_ref, cumulative_ref, step_ref, diagonal_ref, queries_ref, entry_ref
):
    count = conv_ref.shape[0]
    cumulative = cumulative_ref[...] * LOG2E
    across = cumulative - jnp.log2(step_ref[0])
    down = cumulative.T
    entry_ref[...] = jnp.concatenate(halves(jnp.exp2(cumulative)), axis=0)
    edge_row = iota((count, 128), 0) < KERNEL_EDGE
    causal = iota((count, 128), 0) >= iota((count, 128), 1)
    lane_head = iota((count, 128), 1) // HEAD_DIM

    def tile_of(j):
        cols = slice(j * 128, (j + 1) * 128)
        rows = jnp.concatenate([edge_ref[:, cols], jnp.zeros((count - 8, 128), f32)], axis=0)
        return jnp.where(edge_row, rows, conv_ref[:, cols].astype(f32))

    keys = [tile_of(16 + i).astype(bf16) for i in range(2)]
    queries = [tile_of(18 + i).astype(bf16) for i in range(2)]
    for i in range(2):
        queries_ref[:, i * 128 : (i + 1) * 128] = queries[i]
    for group in range(BC_GROUPS):
        part = slice((group % 2) * STATE, (group % 2 + 1) * STATE)
        scores = dot(queries[group // 2][:, part], keys[group // 2][:, part], ((1,), (1,)))
        for i in range(4):
            j = group * 4 + i
            values = tile_of(j)
            weights, parts = [], []
            gain = jnp.zeros((1, 128), f32)
            for k in range(4):
                head = 4 * j + k
                gap = down[:, head : head + 1] - across[head : head + 1, :]
                weights.append((jnp.exp2(jnp.where(causal, gap, -1e30)) * scores).astype(bf16))
                parts.append(jnp.where(lane_head == k, values, 0.0).astype(bf16))
                gain = jnp.where(lane_head[:1] == k, skip_ref[0, head], gain)
            total = dot(jnp.concatenate(weights, axis=1), jnp.concatenate(parts, axis=0))
            diagonal_ref[:, j * 128 : (j + 1) * 128] = total + gain * values


def finish_kernel(
    lengths_ref, first_ref, second_ref, weight_ref, bias_ref, diagonal_ref, queries_ref, entry_ref, out_ref
):
    position = lax.axis_index("ctx")
    fresh = is_fresh(lengths_ref, position)
    before_fresh = is_fresh(lengths_ref, position - 1)
    goes_on = (1 - before_fresh).astype(f32)
    weight = weight_ref[...].astype(f32) * 0.5
    bias = bias_ref[...].astype(f32) * 0.5
    tail_block = second_ref[STATE_ROWS:, :].astype(f32)
    head_block = first_ref[HEAD_AT : HEAD_AT + 16, :].astype(f32)
    block = edge_rows(tail_block, head_block, weight, bias)
    chunks = [unblocked(block, k) for k in range(5)]
    scales = first_ref[SCALE_AT : SCALE_AT + 16, :128]
    matrix = spread_matrix()
    for group in range(BC_GROUPS):
        at = slice(group * STATE, (group + 1) * STATE)
        cols = slice(group * WIDE, (group + 1) * WIDE)
        scale = edge_scales(scales, group)[:8] * goes_on
        extra = edge_state(chunks[group], edge_keys(chunks[4], group), scale, group)
        decay = scale[KERNEL_EDGE : KERNEL_EDGE + 1]
        total = first_ref[at, :].astype(f32) + extra + decay * second_ref[at, :].astype(f32)
        incoming = jnp.where(fresh == 1, 0.0, total).astype(bf16)
        low = (group % 2) * STATE
        tile = queries_ref[:, (group // 2) * 128 : (group // 2 + 1) * 128]
        carried = dot(tile[:, low : low + STATE], incoming)
        rows = slice(group * HEADS_GROUP, (group + 1) * HEADS_GROUP)
        low_rows = slice(HEADS + group * HEADS_GROUP, HEADS + (group + 1) * HEADS_GROUP)
        entry = dot(
            jnp.concatenate([entry_ref[rows, :], entry_ref[low_rows, :]], axis=0), matrix, ((0,), (0,))
        )
        out_ref[0, :, cols] = (diagonal_ref[:, cols] + entry * carried).astype(bf16)


def call(kernel, outs, specs, flops, moved, *args):
    return pl.pallas_call(
        kernel,
        out_shape=outs,
        in_specs=specs,
        out_specs=jax.tree.map(lambda _: VMEM, outs),
        compiler_params=pltpu.CompilerParams(vmem_limit_bytes=24 * 1024 * 1024),
        cost_estimate=pl.CostEstimate(flops=flops, bytes_accessed=moved, transcendentals=0),
    )(*args)


def shard_near(pre_conv, step_size, lengths, conv_weight, conv_bias, decay_rate, skip_gain):
    count = pre_conv.shape[1]
    size = lax.axis_size("ctx")
    bias = conv_bias.reshape(-1, 128)
    rate = decay_rate.reshape(1, -1)
    skip = skip_gain.reshape(1, -1)
    sds = jax.ShapeDtypeStruct
    conv, cumulative, own = call(
        state_kernel,
        (
            sds(pre_conv.shape[1:], bf16),
            sds((HEADS, count), f32),
            sds((FIRST_ROWS, WIDE), bf16),
        ),
        [SMEM, VMEM, VMEM, VMEM, VMEM, VMEM],
        60_000_000,
        2_000_000,
        lengths,
        pre_conv,
        step_size,
        conv_weight,
        bias,
        rate,
    )
    first = lax.ppermute(own, "ctx", [(i, (i + 1) % size) for i in range(size)])
    sent, edge = call(
        combine_kernel,
        (sds((SECOND_ROWS, WIDE), bf16), sds((8, pre_conv.shape[2]), f32)),
        [SMEM, VMEM, VMEM, VMEM, VMEM],
        1_000_000,
        1_000_000,
        lengths,
        own,
        first,
        conv_weight,
        bias,
    )
    second = lax.ppermute(sent, "ctx", [(i, i + 2) for i in range(size - 2)])
    diagonal, queries, entry = call(
        diagonal_kernel,
        (
            sds((count, VALUES), f32),
            sds((count, BC_GROUPS * STATE), bf16),
            sds((2 * HEADS, count), bf16),
        ),
        [SMEM, VMEM, VMEM, VMEM, VMEM],
        400_000_000,
        4_000_000,
        skip,
        conv,
        edge,
        cumulative,
        step_size,
    )
    return call(
        finish_kernel,
        sds((1, count, VALUES), bf16),
        [SMEM] + [VMEM] * 7,
        100_000_000,
        2_000_000,
        lengths,
        first,
        second,
        conv_weight,
        bias,
        diagonal,
        queries,
        entry,
    )


def shifted(value, axis, steps):
    count = lax.axis_size(axis)
    first, last = (max(0, -steps), min(count, count - steps))
    return lax.ppermute(value, axis, [(source, source + steps) for source in range(first, last)])


def carried_in(array, axis, combine, identity):
    length, index = (lax.axis_size(axis), lax.axis_index(axis))
    everything = jax.tree.map(
        lambda part, kind: lax.all_gather(part.astype(kind), axis),
        array,
        (jnp.bfloat16, jnp.bfloat16),
    )
    start = jax.tree.map(
        lambda part, zero: jnp.broadcast_to(jnp.asarray(zero, part.dtype), part.shape),
        array,
        identity,
    )

    def step(k, before):
        reached = k < index
        new = combine(
            before, jax.tree.map(lambda part, own: part[k].astype(own.dtype), everything, array)
        )
        return jax.tree.map(lambda a, b: jnp.where(reached, a, b), new, before)

    return lax.fori_loop(0, length, step, start)


def convolve(padded, conv_weight, conv_bias, count_rows):
    total = conv_bias.astype(jnp.float32)[None, :]
    for offset in range(conv_weight.shape[0]):
        total = (
            total
            + padded[offset : offset + count_rows].astype(jnp.float32)
            * conv_weight[offset].astype(jnp.float32)[None, :]
        )
    return jax.nn.silu(total).astype(jnp.bfloat16)


def group_terms(values, keys_in, queries, decay_rate, step_rows):
    heads_group = step_rows.shape[0]
    count_rows = step_rows.shape[1]
    values = values.reshape(count_rows, heads_group, -1)
    cumulative = jnp.cumsum(-step_rows * decay_rate[:, None], axis=1)
    scores = jnp.einsum("tn,sn->ts", queries, keys_in, preferred_element_type=jnp.float32)
    later = lax.broadcasted_iota(jnp.int32, (count_rows, count_rows), 0)
    earlier = lax.broadcasted_iota(jnp.int32, (count_rows, count_rows), 1)
    spread = jnp.where(
        (later >= earlier)[None], cumulative[:, :, None] - cumulative[:, None, :], -1e30
    )
    weights = (jnp.exp(spread) * scores[None]).astype(jnp.bfloat16)
    scaled = (values * step_rows.T[:, :, None]).astype(jnp.bfloat16)
    diagonal_part = jnp.einsum("hts,shp->thp", weights, scaled, preferred_element_type=jnp.float32)
    tail_weight = jnp.exp(cumulative[:, -1:] - cumulative)
    written = (values * (step_rows * tail_weight).T[:, :, None]).astype(jnp.bfloat16)
    local_state = jnp.einsum("tn,thp->hpn", keys_in, written, preferred_element_type=jnp.float32)
    return (diagonal_part, local_state, jnp.exp(cumulative[:, -1]), jnp.exp(cumulative), values)


def finish_group(diagonal_part, entry_decay, queries, incoming, values, skip_gain):
    incoming_rounded = incoming.astype(jnp.bfloat16)
    carried_part = jnp.einsum(
        "tn,hpn->thp", queries, incoming_rounded, preferred_element_type=jnp.float32
    )
    carried_part = carried_part * entry_decay.T[:, :, None]
    return diagonal_part + carried_part + skip_gain[None, :, None] * values.astype(jnp.float32)


def combine(earlier, later):
    return (earlier[0] * later[0], later[0][:, None, None] * earlier[1] + later[1])


def shard_far(pre_conv, step_size, lengths, conv_weight, conv_bias, decay_rate, skip_gain):
    count_rows = pre_conv.shape[1]
    kernel_len = conv_weight.shape[0]
    heads_group = HEADS // BC_GROUPS
    position = lax.axis_index("ctx")
    sizes_row = lengths[0]
    starts = jnp.cumsum(sizes_row) - sizes_row
    fresh = jnp.any(starts == position)
    retain = jnp.where(fresh, 0.0, 1.0).astype(jnp.float32)
    own_rows = pre_conv[0]
    previous = shifted(own_rows[count_rows - kernel_len + 1 :], "ctx", 1)
    previous = jnp.where(fresh, jnp.zeros_like(previous), previous)
    convolved = convolve(
        jnp.concatenate([previous, own_rows], axis=0), conv_weight, conv_bias, count_rows
    )
    values = convolved[:, : HEADS * HEAD_DIM]
    keys_all = convolved[:, HEADS * HEAD_DIM : HEADS * HEAD_DIM + BC_GROUPS * STATE]
    queries_all = convolved[:, HEADS * HEAD_DIM + BC_GROUPS * STATE :]
    step_rows = step_size[0]
    results = []
    pieces = []
    for bc_group in range(BC_GROUPS):
        low = bc_group * heads_group
        high = low + heads_group
        pieces.append(
            group_terms(
                values[:, low * HEAD_DIM : high * HEAD_DIM],
                keys_all[:, bc_group * STATE : (bc_group + 1) * STATE],
                queries_all[:, bc_group * STATE : (bc_group + 1) * STATE],
                decay_rate[low:high],
                step_rows[low:high],
            )
        )
    decays = jnp.concatenate([piece[2] for piece in pieces], axis=0) * retain
    states = jnp.concatenate([piece[1] for piece in pieces], axis=0)
    identity = (jnp.ones_like(decays), jnp.zeros_like(states))
    totals = carried_in((decays, states), "ctx", combine, identity)
    incoming = totals[1] * retain
    for bc_group in range(BC_GROUPS):
        low = bc_group * heads_group
        high = low + heads_group
        piece = pieces[bc_group]
        results.append(
            finish_group(
                piece[0],
                piece[3],
                queries_all[:, bc_group * STATE : (bc_group + 1) * STATE],
                incoming[low:high],
                piece[4],
                skip_gain[low:high],
            )
        )
    output = (
        jnp.concatenate(results, axis=1).reshape(count_rows, HEADS * HEAD_DIM).astype(jnp.bfloat16)
    )
    return output[None]


def solution(mesh):
    in_specs = (
        P(("groups", "lane"), "ctx", None),
        P(("groups", "lane"), None, "ctx"),
        P(("groups", "lane"), None),
        P(),
        P(),
        P(),
        P(),
    )
    out_specs = P(("groups", "lane"), "ctx", None)
    shards = shard_near if mesh.shape["ctx"] <= 8 else shard_far
    return jax.shard_map(shards, mesh=mesh, in_specs=in_specs, out_specs=out_specs, check_vma=False)
```

```python
import jax
import jax.numpy as jnp
from jax import lax
from jax.experimental import pallas as pl
from jax.experimental.pallas import tpu as pltpu
from jax.sharding import PartitionSpec as P

HEADS = 64
HEAD_DIM = 32
EDGE = 3
STATE = 64
BC_GROUPS = 4
HEADS_GROUP = HEADS // BC_GROUPS
VALUES = HEADS * HEAD_DIM
WIDE = HEADS_GROUP * HEAD_DIM
STATE_ROWS = BC_GROUPS * STATE
TAIL_AT = STATE_ROWS
HEAD_AT = TAIL_AT + 16
SCALE_AT = HEAD_AT + 16
FIRST_ROWS = SCALE_AT + 16
SECOND_ROWS = STATE_ROWS + 16
LOG2E = 1.4426950408889634
VMEM = pl.BlockSpec(memory_space=pltpu.VMEM)
HBM = pl.BlockSpec(memory_space=pltpu.HBM)
SMEM = pl.BlockSpec(memory_space=pltpu.SMEM)
f32 = jnp.float32
bf16 = jnp.bfloat16


def iota(shape, dim):
    return lax.broadcasted_iota(jnp.int32, shape, dim)


def dot(a, b, contract=((1,), (0,)), precision=None):
    return lax.dot_general(
        a, b, (contract, ((), ())), preferred_element_type=f32, precision=precision
    )


def is_fresh(lengths_ref, position):
    found = jnp.int32(0)
    start = jnp.int32(0)
    for k in range(lengths_ref.shape[1]):
        found = jnp.where(start == position, jnp.int32(1), found)
        start = start + lengths_ref[0, k]
    return found


def halves(value):
    high = value.astype(bf16)
    return high, (value - high.astype(f32)).astype(bf16)


def cumulative_of(step, rate_row):
    eye = iota((HEADS, HEADS), 0) == iota((HEADS, HEADS), 1)
    rate = jnp.sum(jnp.where(eye, rate_row, 0.0), axis=1, keepdims=True)
    tokens = step.shape[1]
    upto = (iota((tokens, tokens), 0) <= iota((tokens, tokens), 1)).astype(f32)
    return dot(-step * rate, upto, precision=lax.Precision.HIGHEST)


def spread_matrix():
    rows, lanes = 2 * HEADS_GROUP, WIDE
    return (iota((rows, lanes), 0) % HEADS_GROUP == iota((rows, lanes), 1) // HEAD_DIM).astype(bf16)


def spread(per_head, group, matrix):
    part = per_head[group * HEADS_GROUP : (group + 1) * HEADS_GROUP]
    return dot(jnp.concatenate(halves(part), axis=0), matrix, ((0,), (0,)))


def half_silu(half):
    return half + half * jnp.tanh(half)


def to_rows(strip, first):
    rows = iota((8, WIDE), 0)
    top = jnp.zeros((8, WIDE), f32)
    low = jnp.zeros((8, WIDE), f32)
    for k in range(strip.shape[1] // WIDE):
        moved = pltpu.roll(strip[:, k * WIDE : (k + 1) * WIDE], (3 * k - first) % 8, 0)
        if 3 * k < 8:
            top = jnp.where((rows >= 3 * k) & (rows < 3 * k + 3), moved, top)
        if 3 * k + 2 >= 8:
            low = jnp.where((rows >= 3 * k - 8) & (rows < 3 * k - 5), moved, low)
    return jnp.concatenate([top, low], axis=0)


def conv_rows(x, weight, bias):
    padded = jnp.concatenate([jnp.zeros((8, x.shape[1]), f32), x], axis=0)
    total = bias + x * weight[3:4]
    for back in range(1, 4):
        total = total + padded[8 - back : 8 - back + x.shape[0]] * weight[3 - back : 4 - back]
    return half_silu(total)


def state_kernel(
    lengths_hbm, x_hbm, step_hbm, weight_hbm, bias_hbm, rate_hbm,
    conv_ref, cumulative_ref, sent_ref,
    lengths_ref, x_ref, step_ref, weight_ref, bias_ref, rate_ref, sems,
):
    order = (4, 0, 1, 2, 3)
    small = [
        pltpu.make_async_copy(source, target, sems.at[i])
        for i, (source, target) in enumerate(
            (
                (step_hbm.at[0], step_ref),
                (rate_hbm, rate_ref),
                (lengths_hbm, lengths_ref),
                (weight_hbm, weight_ref),
                (bias_hbm, bias_ref),
            )
        )
    ]
    large = [
        pltpu.make_async_copy(
            x_hbm.at[0, :, pl.ds(k * WIDE, WIDE)], x_ref.at[:, pl.ds(k * WIDE, WIDE)], sems.at[5 + k]
        )
        for k in range(5)
    ]
    for copy in small:
        copy.start()
    for k in order:
        large[k].start()
    count = x_ref.shape[0]
    for copy in small:
        copy.wait()
    fresh = is_fresh(lengths_ref, lax.axis_index("ctx"))
    step = step_ref[...]
    cumulative = cumulative_of(step, rate_ref[...])
    cumulative_ref[...] = cumulative
    last = cumulative[:, count - 1 :]
    tail = step * jnp.exp(last - cumulative)
    lanes = iota((HEADS, count), 1)
    kept = jnp.where((lanes >= EDGE) | (fresh == 1), tail, 0.0)
    scales = jnp.where(lanes == EDGE, jnp.exp(last), tail)
    high, low = halves(scales)
    place = iota((HEADS, 128), 1) - iota((HEADS, 128), 0)
    picked = dot(high, (place == 0).astype(bf16), ((0,), (0,)))
    picked = picked + dot(low, (place == HEADS).astype(bf16), ((0,), (0,)))
    sent_ref[SCALE_AT : SCALE_AT + 16, :] = jnp.concatenate(
        [picked[:16], jnp.zeros((16, WIDE - 128), f32)], axis=1
    ).astype(bf16)

    matrix = spread_matrix()
    weight = weight_ref[...].astype(f32) * 0.5
    bias = bias_ref[...].astype(f32) * 0.5

    def conv_tile(j):
        cols = slice(j * 128, (j + 1) * 128)
        return conv_rows(x_ref[:, cols].astype(f32), weight[:, cols], bias[j : j + 1, :])

    keys = []
    large[4].wait()
    for j in (16, 17):
        tile = conv_tile(j).astype(bf16)
        conv_ref[:, j * 128 : (j + 1) * 128] = tile
        keys.append(tile)
    for group in range(BC_GROUPS):
        scale = spread(kept, group, matrix)
        large[group].wait()
        parts = []
        for i in range(WIDE // 128):
            j = group * (WIDE // 128) + i
            tile = conv_tile(j)
            conv_ref[:, j * 128 : (j + 1) * 128] = tile.astype(bf16)
            parts.append((tile * scale[:, i * 128 : (i + 1) * 128]).astype(bf16))
        written = jnp.concatenate(parts, axis=1)
        key = keys[group // 2][:, (group % 2) * STATE : (group % 2 + 1) * STATE]
        local = dot(key, written, ((0,), (0,)))
        sent_ref[group * STATE : (group + 1) * STATE, :] = local.astype(bf16)
    sent_ref[TAIL_AT : TAIL_AT + 16, :] = to_rows(x_ref[count - 16 :, :].astype(f32)[8:], 5).astype(bf16)
    sent_ref[HEAD_AT : HEAD_AT + 16, :] = to_rows(x_ref[:16, :].astype(f32)[:8], 0).astype(bf16)


def known_part(head_block, table_ref):
    return (
        table_ref[0]
        + head_block * table_ref[1]
        + pltpu.roll(head_block, 1, 0) * table_ref[2]
        + pltpu.roll(head_block, 2, 0) * table_ref[3]
    )


def edge_rows(tail_block, known, table_ref):
    block = half_silu(
        known
        + tail_block * table_ref[4]
        + pltpu.roll(tail_block, 15, 0) * table_ref[5]
        + pltpu.roll(tail_block, 14, 0) * table_ref[6]
    )
    return [pltpu.roll(block, (16 - 3 * k) % 16, 0)[:8] for k in range(5)]


def edge_scales(scale_rows):
    lanes = iota((128, VALUES), 1) // HEAD_DIM
    matrix = (iota((128, VALUES), 0) % HEADS == lanes).astype(bf16)
    return dot(scale_rows, matrix)[:8]


def prepare_kernel(
    lengths_ref, x_hbm, own_ref, weight_ref, bias_ref, cumulative_ref, step_ref, skip_ref,
    queries_ref, table_ref, known_ref, scale_ref, across_ref, down_ref, entry_ref, gain_ref, x_ref, sem,
):
    count = x_ref.shape[0]
    first = VALUES + BC_GROUPS * STATE
    copy = pltpu.make_async_copy(x_hbm.at[0, :, pl.ds(first, BC_GROUPS * STATE)], x_ref, sem)
    copy.start()
    position = lax.axis_index("ctx")
    goes_on = (1 - is_fresh(lengths_ref, position)).astype(f32)
    went_on = (1 - is_fresh(lengths_ref, position - 1)).astype(f32)
    weight = weight_ref[...].astype(f32) * 0.5
    bias = bias_ref[...].astype(f32) * 0.5
    rows = iota((16, WIDE), 0)
    third = rows % 3
    chunk = rows // 3

    def blocked(lines):
        out = jnp.zeros((16, WIDE), f32)
        for k in range(5):
            out = jnp.where(chunk == k, lines[k], out)
        return out

    taps = [
        blocked([weight[tap : tap + 1, k * WIDE : (k + 1) * WIDE] for k in range(5)])
        for tap in range(4)
    ]
    table_ref[0] = blocked(
        [
            jnp.concatenate([bias[4 * k + i : 4 * k + i + 1, :] for i in range(4)], axis=1)
            for k in range(5)
        ]
    )
    table_ref[1] = taps[3]
    table_ref[2] = jnp.where(third == 0, 0.0, taps[2])
    table_ref[3] = jnp.where(third == 2, taps[1], 0.0)
    table_ref[4] = taps[0]
    table_ref[5] = jnp.where(third == 2, 0.0, taps[1])
    table_ref[6] = jnp.where(third == 0, taps[2], 0.0)
    known_ref[:16, :] = known_part(own_ref[HEAD_AT : HEAD_AT + 16, :].astype(f32), table_ref)
    known_ref[16:, :] = jnp.where(iota((8, WIDE), 0) == 0, goes_on, goes_on * went_on)
    scale_ref[...] = edge_scales(own_ref[SCALE_AT : SCALE_AT + 16, :128]) * goes_on
    cumulative = cumulative_ref[...] * LOG2E
    across_ref[...] = cumulative - jnp.log2(step_ref[0])
    down_ref[...] = cumulative.T
    matrix = spread_matrix()
    entry = jnp.exp2(cumulative)
    for group in range(BC_GROUPS):
        entry_ref[:, group * WIDE : (group + 1) * WIDE] = spread(entry, group, matrix)
    gain = jnp.concatenate(halves(skip_ref[...] + jnp.zeros((16, HEADS), f32)), axis=1)
    gain_ref[...] = edge_scales(gain)
    copy.wait()
    for i in range(2):
        cols = slice(first + i * 128, first + (i + 1) * 128)
        j = first // 128 + i
        tile = conv_rows(
            x_ref[:, i * 128 : (i + 1) * 128].astype(f32), weight[:, cols], bias[j : j + 1, :]
        )
        queries_ref[:, i * 128 : (i + 1) * 128] = tile.astype(bf16)


def edge_state(values_rows, keys_rows, scale, group):
    rows = iota((8, WIDE), 0)
    written = jnp.where(rows < EDGE, values_rows * scale, 0.0)
    tile = keys_rows[:, (group // 2) * 128 : (group // 2 + 1) * 128].astype(bf16)
    return dot(tile[:, (group % 2) * STATE : (group % 2 + 1) * STATE], written.astype(bf16), ((0,), (0,)))


def combine_kernel(own_ref, got_ref, table_ref, known_ref, scale_ref, sent_ref, edge_ref):
    tail_block = got_ref[TAIL_AT : TAIL_AT + 16, :].astype(f32) * known_ref[16:17, :]
    chunks = edge_rows(tail_block, known_ref[:16, :], table_ref)
    for k in range(5):
        edge_ref[:, k * WIDE : (k + 1) * WIDE] = chunks[k]
    sent_ref[STATE_ROWS:, :] = own_ref[TAIL_AT : TAIL_AT + 16, :]
    for group in range(BC_GROUPS):
        at = slice(group * STATE, (group + 1) * STATE)
        scale = scale_ref[:, group * WIDE : (group + 1) * WIDE]
        extra = edge_state(chunks[group], chunks[4], scale, group)
        total = own_ref[at, :].astype(f32) + extra + scale[EDGE : EDGE + 1] * got_ref[at, :].astype(f32)
        sent_ref[at, :] = total.astype(bf16)


def diagonal_kernel(
    conv_ref, raw_queries_ref, edge_ref, across_ref, down_ref, gain_ref, got_ref, table_ref, gates_ref,
    diagonal_ref, queries_ref, known_ref, scale_ref,
):
    known_ref[:16, :] = known_part(got_ref[HEAD_AT : HEAD_AT + 16, :].astype(f32), table_ref)
    known_ref[16:, :] = gates_ref[16:, :]
    both = gates_ref[17:18, :1]
    scale_ref[...] = edge_scales(got_ref[SCALE_AT : SCALE_AT + 16, :128]) * both

    count = conv_ref.shape[0]
    edge_row = iota((count, 128), 0) < EDGE
    causal = iota((count, 128), 0) >= iota((count, 128), 1)
    lane_head = iota((count, 128), 1) // HEAD_DIM

    def patched(tile, j):
        rows = jnp.concatenate(
            [edge_ref[:, j * 128 : (j + 1) * 128], jnp.zeros((count - 8, 128), f32)], axis=0
        )
        return jnp.where(edge_row, rows, tile.astype(f32))

    keys = [patched(conv_ref[:, (16 + i) * 128 : (17 + i) * 128], 16 + i).astype(bf16) for i in range(2)]
    queries = [
        patched(raw_queries_ref[:, i * 128 : (i + 1) * 128], 18 + i).astype(bf16) for i in range(2)
    ]
    for i in range(2):
        queries_ref[:, i * 128 : (i + 1) * 128] = queries[i]
    for group in range(BC_GROUPS):
        part = slice((group % 2) * STATE, (group % 2 + 1) * STATE)
        scores = dot(queries[group // 2][:, part], keys[group // 2][:, part], ((1,), (1,)))
        for i in range(4):
            j = group * 4 + i
            cols = slice(j * 128, (j + 1) * 128)
            values = patched(conv_ref[:, cols], j)
            weights, parts = [], []
            for k in range(4):
                at = 4 * j + k
                gap = down_ref[:, at : at + 1] - across_ref[at : at + 1, :]
                weights.append((jnp.exp2(jnp.where(causal, gap, -1e30)) * scores).astype(bf16))
                parts.append(jnp.where(lane_head == k, values, 0.0).astype(bf16))
            total = dot(jnp.concatenate(weights, axis=1), jnp.concatenate(parts, axis=0))
            diagonal_ref[:, cols] = total + gain_ref[:1, cols] * values


def finish_kernel(
    first_ref, second_ref, table_ref, known_ref, scale_ref, diagonal_ref, queries_ref, entry_ref, out_hbm, out_ref, sems
):
    tail_block = second_ref[STATE_ROWS:, :].astype(f32)
    chunks = edge_rows(tail_block, known_ref[:16, :], table_ref)
    kept = known_ref[16:17, :]
    copies = []
    for group in range(BC_GROUPS):
        at = slice(group * STATE, (group + 1) * STATE)
        cols = slice(group * WIDE, (group + 1) * WIDE)
        scale = scale_ref[:, cols]
        extra = edge_state(chunks[group], chunks[4], scale, group)
        total = first_ref[at, :].astype(f32) * kept + extra
        total = total + scale[EDGE : EDGE + 1] * second_ref[at, :].astype(f32)
        low = (group % 2) * STATE
        tile = queries_ref[:, (group // 2) * 128 : (group // 2 + 1) * 128]
        carried = dot(tile[:, low : low + STATE], total.astype(bf16))
        out_ref[:, cols] = (diagonal_ref[:, cols] + entry_ref[:, cols] * carried).astype(bf16)
        copy = pltpu.make_async_copy(
            out_ref.at[:, pl.ds(group * WIDE, WIDE)],
            out_hbm.at[0, :, pl.ds(group * WIDE, WIDE)],
            sems.at[group],
        )
        copy.start()
        copies.append(copy)
    for copy in copies:
        copy.wait()


def call(kernel, outs, in_specs, cost, args, out_specs=None, scratch=()):
    return pl.pallas_call(
        kernel,
        out_shape=outs,
        in_specs=in_specs,
        out_specs=out_specs or jax.tree.map(lambda _: VMEM, outs),
        scratch_shapes=scratch,
        compiler_params=pltpu.CompilerParams(vmem_limit_bytes=24 * 1024 * 1024),
        cost_estimate=pl.CostEstimate(flops=cost[0], bytes_accessed=cost[1], transcendentals=0),
    )(*args)


def shard_near(pre_conv, step_size, lengths, conv_weight, conv_bias, decay_rate, skip_gain):
    count, channels = pre_conv.shape[1:]
    size = lax.axis_size("ctx")
    lengths, pre_conv, step_size, weight, bias, rate, skip = (
        pltpu.with_memory_space_constraint(array, pltpu.HBM)
        for array in (
            lengths,
            pre_conv,
            step_size,
            conv_weight,
            conv_bias.reshape(-1, 128),
            decay_rate.reshape(1, -1),
            skip_gain.reshape(1, -1),
        )
    )
    sds = jax.ShapeDtypeStruct
    grouped = BC_GROUPS * STATE
    conv, cumulative, own = call(
        state_kernel,
        (
            sds((count, channels - grouped), bf16),
            sds((HEADS, count), f32),
            sds((FIRST_ROWS, WIDE), bf16),
        ),
        [HBM] * 6,
        (60_000_000, 2_000_000),
        (lengths, pre_conv, step_size, weight, bias, rate),
        scratch=(
            pltpu.SMEM(lengths.shape, jnp.int32),
            pltpu.VMEM((count, channels), bf16),
            pltpu.VMEM((HEADS, count), f32),
            pltpu.VMEM(weight.shape, bf16),
            pltpu.VMEM(bias.shape, bf16),
            pltpu.VMEM(rate.shape, f32),
            pltpu.SemaphoreType.DMA((10,)),
        ),
    )
    first = lax.ppermute(own, "ctx", [(i, (i + 1) % size) for i in range(size)])
    raw_queries, table, gates, scale, across, down, entry, gain = call(
        prepare_kernel,
        (
            sds((count, grouped), bf16),
            sds((7, 16, WIDE), f32),
            sds((24, WIDE), f32),
            sds((8, VALUES), f32),
            sds((HEADS, count), f32),
            sds((count, HEADS), f32),
            sds((count, VALUES), f32),
            sds((8, VALUES), f32),
        ),
        [SMEM, HBM] + [VMEM] * 6,
        (10_000_000, 1_000_000),
        (lengths, pre_conv, own, weight, bias, cumulative, step_size, skip),
        scratch=(pltpu.VMEM((count, grouped), bf16), pltpu.SemaphoreType.DMA(())),
    )
    sent, edge = call(
        combine_kernel,
        (sds((SECOND_ROWS, WIDE), bf16), sds((8, channels), f32)),
        [VMEM] * 5,
        (1_000_000, 1_000_000),
        (own, first, table, gates, scale),
    )
    second = lax.ppermute(sent, "ctx", [(i, i + 2) for i in range(size - 2)])
    diagonal, queries, known, scale = call(
        diagonal_kernel,
        (
            sds((count, VALUES), f32),
            sds((count, grouped), bf16),
            sds((24, WIDE), f32),
            sds((8, VALUES), f32),
        ),
        [VMEM] * 9,
        (400_000_000, 4_000_000),
        (conv, raw_queries, edge, across, down, gain, first, table, gates),
    )
    return call(
        finish_kernel,
        sds((1, count, VALUES), bf16),
        [VMEM] * 8,
        (100_000_000, 2_000_000),
        (first, second, table, known, scale, diagonal, queries, entry),
        out_specs=HBM,
        scratch=(pltpu.VMEM((count, VALUES), bf16), pltpu.SemaphoreType.DMA((BC_GROUPS,))),
    )


def shifted(value, axis, steps):
    count = lax.axis_size(axis)
    first, last = (max(0, -steps), min(count, count - steps))
    return lax.ppermute(value, axis, [(source, source + steps) for source in range(first, last)])


def carried_in(array, axis, combine, identity):
    length, index = (lax.axis_size(axis), lax.axis_index(axis))
    everything = jax.tree.map(
        lambda part, kind: lax.all_gather(part.astype(kind), axis),
        array,
        (jnp.bfloat16, jnp.bfloat16),
    )
    start = jax.tree.map(
        lambda part, zero: jnp.broadcast_to(jnp.asarray(zero, part.dtype), part.shape),
        array,
        identity,
    )

    def step(k, before):
        reached = k < index
        new = combine(
            before, jax.tree.map(lambda part, own: part[k].astype(own.dtype), everything, array)
        )
        return jax.tree.map(lambda a, b: jnp.where(reached, a, b), new, before)

    return lax.fori_loop(0, length, step, start)


def convolve(padded, conv_weight, conv_bias, count_rows):
    total = conv_bias.astype(jnp.float32)[None, :]
    for offset in range(conv_weight.shape[0]):
        total = (
            total
            + padded[offset : offset + count_rows].astype(jnp.float32)
            * conv_weight[offset].astype(jnp.float32)[None, :]
        )
    return jax.nn.silu(total).astype(jnp.bfloat16)


def group_terms(values, keys_in, queries, decay_rate, step_rows):
    heads_group = step_rows.shape[0]
    count_rows = step_rows.shape[1]
    values = values.reshape(count_rows, heads_group, -1)
    cumulative = jnp.cumsum(-step_rows * decay_rate[:, None], axis=1)
    scores = jnp.einsum("tn,sn->ts", queries, keys_in, preferred_element_type=jnp.float32)
    later = lax.broadcasted_iota(jnp.int32, (count_rows, count_rows), 0)
    earlier = lax.broadcasted_iota(jnp.int32, (count_rows, count_rows), 1)
    spread = jnp.where(
        (later >= earlier)[None], cumulative[:, :, None] - cumulative[:, None, :], -1e30
    )
    weights = (jnp.exp(spread) * scores[None]).astype(jnp.bfloat16)
    scaled = (values * step_rows.T[:, :, None]).astype(jnp.bfloat16)
    diagonal_part = jnp.einsum("hts,shp->thp", weights, scaled, preferred_element_type=jnp.float32)
    tail_weight = jnp.exp(cumulative[:, -1:] - cumulative)
    written = (values * (step_rows * tail_weight).T[:, :, None]).astype(jnp.bfloat16)
    local_state = jnp.einsum("tn,thp->hpn", keys_in, written, preferred_element_type=jnp.float32)
    return (diagonal_part, local_state, jnp.exp(cumulative[:, -1]), jnp.exp(cumulative), values)


def finish_group(diagonal_part, entry_decay, queries, incoming, values, skip_gain):
    incoming_rounded = incoming.astype(jnp.bfloat16)
    carried_part = jnp.einsum(
        "tn,hpn->thp", queries, incoming_rounded, preferred_element_type=jnp.float32
    )
    carried_part = carried_part * entry_decay.T[:, :, None]
    return diagonal_part + carried_part + skip_gain[None, :, None] * values.astype(jnp.float32)


def combine(earlier, later):
    return (earlier[0] * later[0], later[0][:, None, None] * earlier[1] + later[1])


def shard_far(pre_conv, step_size, lengths, conv_weight, conv_bias, decay_rate, skip_gain):
    count_rows = pre_conv.shape[1]
    kernel_len = conv_weight.shape[0]
    heads_group = HEADS // BC_GROUPS
    position = lax.axis_index("ctx")
    sizes_row = lengths[0]
    starts = jnp.cumsum(sizes_row) - sizes_row
    fresh = jnp.any(starts == position)
    retain = jnp.where(fresh, 0.0, 1.0).astype(jnp.float32)
    own_rows = pre_conv[0]
    previous = shifted(own_rows[count_rows - kernel_len + 1 :], "ctx", 1)
    previous = jnp.where(fresh, jnp.zeros_like(previous), previous)
    convolved = convolve(
        jnp.concatenate([previous, own_rows], axis=0), conv_weight, conv_bias, count_rows
    )
    values = convolved[:, : HEADS * HEAD_DIM]
    keys_all = convolved[:, HEADS * HEAD_DIM : HEADS * HEAD_DIM + BC_GROUPS * STATE]
    queries_all = convolved[:, HEADS * HEAD_DIM + BC_GROUPS * STATE :]
    step_rows = step_size[0]
    results = []
    pieces = []
    for bc_group in range(BC_GROUPS):
        low = bc_group * heads_group
        high = low + heads_group
        pieces.append(
            group_terms(
                values[:, low * HEAD_DIM : high * HEAD_DIM],
                keys_all[:, bc_group * STATE : (bc_group + 1) * STATE],
                queries_all[:, bc_group * STATE : (bc_group + 1) * STATE],
                decay_rate[low:high],
                step_rows[low:high],
            )
        )
    decays = jnp.concatenate([piece[2] for piece in pieces], axis=0) * retain
    states = jnp.concatenate([piece[1] for piece in pieces], axis=0)
    identity = (jnp.ones_like(decays), jnp.zeros_like(states))
    totals = carried_in((decays, states), "ctx", combine, identity)
    incoming = totals[1] * retain
    for bc_group in range(BC_GROUPS):
        low = bc_group * heads_group
        high = low + heads_group
        piece = pieces[bc_group]
        results.append(
            finish_group(
                piece[0],
                piece[3],
                queries_all[:, bc_group * STATE : (bc_group + 1) * STATE],
                incoming[low:high],
                piece[4],
                skip_gain[low:high],
            )
        )
    output = (
        jnp.concatenate(results, axis=1).reshape(count_rows, HEADS * HEAD_DIM).astype(jnp.bfloat16)
    )
    return output[None]


def solution(mesh):
    in_specs = (
        P(("groups", "lane"), "ctx", None),
        P(("groups", "lane"), None, "ctx"),
        P(("groups", "lane"), None),
        P(),
        P(),
        P(),
        P(),
    )
    out_specs = P(("groups", "lane"), "ctx", None)
    shards = shard_near if mesh.shape["ctx"] <= 8 else shard_far
    return jax.shard_map(shards, mesh=mesh, in_specs=in_specs, out_specs=out_specs, check_vma=False)
```

```python
import jax
import jax.numpy as jnp
from jax import lax
from jax.experimental import pallas as pl
from jax.experimental.pallas import tpu as pltpu
from jax.sharding import PartitionSpec as P

HEADS = 64
HEAD_DIM = 32
EDGE = 3
STATE = 64
BC_GROUPS = 4
HEADS_GROUP = HEADS // BC_GROUPS
VALUES = HEADS * HEAD_DIM
WIDE = HEADS_GROUP * HEAD_DIM
GROUPED = BC_GROUPS * STATE
CHUNKS = 2
PADS = 4
PER_CHUNK = BC_GROUPS // CHUNKS
HALF = PER_CHUNK * WIDE
ROWS = PER_CHUNK * STATE
TAIL_AT = ROWS
HEAD_AT = ROWS
SENT = ROWS + 16
LOG2E = 1.4426950408889634
VMEM = pl.BlockSpec(memory_space=pltpu.VMEM)
HBM = pl.BlockSpec(memory_space=pltpu.HBM)
f32 = jnp.float32
bf16 = jnp.bfloat16


def iota(shape, dim):
    return lax.broadcasted_iota(jnp.int32, shape, dim)


def dot(a, b, contract=((1,), (0,))):
    return lax.dot_general(a, b, (contract, ((), ())), preferred_element_type=f32)


def is_fresh(lengths_ref, position):
    found = jnp.int32(0)
    start = jnp.int32(0)
    for k in range(lengths_ref.shape[1]):
        found = jnp.where(start == position, jnp.int32(1), found)
        start = start + lengths_ref[0, k]
    return found


def halves(value):
    high = value.astype(bf16)
    return high, (value - high.astype(f32)).astype(bf16)


def cumulative_of(step, rate_row):
    eye = iota((HEADS, HEADS), 0) == iota((HEADS, HEADS), 1)
    rate = jnp.sum(jnp.where(eye, rate_row, 0.0), axis=1, keepdims=True)
    tokens = step.shape[1]
    upto = iota((tokens, tokens), 0) <= iota((tokens, tokens), 1)
    upto = upto.astype(bf16)
    rest = -step * rate
    total = jnp.zeros_like(rest)
    for _ in range(3):
        part = rest.astype(bf16)
        rest = rest - part.astype(f32)
        total = total + dot(part, upto)
    return total


def spread_matrix():
    rows, lanes = 2 * HEADS_GROUP, WIDE
    return (iota((rows, lanes), 0) % HEADS_GROUP == iota((rows, lanes), 1) // HEAD_DIM).astype(bf16)


def spread(per_head, group, matrix):
    part = per_head[group * HEADS_GROUP : (group + 1) * HEADS_GROUP]
    return dot(jnp.concatenate(halves(part), axis=0), matrix, ((0,), (0,)))


def half_silu(half):
    return half + half * jnp.tanh(half)


def to_rows(strip, first):
    rows = iota((8, WIDE), 0)
    top = jnp.zeros((8, WIDE), f32)
    low = jnp.zeros((8, WIDE), f32)
    for k in range(strip.shape[1] // WIDE):
        moved = pltpu.roll(strip[:, k * WIDE : (k + 1) * WIDE], (3 * k - first) % 8, 0)
        if 3 * k < 8:
            top = jnp.where((rows >= 3 * k) & (rows < 3 * k + 3), moved, top)
        if 3 * k + 2 >= 8:
            low = jnp.where((rows >= 3 * k - 8) & (rows < 3 * k - 5), moved, low)
    return jnp.concatenate([top, low], axis=0)


def conv_rows(x, weight, bias, pad_ref):
    count = x.shape[0]
    pad_ref[8 : 8 + count, :] = x
    total = bias + x * weight[3:4]
    for back in range(1, 4):
        total = total + pad_ref[8 - back : 8 - back + count, :] * weight[3 - back : 4 - back]
    return half_silu(total)


def clear(pads_ref):
    for slot in range(PADS):
        pads_ref[slot, :8, :] = jnp.zeros((8, 128), f32)


def half_taps(weight_ref, bias_ref):
    return weight_ref[...].astype(f32) * 0.5, bias_ref[...].astype(f32) * 0.5


def chunk_states(chunk, x_of, key_x, weight, bias, kept, conv_ref, key_ref, sent_ref, pads_ref, wait):
    matrix = spread_matrix()
    lanes = 128
    j = VALUES // lanes + chunk
    clear(pads_ref)
    key = conv_rows(key_x(), weight[:, j * lanes : (j + 1) * lanes], bias[j : j + 1], pads_ref.at[0]).astype(bf16)
    key_ref[...] = key
    for index in range(PER_CHUNK):
        group = chunk * PER_CHUNK + index
        scale = spread(kept, group, matrix)
        wait(index)
        parts = []
        for i in range(WIDE // lanes):
            local = index * WIDE + i * lanes
            j = (chunk * HALF + local) // lanes
            tile = conv_rows(
                x_of(local), weight[:, j * lanes : (j + 1) * lanes], bias[j : j + 1], pads_ref.at[(j + 1) % PADS]
            )
            conv_ref[:, local : local + lanes] = tile.astype(bf16)
            parts.append((tile * scale[:, i * lanes : (i + 1) * lanes]).astype(bf16))
        state = dot(
            key[:, index * STATE : (index + 1) * STATE], jnp.concatenate(parts, axis=1), ((0,), (0,))
        )
        sent_ref[index * STATE : (index + 1) * STATE, :] = state.astype(bf16)


def first_kernel(
    lengths_hbm, x_hbm, step_hbm, weight_hbm, bias_hbm, rate_hbm, skip_hbm,
    conv_ref, key_ref, cumulative_ref, kept_ref, sent_ref, later_ref, query_x_ref, weight_ref, bias_ref, step_ref,
    skip_ref, gates_ref, head_ref,
    lengths_ref, x_ref, key_x_ref, edges_ref, rate_ref, pads_ref, sems,
):
    count = x_ref.shape[0]
    keys_at = VALUES
    pairs = [
        (step_hbm.at[0], step_ref),
        (rate_hbm, rate_ref),
        (lengths_hbm, lengths_ref),
        (weight_hbm, weight_ref),
        (bias_hbm, bias_ref),
        (x_hbm.at[0, :, pl.ds(keys_at, 128)], key_x_ref),
        (x_hbm.at[0, :, pl.ds(0, WIDE)], x_ref.at[:, pl.ds(0, WIDE)]),
        (x_hbm.at[0, :, pl.ds(WIDE, WIDE)], x_ref.at[:, pl.ds(WIDE, WIDE)]),
        (x_hbm.at[0, pl.ds(0, 16), :], edges_ref.at[pl.ds(0, 16), :]),
        (x_hbm.at[0, pl.ds(count - 16, 16), :], edges_ref.at[pl.ds(16, 16), :]),
        (x_hbm.at[0, :, pl.ds(HALF, HALF)], later_ref.at[:, pl.ds(0, HALF)]),
        (x_hbm.at[0, :, pl.ds(keys_at + 128, 128)], later_ref.at[:, pl.ds(HALF, 128)]),
        (x_hbm.at[0, :, pl.ds(keys_at + GROUPED, GROUPED)], query_x_ref),
        (skip_hbm, skip_ref),
    ]
    copies = [pltpu.make_async_copy(a, b, sems.at[i]) for i, (a, b) in enumerate(pairs)]
    for copy in copies:
        copy.start()
    for copy in copies[:7]:
        copy.wait()
    position = lax.axis_index("ctx")
    fresh = is_fresh(lengths_ref, position)
    goes_on = (1 - fresh).astype(f32)
    both = goes_on * (1 - is_fresh(lengths_ref, position - 1)).astype(f32)
    third = jnp.where(position == 2, 1.0, 0.0).astype(f32)
    rows = iota((8, WIDE), 0)
    gates_ref[...] = jnp.where(rows == 0, goes_on, jnp.where(rows == 1, both, third))
    step = step_ref[...]
    cumulative = cumulative_of(step, rate_ref[...])
    cumulative_ref[...] = cumulative
    last = cumulative[:, count - 1 :]
    tail = step * jnp.exp(last - cumulative)
    lanes = iota((HEADS, count), 1)
    kept = jnp.where((lanes >= EDGE) | (fresh == 1), tail, 0.0)
    kept_ref[...] = kept
    weight, bias = half_taps(weight_ref, bias_ref)
    chunk_states(
        0,
        lambda at: x_ref[:, at : at + 128].astype(f32),
        lambda: key_x_ref[...].astype(f32),
        weight, bias, kept, conv_ref, key_ref, sent_ref, pads_ref,
        lambda index: copies[7].wait() if index else None,
    )
    scales = jnp.where(lanes == EDGE, jnp.exp(last), tail)
    high, low = halves(scales)
    place = iota((HEADS, 128), 1) - iota((HEADS, 128), 0)
    picked = dot(high, (place == 0).astype(bf16), ((0,), (0,)))
    picked = picked + dot(low, (place == HEADS).astype(bf16), ((0,), (0,)))
    line = jnp.concatenate([picked[k : k + 1] for k in range(4)], axis=1)
    copies[8].wait()
    copies[9].wait()
    tail_rows = to_rows(edges_ref[16:, :].astype(f32)[8:], 5)
    tail_rows = jnp.where(iota((16, WIDE), 0) == 15, line, tail_rows)
    sent_ref[TAIL_AT : TAIL_AT + 16, :] = tail_rows.astype(bf16)
    head_ref[...] = edges_ref[:16, :]
    for copy in copies[10:]:
        copy.wait()


def later_kernel(
    x_ref, head_ref, weight_ref, bias_ref, kept_ref, before_ref, conv_ref, key_ref, sent_ref, early_ref, pads_ref
):
    weight, bias = half_taps(weight_ref, bias_ref)
    chunk_states(
        1,
        lambda at: x_ref[:, at : at + 128].astype(f32),
        lambda: x_ref[:, HALF : HALF + 128].astype(f32),
        weight, bias, kept_ref[...], conv_ref, key_ref, sent_ref, pads_ref,
        lambda index: None,
    )
    sent_ref[HEAD_AT : HEAD_AT + 16, :] = to_rows(head_ref[...].astype(f32)[:8], 0).astype(bf16)
    early_ref[:ROWS, :] = before_ref[:ROWS, :]
    early_ref[ROWS : 2 * ROWS, :] = sent_ref[:ROWS, :]
    early_ref[2 * ROWS :, :] = before_ref[TAIL_AT : TAIL_AT + 16, :]


def known_part(head_block, table_ref):
    return (
        table_ref[0]
        + head_block * table_ref[1]
        + pltpu.roll(head_block, 1, 0) * table_ref[2]
        + pltpu.roll(head_block, 2, 0) * table_ref[3]
    )


def edge_rows(tail_block, known, table_ref):
    block = half_silu(
        known
        + tail_block * table_ref[4]
        + pltpu.roll(tail_block, 15, 0) * table_ref[5]
        + pltpu.roll(tail_block, 14, 0) * table_ref[6]
    )
    return [pltpu.roll(block, (16 - 3 * k) % 16, 0)[:8] for k in range(5)]


def head_lanes(rows):
    lanes = iota((128, VALUES), 1) // HEAD_DIM
    matrix = (iota((128, VALUES), 0) % HEADS == lanes).astype(bf16)
    return dot(rows, matrix)[:8]


def edge_scales(tail_rows):
    line = tail_rows[15:16].astype(f32)
    rows = [line[:, k * 128 : (k + 1) * 128] for k in range(4)]
    return head_lanes(jnp.concatenate(rows + [jnp.zeros((12, 128), f32)], axis=0).astype(bf16))


def prepare_kernel(
    own_ref, later_ref, query_x_ref, weight_ref, bias_ref, cumulative_ref, step_ref, skip_ref, gates_ref,
    queries_ref, table_ref, known_ref, scale_ref, decay_ref, entry_ref, gain_ref, pads_ref,
):
    clear(pads_ref)
    weight, bias = half_taps(weight_ref, bias_ref)
    rows = iota((16, WIDE), 0)
    third = rows % 3
    chunk = rows // 3

    def blocked(lines):
        out = jnp.zeros((16, WIDE), f32)
        for k in range(5):
            out = jnp.where(chunk == k, lines[k], out)
        return out

    taps = [
        blocked([weight[tap : tap + 1, k * WIDE : (k + 1) * WIDE] for k in range(5)])
        for tap in range(4)
    ]
    table_ref[0] = blocked(
        [
            jnp.concatenate([bias[4 * k + i : 4 * k + i + 1, :] for i in range(4)], axis=1)
            for k in range(5)
        ]
    )
    table_ref[1] = taps[3]
    table_ref[2] = jnp.where(third == 0, 0.0, taps[2])
    table_ref[3] = jnp.where(third == 2, taps[1], 0.0)
    table_ref[4] = taps[0]
    table_ref[5] = jnp.where(third == 2, 0.0, taps[1])
    table_ref[6] = jnp.where(third == 0, taps[2], 0.0)
    known_ref[...] = known_part(later_ref[HEAD_AT : HEAD_AT + 16, :].astype(f32), table_ref)
    scale_ref[...] = edge_scales(own_ref[TAIL_AT : TAIL_AT + 16, :]) * gates_ref[:1, :1]
    cumulative = cumulative_ref[...] * LOG2E
    across = cumulative - jnp.log2(step_ref[...])
    down = cumulative.T
    count = down.shape[0]
    causal = iota((count, count), 0) >= iota((count, count), 1)
    for at in range(HEADS):
        gap = down[:, at : at + 1] - across[at : at + 1, :]
        decay_ref[at] = jnp.exp2(jnp.where(causal, gap, -1e30))
    matrix = spread_matrix()
    entry = jnp.exp2(cumulative)
    for group in range(BC_GROUPS):
        entry_ref[:, group * WIDE : (group + 1) * WIDE] = spread(entry, group, matrix)
    gain_ref[...] = head_lanes(
        jnp.concatenate(halves(skip_ref[...] + jnp.zeros((16, HEADS), f32)), axis=1)
    )
    first = VALUES + GROUPED
    for i in range(2):
        cols = slice(first + i * 128, first + (i + 1) * 128)
        j = first // 128 + i
        tile = conv_rows(
            query_x_ref[:, i * 128 : (i + 1) * 128].astype(f32), weight[:, cols], bias[j : j + 1, :], pads_ref.at[i]
        )
        queries_ref[:, i * 128 : (i + 1) * 128] = tile.astype(bf16)


def edge_state(values_rows, keys_rows, scale, group):
    rows = iota((8, WIDE), 0)
    written = jnp.where(rows < EDGE, values_rows * scale, 0.0)
    tile = keys_rows[:, (group // 2) * 128 : (group // 2 + 1) * 128].astype(bf16)
    return dot(tile[:, (group % 2) * STATE : (group % 2 + 1) * STATE], written.astype(bf16), ((0,), (0,)))


def combine_chunk(chunk, own_ref, got_ref, scale_ref, sent_ref, edge_of):
    keys = edge_of(BC_GROUPS)
    for index in range(PER_CHUNK):
        group = chunk * PER_CHUNK + index
        at = slice(index * STATE, (index + 1) * STATE)
        scale = scale_ref[:, group * WIDE : (group + 1) * WIDE]
        extra = edge_state(edge_of(group), keys, scale, group)
        total = own_ref[at, :].astype(f32) + extra + scale[EDGE : EDGE + 1] * got_ref[at, :].astype(f32)
        sent_ref[at, :] = total.astype(bf16)


def combine_first_kernel(own_ref, got_ref, table_ref, known_ref, gates_ref, scale_ref, sent_ref, edge_ref):
    tail_block = got_ref[TAIL_AT : TAIL_AT + 16, :].astype(f32) * gates_ref[:1, :]
    chunks = edge_rows(tail_block, known_ref[...], table_ref)
    combine_chunk(0, own_ref, got_ref, scale_ref, sent_ref, lambda k: chunks[k])
    sent_ref[ROWS:, :] = own_ref[TAIL_AT : TAIL_AT + 16, :]
    for k in range(5):
        edge_ref[:, k * WIDE : (k + 1) * WIDE] = chunks[k]


def combine_later_kernel(own_ref, got_ref, scale_ref, edge_ref, sent_ref):
    combine_chunk(
        1, own_ref, got_ref, scale_ref, sent_ref, lambda k: edge_ref[:, k * WIDE : (k + 1) * WIDE]
    )


def diagonal_kernel(
    conv0_ref, conv1_ref, key0_ref, key1_ref, raw_queries_ref, edge_ref, decay_ref, gain_ref,
    got_ref, later_ref, table_ref, gates_ref,
    diagonal_ref, queries_ref, known_ref, scale_ref,
):
    known_ref[...] = known_part(later_ref[HEAD_AT : HEAD_AT + 16, :].astype(f32), table_ref)
    scale_ref[...] = edge_scales(got_ref[TAIL_AT : TAIL_AT + 16, :]) * gates_ref[1:2, :1]
    count = conv0_ref.shape[0]
    edge_row = iota((count, 128), 0) < EDGE
    lane_head = iota((count, 128), 1) // HEAD_DIM

    def patched(tile, j):
        rows = jnp.concatenate(
            [edge_ref[:, j * 128 : (j + 1) * 128], jnp.zeros((count - 8, 128), f32)], axis=0
        )
        return jnp.where(edge_row, rows, tile.astype(f32))

    keys = [patched(ref[...], 16 + i).astype(bf16) for i, ref in enumerate((key0_ref, key1_ref))]
    queries = [
        patched(raw_queries_ref[:, i * 128 : (i + 1) * 128], 18 + i).astype(bf16) for i in range(2)
    ]
    for i in range(2):
        queries_ref[:, i * 128 : (i + 1) * 128] = queries[i]
    for group in range(BC_GROUPS):
        part = slice((group % 2) * STATE, (group % 2 + 1) * STATE)
        scores = dot(queries[group // 2][:, part], keys[group // 2][:, part], ((1,), (1,)))
        conv_ref = (conv0_ref, conv1_ref)[group // PER_CHUNK]
        for i in range(4):
            j = group * 4 + i
            cols = slice(j * 128, (j + 1) * 128)
            at = (j * 128) % HALF
            values = patched(conv_ref[:, at : at + 128], j)
            weights, parts = [], []
            for k in range(4):
                at = 4 * j + k
                weights.append((decay_ref[at] * scores).astype(bf16))
                parts.append(jnp.where(lane_head == k, values, 0.0).astype(bf16))
            total = dot(jnp.concatenate(weights, axis=1), jnp.concatenate(parts, axis=0))
            diagonal_ref[:, cols] = total + gain_ref[:1, cols] * values


def group_out(group, total, diagonal_ref, queries_ref, entry_ref):
    cols = slice(group * WIDE, (group + 1) * WIDE)
    low = (group % 2) * STATE
    tile = queries_ref[:, (group // 2) * 128 : (group // 2 + 1) * 128]
    carried = dot(tile[:, low : low + STATE], total.astype(bf16))
    return (diagonal_ref[:, cols] + entry_ref[:, cols] * carried).astype(bf16)


def finish_first_kernel(
    first0_ref, first1_ref, second_ref, early_ref, table_ref, known_ref, gates_ref, scale_ref, diagonal_ref,
    queries_ref, entry_ref,
    out_ref, base_ref,
):
    third = gates_ref[2:3, :] > 0.5
    kept = gates_ref[:1, :]

    def second_of(at, early_at, rows):
        a = second_ref[at : at + rows, :].astype(f32)
        return jnp.where(third, early_ref[early_at : early_at + rows, :].astype(f32), a)

    chunks = edge_rows(second_of(ROWS, 2 * ROWS, 16), known_ref[...], table_ref)
    for group in range(BC_GROUPS):
        chunk, index = divmod(group, PER_CHUNK)
        at = slice(index * STATE, (index + 1) * STATE)
        scale = scale_ref[:, group * WIDE : (group + 1) * WIDE]
        first = (first0_ref, first1_ref)[chunk][at, :].astype(f32)
        total = first * kept + edge_state(chunks[group], chunks[BC_GROUPS], scale, group)
        if chunk == 0:
            total = total + scale[EDGE : EDGE + 1] * second_of(index * STATE, index * STATE, STATE)
            out_ref[:, group * WIDE : (group + 1) * WIDE] = group_out(
                group, total, diagonal_ref, queries_ref, entry_ref
            )
        else:
            base_ref[at, :] = total


def finish_later_kernel(
    second_ref, early_ref, base_ref, gates_ref, scale_ref, diagonal_ref, queries_ref, entry_ref, before_ref,
    out_hbm, out_ref, sems,
):
    third = gates_ref[2:3, :] > 0.5
    copies = [
        pltpu.make_async_copy(before_ref, out_hbm.at[0, :, pl.ds(0, HALF)], sems.at[PER_CHUNK])
    ]
    copies[0].start()
    for index in range(PER_CHUNK):
        group = PER_CHUNK + index
        at = slice(index * STATE, (index + 1) * STATE)
        early = early_ref[ROWS + index * STATE : ROWS + (index + 1) * STATE, :].astype(f32)
        second = jnp.where(third, early, second_ref[at, :].astype(f32))
        decay = scale_ref[EDGE : EDGE + 1, group * WIDE : (group + 1) * WIDE]
        total = base_ref[at, :] + decay * second
        here = pl.ds(index * WIDE, WIDE)
        out_ref[:, here] = group_out(group, total, diagonal_ref, queries_ref, entry_ref)
        copy = pltpu.make_async_copy(
            out_ref.at[:, here], out_hbm.at[0, :, pl.ds(group * WIDE, WIDE)], sems.at[index]
        )
        copy.start()
        copies.append(copy)
    for copy in copies:
        copy.wait()


def call(kernel, outs, in_specs, cost, args, out_specs=None, scratch=()):
    return pl.pallas_call(
        kernel,
        out_shape=outs,
        in_specs=in_specs,
        out_specs=out_specs or jax.tree.map(lambda _: VMEM, outs),
        scratch_shapes=scratch,
        compiler_params=pltpu.CompilerParams(vmem_limit_bytes=24 * 1024 * 1024),
        cost_estimate=pl.CostEstimate(flops=cost[0], bytes_accessed=cost[1], transcendentals=0),
    )(*args)


def permuted(array, edges):
    size, lanes = lax.axis_size("ctx"), lax.axis_size("lane")
    table = []
    for source in range(size):
        for lane in range(lanes):
            if source in edges:
                target = edges[source] * lanes + lane
            else:
                target = source * lanes + (lane + 1) % lanes
            table.append((source * lanes + lane, target))
    return lax.ppermute(array, ("ctx", "lane"), table)


def shard_near(pre_conv, step_size, lengths, conv_weight, conv_bias, decay_rate, skip_gain):
    count, channels = pre_conv.shape[1:]
    size = lax.axis_size("ctx")
    ring = [(i, (i + 1) % size) for i in range(size)]
    onward = {i: i + 2 for i in range(1, size - 2)}
    onward[size - 2] = 2
    onward[size - 1] = 1
    arguments = tuple(
        pltpu.with_memory_space_constraint(array, pltpu.HBM)
        for array in (
            lengths,
            pre_conv,
            step_size,
            conv_weight,
            conv_bias.reshape(-1, 128),
            decay_rate.reshape(1, -1),
            skip_gain.reshape(1, -1),
        )
    )
    sds = jax.ShapeDtypeStruct
    pads = pltpu.VMEM((PADS, count + 8, 128), f32)
    conv0, key0, cumulative, kept, own0, later_x, query_x, weight, bias, step, skip, gates, head = call(
        first_kernel,
        (
            sds((count, HALF), bf16),
            sds((count, 128), bf16),
            sds((HEADS, count), f32),
            sds((HEADS, count), f32),
            sds((SENT, WIDE), bf16),
            sds((count, HALF + 128), bf16),
            sds((count, GROUPED), bf16),
            sds(conv_weight.shape, bf16),
            sds((channels // 128, 128), bf16),
            sds((HEADS, count), f32),
            sds((1, HEADS), f32),
            sds((8, WIDE), f32),
            sds((16, channels), bf16),
        ),
        [HBM] * 7,
        (40_000_000, 2_000_000),
        arguments,
        scratch=(
            pltpu.SMEM(lengths.shape, jnp.int32),
            pltpu.VMEM((count, HALF), bf16),
            pltpu.VMEM((count, 128), bf16),
            pltpu.VMEM((32, channels), bf16),
            pltpu.VMEM((1, HEADS), f32),
            pads,
            pltpu.SemaphoreType.DMA((14,)),
        ),
    )
    first0 = lax.ppermute(own0, "ctx", ring)
    conv1, key1, own1, early = call(
        later_kernel,
        (
            sds((count, HALF), bf16),
            sds((count, 128), bf16),
            sds((SENT, WIDE), bf16),
            sds((2 * ROWS + 16, WIDE), bf16),
        ),
        [VMEM] * 6,
        (40_000_000, 2_000_000),
        (later_x, head, weight, bias, kept, own0),
        scratch=(pads,),
    )
    first1 = lax.ppermute(own1, "ctx", ring)
    early = permuted(early, {0: 2, 2: 0})
    raw_queries, table, known, scale, decay, entry, gain = call(
        prepare_kernel,
        (
            sds((count, GROUPED), bf16),
            sds((7, 16, WIDE), f32),
            sds((16, WIDE), f32),
            sds((8, VALUES), f32),
            sds((HEADS, count, count), f32),
            sds((count, VALUES), f32),
            sds((8, VALUES), f32),
        ),
        [VMEM] * 9,
        (100_000_000, 1_000_000),
        (own0, own1, query_x, weight, bias, cumulative, step, skip, gates),
        scratch=(pads,),
    )
    sent0, edge = call(
        combine_first_kernel,
        (sds((ROWS + 16, WIDE), bf16), sds((8, channels), f32)),
        [VMEM] * 6,
        (1_000_000, 1_000_000),
        (own0, first0, table, known, gates, scale),
    )
    second0 = permuted(sent0, onward)
    sent1 = call(
        combine_later_kernel,
        sds((ROWS, WIDE), bf16),
        [VMEM] * 4,
        (1_000_000, 1_000_000),
        (own1, first1, scale, edge),
    )
    second1 = permuted(sent1, onward)
    diagonal, queries, known, scale = call(
        diagonal_kernel,
        (
            sds((count, VALUES), f32),
            sds((count, GROUPED), bf16),
            sds((16, WIDE), f32),
            sds((8, VALUES), f32),
        ),
        [VMEM] * 12,
        (400_000_000, 4_000_000),
        (conv0, conv1, key0, key1, raw_queries, edge, decay, gain, first0, first1, table, gates),
    )
    out0, base = call(
        finish_first_kernel,
        (sds((count, HALF), bf16), sds((ROWS, WIDE), f32)),
        [VMEM] * 11,
        (50_000_000, 2_000_000),
        (first0, first1, second0, early, table, known, gates, scale, diagonal, queries, entry),
    )
    return call(
        finish_later_kernel,
        sds((1, count, VALUES), bf16),
        [VMEM] * 9,
        (50_000_000, 2_000_000),
        (second1, early, base, gates, scale, diagonal, queries, entry, out0),
        out_specs=HBM,
        scratch=(pltpu.VMEM((count, HALF), bf16), pltpu.SemaphoreType.DMA((PER_CHUNK + 1,))),
    )


def shifted(value, axis, steps):
    count = lax.axis_size(axis)
    first, last = (max(0, -steps), min(count, count - steps))
    return lax.ppermute(value, axis, [(source, source + steps) for source in range(first, last)])


def carried_in(array, axis, combine, identity):
    length, index = (lax.axis_size(axis), lax.axis_index(axis))
    everything = jax.tree.map(
        lambda part, kind: lax.all_gather(part.astype(kind), axis),
        array,
        (jnp.bfloat16, jnp.bfloat16),
    )
    start = jax.tree.map(
        lambda part, zero: jnp.broadcast_to(jnp.asarray(zero, part.dtype), part.shape),
        array,
        identity,
    )

    def step(k, before):
        reached = k < index
        new = combine(
            before, jax.tree.map(lambda part, own: part[k].astype(own.dtype), everything, array)
        )
        return jax.tree.map(lambda a, b: jnp.where(reached, a, b), new, before)

    return lax.fori_loop(0, length, step, start)


def convolve(padded, conv_weight, conv_bias, count_rows):
    total = conv_bias.astype(jnp.float32)[None, :]
    for offset in range(conv_weight.shape[0]):
        total = (
            total
            + padded[offset : offset + count_rows].astype(jnp.float32)
            * conv_weight[offset].astype(jnp.float32)[None, :]
        )
    return jax.nn.silu(total).astype(jnp.bfloat16)


def group_terms(values, keys_in, queries, decay_rate, step_rows):
    heads_group = step_rows.shape[0]
    count_rows = step_rows.shape[1]
    values = values.reshape(count_rows, heads_group, -1)
    cumulative = jnp.cumsum(-step_rows * decay_rate[:, None], axis=1)
    scores = jnp.einsum("tn,sn->ts", queries, keys_in, preferred_element_type=jnp.float32)
    later = lax.broadcasted_iota(jnp.int32, (count_rows, count_rows), 0)
    earlier = lax.broadcasted_iota(jnp.int32, (count_rows, count_rows), 1)
    spread = jnp.where(
        (later >= earlier)[None], cumulative[:, :, None] - cumulative[:, None, :], -1e30
    )
    weights = (jnp.exp(spread) * scores[None]).astype(jnp.bfloat16)
    scaled = (values * step_rows.T[:, :, None]).astype(jnp.bfloat16)
    diagonal_part = jnp.einsum("hts,shp->thp", weights, scaled, preferred_element_type=jnp.float32)
    tail_weight = jnp.exp(cumulative[:, -1:] - cumulative)
    written = (values * (step_rows * tail_weight).T[:, :, None]).astype(jnp.bfloat16)
    local_state = jnp.einsum("tn,thp->hpn", keys_in, written, preferred_element_type=jnp.float32)
    return (diagonal_part, local_state, jnp.exp(cumulative[:, -1]), jnp.exp(cumulative), values)


def finish_group(diagonal_part, entry_decay, queries, incoming, values, skip_gain):
    incoming_rounded = incoming.astype(jnp.bfloat16)
    carried_part = jnp.einsum(
        "tn,hpn->thp", queries, incoming_rounded, preferred_element_type=jnp.float32
    )
    carried_part = carried_part * entry_decay.T[:, :, None]
    return diagonal_part + carried_part + skip_gain[None, :, None] * values.astype(jnp.float32)


def combine(earlier, later):
    return (earlier[0] * later[0], later[0][:, None, None] * earlier[1] + later[1])


def shard_far(pre_conv, step_size, lengths, conv_weight, conv_bias, decay_rate, skip_gain):
    count_rows = pre_conv.shape[1]
    kernel_len = conv_weight.shape[0]
    heads_group = HEADS // BC_GROUPS
    position = lax.axis_index("ctx")
    sizes_row = lengths[0]
    starts = jnp.cumsum(sizes_row) - sizes_row
    fresh = jnp.any(starts == position)
    retain = jnp.where(fresh, 0.0, 1.0).astype(jnp.float32)
    own_rows = pre_conv[0]
    previous = shifted(own_rows[count_rows - kernel_len + 1 :], "ctx", 1)
    previous = jnp.where(fresh, jnp.zeros_like(previous), previous)
    convolved = convolve(
        jnp.concatenate([previous, own_rows], axis=0), conv_weight, conv_bias, count_rows
    )
    values = convolved[:, : HEADS * HEAD_DIM]
    keys_all = convolved[:, HEADS * HEAD_DIM : HEADS * HEAD_DIM + BC_GROUPS * STATE]
    queries_all = convolved[:, HEADS * HEAD_DIM + BC_GROUPS * STATE :]
    step_rows = step_size[0]
    results = []
    pieces = []
    for bc_group in range(BC_GROUPS):
        low = bc_group * heads_group
        high = low + heads_group
        pieces.append(
            group_terms(
                values[:, low * HEAD_DIM : high * HEAD_DIM],
                keys_all[:, bc_group * STATE : (bc_group + 1) * STATE],
                queries_all[:, bc_group * STATE : (bc_group + 1) * STATE],
                decay_rate[low:high],
                step_rows[low:high],
            )
        )
    decays = jnp.concatenate([piece[2] for piece in pieces], axis=0) * retain
    states = jnp.concatenate([piece[1] for piece in pieces], axis=0)
    identity = (jnp.ones_like(decays), jnp.zeros_like(states))
    totals = carried_in((decays, states), "ctx", combine, identity)
    incoming = totals[1] * retain
    for bc_group in range(BC_GROUPS):
        low = bc_group * heads_group
        high = low + heads_group
        piece = pieces[bc_group]
        results.append(
            finish_group(
                piece[0],
                piece[3],
                queries_all[:, bc_group * STATE : (bc_group + 1) * STATE],
                incoming[low:high],
                piece[4],
                skip_gain[low:high],
            )
        )
    output = (
        jnp.concatenate(results, axis=1).reshape(count_rows, HEADS * HEAD_DIM).astype(jnp.bfloat16)
    )
    return output[None]


def solution(mesh):
    in_specs = (
        P(("groups", "lane"), "ctx", None),
        P(("groups", "lane"), None, "ctx"),
        P(("groups", "lane"), None),
        P(),
        P(),
        P(),
        P(),
    )
    out_specs = P(("groups", "lane"), "ctx", None)
    shards = shard_near if mesh.shape["ctx"] <= 8 else shard_far
    return jax.shard_map(shards, mesh=mesh, in_specs=in_specs, out_specs=out_specs, check_vma=False)
```

```python
import jax
import jax.numpy as jnp
from jax import lax
from jax.experimental import pallas as pl
from jax.experimental.pallas import tpu as pltpu
from jax.sharding import PartitionSpec as P

HEADS = 64
HEAD_DIM = 32
EDGE = 3
STATE = 64
BC_GROUPS = 4
HEADS_GROUP = HEADS // BC_GROUPS
VALUES = HEADS * HEAD_DIM
WIDE = HEADS_GROUP * HEAD_DIM
GROUPED = BC_GROUPS * STATE
CHUNKS = 2
PADS = 4
ORDER = (0, 1, 2, 5, 3, 4, 6)
PER_CHUNK = BC_GROUPS // CHUNKS
HALF = PER_CHUNK * WIDE
ROWS = PER_CHUNK * STATE
TAIL_AT = ROWS
HEAD_AT = ROWS
SENT = ROWS + 16
LOG2E = 1.4426950408889634
VMEM = pl.BlockSpec(memory_space=pltpu.VMEM)
HBM = pl.BlockSpec(memory_space=pltpu.HBM)
f32 = jnp.float32
bf16 = jnp.bfloat16


def iota(shape, dim):
    return lax.broadcasted_iota(jnp.int32, shape, dim)


def dot(a, b, contract=((1,), (0,))):
    return lax.dot_general(a, b, (contract, ((), ())), preferred_element_type=f32)


def is_fresh(lengths_ref, position):
    found = jnp.int32(0)
    start = jnp.int32(0)
    for k in range(lengths_ref.shape[1]):
        found = jnp.where(start == position, jnp.int32(1), found)
        start = start + lengths_ref[0, k]
    return found


def halves(value):
    high = value.astype(bf16)
    return high, (value - high.astype(f32)).astype(bf16)


def cumulative_of(step, rate_row):
    eye = iota((HEADS, HEADS), 0) == iota((HEADS, HEADS), 1)
    rate = jnp.sum(jnp.where(eye, rate_row, 0.0), axis=1, keepdims=True)
    tokens = step.shape[1]
    upto = iota((tokens, tokens), 0) <= iota((tokens, tokens), 1)
    upto = upto.astype(bf16)
    rest = -step * rate
    total = jnp.zeros_like(rest)
    for _ in range(3):
        part = rest.astype(bf16)
        rest = rest - part.astype(f32)
        total = total + dot(part, upto)
    return total


def spread_matrix():
    rows, lanes = 2 * HEADS_GROUP, WIDE
    return (iota((rows, lanes), 0) % HEADS_GROUP == iota((rows, lanes), 1) // HEAD_DIM).astype(bf16)


def spread(per_head, group, matrix):
    part = per_head[group * HEADS_GROUP : (group + 1) * HEADS_GROUP]
    return dot(jnp.concatenate(halves(part), axis=0), matrix, ((0,), (0,)))


def half_silu(half):
    return half + half * jnp.tanh(half)


def to_rows(strip, first):
    rows = iota((8, WIDE), 0)
    top = jnp.zeros((8, WIDE), f32)
    low = jnp.zeros((8, WIDE), f32)
    for k in range(strip.shape[1] // WIDE):
        moved = pltpu.roll(strip[:, k * WIDE : (k + 1) * WIDE], (3 * k - first) % 8, 0)
        if 3 * k < 8:
            top = jnp.where((rows >= 3 * k) & (rows < 3 * k + 3), moved, top)
        if 3 * k + 2 >= 8:
            low = jnp.where((rows >= 3 * k - 8) & (rows < 3 * k - 5), moved, low)
    return jnp.concatenate([top, low], axis=0)


def conv_rows(x, weight, bias, pad_ref):
    count = x.shape[0]
    pad_ref[8 : 8 + count, :] = x
    total = bias + x * weight[3:4]
    for back in range(1, 4):
        total = total + pad_ref[8 - back : 8 - back + count, :] * weight[3 - back : 4 - back]
    return half_silu(total)


def clear(pads_ref):
    for slot in range(PADS):
        pads_ref[slot, :8, :] = jnp.zeros((8, 128), f32)


def half_taps(weight_ref, bias_ref):
    return weight_ref[...].astype(f32) * 0.5, bias_ref[...].astype(f32) * 0.5


def chunk_states(chunk, x_ref, weight, bias, kept, conv_ref, key_ref, sent_ref, pads_ref):
    matrix = spread_matrix()
    clear(pads_ref)

    def conv_tile(j):
        cols = slice(j * 128, (j + 1) * 128)
        return conv_rows(x_ref[:, cols].astype(f32), weight[:, cols], bias[j : j + 1], pads_ref.at[j % PADS])

    key = conv_tile(VALUES // 128 + chunk).astype(bf16)
    key_ref[...] = key
    for index in range(PER_CHUNK):
        group = chunk * PER_CHUNK + index
        scale = spread(kept, group, matrix)
        parts = []
        for i in range(WIDE // 128):
            local = index * WIDE + i * 128
            tile = conv_tile((chunk * HALF + local) // 128)
            conv_ref[:, local : local + 128] = tile.astype(bf16)
            parts.append((tile * scale[:, i * 128 : (i + 1) * 128]).astype(bf16))
        state = dot(
            key[:, index * STATE : (index + 1) * STATE], jnp.concatenate(parts, axis=1), ((0,), (0,))
        )
        sent_ref[index * STATE : (index + 1) * STATE, :] = state.astype(bf16)


def first_kernel(
    lengths_hbm, x_hbm, step_hbm, weight_hbm, bias_hbm, rate_hbm, skip_hbm,
    conv_ref, key_ref, cumulative_ref, kept_ref, sent_ref, x_ref, weight_ref, bias_ref, step_ref, skip_ref, gates_ref,
    lengths_ref, rate_ref, pads_ref, sems,
):
    count = x_ref.shape[0]
    pairs = [
        (step_hbm.at[0], step_ref),
        (rate_hbm, rate_ref),
        (lengths_hbm, lengths_ref),
        (weight_hbm, weight_ref),
        (bias_hbm, bias_ref),
        (x_hbm.at[0], x_ref),
        (skip_hbm, skip_ref),
    ]
    copies = [pltpu.make_async_copy(a, b, sems.at[i]) for i, (a, b) in enumerate(pairs)]
    for i in ORDER:
        copies[i].start()
    for copy in copies[:3]:
        copy.wait()
    position = lax.axis_index("ctx")
    fresh = is_fresh(lengths_ref, position)
    goes_on = (1 - fresh).astype(f32)
    both = goes_on * (1 - is_fresh(lengths_ref, position - 1)).astype(f32)
    third = jnp.where(position == 2, 1.0, 0.0).astype(f32)
    rows = iota((8, WIDE), 0)
    gates_ref[...] = jnp.where(rows == 0, goes_on, jnp.where(rows == 1, both, third))
    step = step_ref[...]
    cumulative = cumulative_of(step, rate_ref[...])
    cumulative_ref[...] = cumulative
    last = cumulative[:, count - 1 :]
    tail = step * jnp.exp(last - cumulative)
    lanes = iota((HEADS, count), 1)
    kept = jnp.where((lanes >= EDGE) | (fresh == 1), tail, 0.0)
    kept_ref[...] = kept
    for copy in copies[3:6]:
        copy.wait()
    weight, bias = half_taps(weight_ref, bias_ref)
    chunk_states(
        0,
        x_ref, weight, bias, kept, conv_ref, key_ref, sent_ref, pads_ref,
    )
    scales = jnp.where(lanes == EDGE, jnp.exp(last), tail)
    high, low = halves(scales)
    place = iota((HEADS, 128), 1) - iota((HEADS, 128), 0)
    picked = dot(high, (place == 0).astype(bf16), ((0,), (0,)))
    picked = picked + dot(low, (place == HEADS).astype(bf16), ((0,), (0,)))
    line = jnp.concatenate([picked[k : k + 1] for k in range(4)], axis=1)
    tail_rows = to_rows(x_ref[count - 16 :, :].astype(f32)[8:], 5)
    tail_rows = jnp.where(iota((16, WIDE), 0) == 15, line, tail_rows)
    sent_ref[TAIL_AT : TAIL_AT + 16, :] = tail_rows.astype(bf16)
    copies[6].wait()


def later_kernel(
    x_ref, weight_ref, bias_ref, kept_ref, before_ref, conv_ref, key_ref, sent_ref, early_ref, pads_ref
):
    weight, bias = half_taps(weight_ref, bias_ref)
    chunk_states(
        1,
        x_ref, weight, bias, kept_ref[...], conv_ref, key_ref, sent_ref, pads_ref,
    )
    sent_ref[HEAD_AT : HEAD_AT + 16, :] = to_rows(x_ref[:16, :].astype(f32)[:8], 0).astype(bf16)
    early_ref[:ROWS, :] = before_ref[:ROWS, :]
    early_ref[ROWS : 2 * ROWS, :] = sent_ref[:ROWS, :]
    early_ref[2 * ROWS :, :] = before_ref[TAIL_AT : TAIL_AT + 16, :]


def known_part(head_block, table_ref):
    return (
        table_ref[0]
        + head_block * table_ref[1]
        + pltpu.roll(head_block, 1, 0) * table_ref[2]
        + pltpu.roll(head_block, 2, 0) * table_ref[3]
    )


def edge_rows(tail_block, known, table_ref):
    block = half_silu(
        known
        + tail_block * table_ref[4]
        + pltpu.roll(tail_block, 15, 0) * table_ref[5]
        + pltpu.roll(tail_block, 14, 0) * table_ref[6]
    )
    return [pltpu.roll(block, (16 - 3 * k) % 16, 0)[:8] for k in range(5)]


def head_lanes(rows):
    lanes = iota((128, VALUES), 1) // HEAD_DIM
    matrix = (iota((128, VALUES), 0) % HEADS == lanes).astype(bf16)
    return dot(rows, matrix)[:8]


def edge_scales(tail_rows):
    line = tail_rows[15:16].astype(f32)
    rows = [line[:, k * 128 : (k + 1) * 128] for k in range(4)]
    return head_lanes(jnp.concatenate(rows + [jnp.zeros((12, 128), f32)], axis=0).astype(bf16))


def prepare_kernel(
    own_ref, later_ref, x_ref, weight_ref, bias_ref, cumulative_ref, step_ref, skip_ref, gates_ref,
    queries_ref, table_ref, known_ref, scale_ref, decay_ref, entry_ref, gain_ref, pads_ref,
):
    clear(pads_ref)
    weight, bias = half_taps(weight_ref, bias_ref)
    rows = iota((16, WIDE), 0)
    third = rows % 3
    chunk = rows // 3

    def blocked(lines):
        out = jnp.zeros((16, WIDE), f32)
        for k in range(5):
            out = jnp.where(chunk == k, lines[k], out)
        return out

    taps = [
        blocked([weight[tap : tap + 1, k * WIDE : (k + 1) * WIDE] for k in range(5)])
        for tap in range(4)
    ]
    table_ref[0] = blocked(
        [
            jnp.concatenate([bias[4 * k + i : 4 * k + i + 1, :] for i in range(4)], axis=1)
            for k in range(5)
        ]
    )
    table_ref[1] = taps[3]
    table_ref[2] = jnp.where(third == 0, 0.0, taps[2])
    table_ref[3] = jnp.where(third == 2, taps[1], 0.0)
    table_ref[4] = taps[0]
    table_ref[5] = jnp.where(third == 2, 0.0, taps[1])
    table_ref[6] = jnp.where(third == 0, taps[2], 0.0)
    known_ref[...] = known_part(later_ref[HEAD_AT : HEAD_AT + 16, :].astype(f32), table_ref)
    scale_ref[...] = edge_scales(own_ref[TAIL_AT : TAIL_AT + 16, :]) * gates_ref[:1, :1]
    cumulative = cumulative_ref[...] * LOG2E
    across = cumulative - jnp.log2(step_ref[...])
    down = cumulative.T
    count = down.shape[0]
    causal = iota((count, count), 0) >= iota((count, count), 1)
    for at in range(HEADS):
        gap = down[:, at : at + 1] - across[at : at + 1, :]
        decay_ref[at] = jnp.exp2(jnp.where(causal, gap, -1e30))
    matrix = spread_matrix()
    entry = jnp.exp2(cumulative)
    for group in range(BC_GROUPS):
        entry_ref[:, group * WIDE : (group + 1) * WIDE] = spread(entry, group, matrix)
    gain_ref[...] = head_lanes(
        jnp.concatenate(halves(skip_ref[...] + jnp.zeros((16, HEADS), f32)), axis=1)
    )
    first = VALUES + GROUPED
    for i in range(2):
        cols = slice(first + i * 128, first + (i + 1) * 128)
        j = first // 128 + i
        tile = conv_rows(
            x_ref[:, cols].astype(f32), weight[:, cols], bias[j : j + 1, :], pads_ref.at[i]
        )
        queries_ref[:, i * 128 : (i + 1) * 128] = tile.astype(bf16)


def edge_state(values_rows, keys_rows, scale, group):
    rows = iota((8, WIDE), 0)
    written = jnp.where(rows < EDGE, values_rows * scale, 0.0)
    tile = keys_rows[:, (group // 2) * 128 : (group // 2 + 1) * 128].astype(bf16)
    return dot(tile[:, (group % 2) * STATE : (group % 2 + 1) * STATE], written.astype(bf16), ((0,), (0,)))


def combine_chunk(chunk, own_ref, got_ref, scale_ref, sent_ref, edge_of):
    keys = edge_of(BC_GROUPS)
    for index in range(PER_CHUNK):
        group = chunk * PER_CHUNK + index
        at = slice(index * STATE, (index + 1) * STATE)
        scale = scale_ref[:, group * WIDE : (group + 1) * WIDE]
        extra = edge_state(edge_of(group), keys, scale, group)
        total = own_ref[at, :].astype(f32) + extra + scale[EDGE : EDGE + 1] * got_ref[at, :].astype(f32)
        sent_ref[at, :] = total.astype(bf16)


def combine_first_kernel(own_ref, got_ref, table_ref, known_ref, gates_ref, scale_ref, sent_ref, edge_ref):
    tail_block = got_ref[TAIL_AT : TAIL_AT + 16, :].astype(f32) * gates_ref[:1, :]
    chunks = edge_rows(tail_block, known_ref[...], table_ref)
    combine_chunk(0, own_ref, got_ref, scale_ref, sent_ref, lambda k: chunks[k])
    sent_ref[ROWS:, :] = own_ref[TAIL_AT : TAIL_AT + 16, :]
    for k in range(5):
        edge_ref[:, k * WIDE : (k + 1) * WIDE] = chunks[k]


def combine_later_kernel(own_ref, got_ref, scale_ref, edge_ref, sent_ref):
    combine_chunk(
        1, own_ref, got_ref, scale_ref, sent_ref, lambda k: edge_ref[:, k * WIDE : (k + 1) * WIDE]
    )


def diagonal_kernel(
    conv0_ref, conv1_ref, key0_ref, key1_ref, raw_queries_ref, edge_ref, decay_ref, gain_ref,
    got_ref, later_ref, table_ref, gates_ref,
    diagonal_ref, queries_ref, known_ref, scale_ref,
):
    known_ref[...] = known_part(later_ref[HEAD_AT : HEAD_AT + 16, :].astype(f32), table_ref)
    scale_ref[...] = edge_scales(got_ref[TAIL_AT : TAIL_AT + 16, :]) * gates_ref[1:2, :1]
    count = conv0_ref.shape[0]
    edge_row = iota((count, 128), 0) < EDGE
    lane_head = iota((count, 128), 1) // HEAD_DIM

    def patched(tile, j):
        rows = jnp.concatenate(
            [edge_ref[:, j * 128 : (j + 1) * 128], jnp.zeros((count - 8, 128), f32)], axis=0
        )
        return jnp.where(edge_row, rows, tile.astype(f32))

    keys = [patched(ref[...], 16 + i).astype(bf16) for i, ref in enumerate((key0_ref, key1_ref))]
    queries = [
        patched(raw_queries_ref[:, i * 128 : (i + 1) * 128], 18 + i).astype(bf16) for i in range(2)
    ]
    for i in range(2):
        queries_ref[:, i * 128 : (i + 1) * 128] = queries[i]
    for group in range(BC_GROUPS):
        part = slice((group % 2) * STATE, (group % 2 + 1) * STATE)
        scores = dot(queries[group // 2][:, part], keys[group // 2][:, part], ((1,), (1,)))
        conv_ref = (conv0_ref, conv1_ref)[group // PER_CHUNK]
        for i in range(4):
            j = group * 4 + i
            cols = slice(j * 128, (j + 1) * 128)
            at = (j * 128) % HALF
            values = patched(conv_ref[:, at : at + 128], j)
            weights, parts = [], []
            for k in range(4):
                at = 4 * j + k
                weights.append((decay_ref[at] * scores).astype(bf16))
                parts.append(jnp.where(lane_head == k, values, 0.0).astype(bf16))
            total = dot(jnp.concatenate(weights, axis=1), jnp.concatenate(parts, axis=0))
            diagonal_ref[:, cols] = total + gain_ref[:1, cols] * values


def group_out(group, total, diagonal_ref, queries_ref, entry_ref):
    cols = slice(group * WIDE, (group + 1) * WIDE)
    low = (group % 2) * STATE
    tile = queries_ref[:, (group // 2) * 128 : (group // 2 + 1) * 128]
    carried = dot(tile[:, low : low + STATE], total.astype(bf16))
    return (diagonal_ref[:, cols] + entry_ref[:, cols] * carried).astype(bf16)


def finish_first_kernel(
    first0_ref, first1_ref, second_ref, early_ref, table_ref, known_ref, gates_ref, scale_ref, diagonal_ref,
    queries_ref, entry_ref,
    out_ref, base_ref,
):
    third = gates_ref[2:3, :] > 0.5
    kept = gates_ref[:1, :]

    def second_of(at, early_at, rows):
        a = second_ref[at : at + rows, :].astype(f32)
        return jnp.where(third, early_ref[early_at : early_at + rows, :].astype(f32), a)

    chunks = edge_rows(second_of(ROWS, 2 * ROWS, 16), known_ref[...], table_ref)
    for group in range(BC_GROUPS):
        chunk, index = divmod(group, PER_CHUNK)
        at = slice(index * STATE, (index + 1) * STATE)
        scale = scale_ref[:, group * WIDE : (group + 1) * WIDE]
        first = (first0_ref, first1_ref)[chunk][at, :].astype(f32)
        total = first * kept + edge_state(chunks[group], chunks[BC_GROUPS], scale, group)
        if chunk == 0:
            total = total + scale[EDGE : EDGE + 1] * second_of(index * STATE, index * STATE, STATE)
            out_ref[:, group * WIDE : (group + 1) * WIDE] = group_out(
                group, total, diagonal_ref, queries_ref, entry_ref
            )
        else:
            base_ref[at, :] = total


def finish_later_kernel(
    second_ref, early_ref, base_ref, gates_ref, scale_ref, diagonal_ref, queries_ref, entry_ref, before_ref,
    out_hbm, out_ref, sems,
):
    third = gates_ref[2:3, :] > 0.5
    copies = [
        pltpu.make_async_copy(before_ref, out_hbm.at[0, :, pl.ds(0, HALF)], sems.at[PER_CHUNK])
    ]
    copies[0].start()
    for index in range(PER_CHUNK):
        group = PER_CHUNK + index
        at = slice(index * STATE, (index + 1) * STATE)
        early = early_ref[ROWS + index * STATE : ROWS + (index + 1) * STATE, :].astype(f32)
        second = jnp.where(third, early, second_ref[at, :].astype(f32))
        decay = scale_ref[EDGE : EDGE + 1, group * WIDE : (group + 1) * WIDE]
        total = base_ref[at, :] + decay * second
        here = pl.ds(index * WIDE, WIDE)
        out_ref[:, here] = group_out(group, total, diagonal_ref, queries_ref, entry_ref)
        copy = pltpu.make_async_copy(
            out_ref.at[:, here], out_hbm.at[0, :, pl.ds(group * WIDE, WIDE)], sems.at[index]
        )
        copy.start()
        copies.append(copy)
    for copy in copies:
        copy.wait()


def call(kernel, outs, in_specs, cost, args, out_specs=None, scratch=()):
    return pl.pallas_call(
        kernel,
        out_shape=outs,
        in_specs=in_specs,
        out_specs=out_specs or jax.tree.map(lambda _: VMEM, outs),
        scratch_shapes=scratch,
        compiler_params=pltpu.CompilerParams(vmem_limit_bytes=24 * 1024 * 1024),
        cost_estimate=pl.CostEstimate(flops=cost[0], bytes_accessed=cost[1], transcendentals=0),
    )(*args)


def permuted(array, edges):
    size, lanes = lax.axis_size("ctx"), lax.axis_size("lane")
    table = []
    for source in range(size):
        for lane in range(lanes):
            if source in edges:
                target = edges[source] * lanes + lane
            else:
                target = source * lanes + (lane + 1) % lanes
            table.append((source * lanes + lane, target))
    return lax.ppermute(array, ("ctx", "lane"), table)


def shard_near(pre_conv, step_size, lengths, conv_weight, conv_bias, decay_rate, skip_gain):
    count, channels = pre_conv.shape[1:]
    size = lax.axis_size("ctx")
    ring = [(i, (i + 1) % size) for i in range(size)]
    onward = {i: i + 2 for i in range(1, size - 2)}
    onward[size - 2] = 2
    onward[size - 1] = 1
    arguments = tuple(
        pltpu.with_memory_space_constraint(array, pltpu.HBM)
        for array in (
            lengths,
            pre_conv,
            step_size,
            conv_weight,
            conv_bias.reshape(-1, 128),
            decay_rate.reshape(1, -1),
            skip_gain.reshape(1, -1),
        )
    )
    sds = jax.ShapeDtypeStruct
    pads = pltpu.VMEM((PADS, count + 8, 128), f32)
    conv0, key0, cumulative, kept, own0, x, weight, bias, step, skip, gates = call(
        first_kernel,
        (
            sds((count, HALF), bf16),
            sds((count, 128), bf16),
            sds((HEADS, count), f32),
            sds((HEADS, count), f32),
            sds((SENT, WIDE), bf16),
            sds((count, channels), bf16),
            sds(conv_weight.shape, bf16),
            sds((channels // 128, 128), bf16),
            sds((HEADS, count), f32),
            sds((1, HEADS), f32),
            sds((8, WIDE), f32),
        ),
        [HBM] * 7,
        (40_000_000, 2_000_000),
        arguments,
        scratch=(
            pltpu.SMEM(lengths.shape, jnp.int32),
            pltpu.VMEM((1, HEADS), f32),
            pads,
            pltpu.SemaphoreType.DMA((7,)),
        ),
    )
    first0 = lax.ppermute(own0, "ctx", ring)
    conv1, key1, own1, early = call(
        later_kernel,
        (
            sds((count, HALF), bf16),
            sds((count, 128), bf16),
            sds((SENT, WIDE), bf16),
            sds((2 * ROWS + 16, WIDE), bf16),
        ),
        [VMEM] * 5,
        (40_000_000, 2_000_000),
        (x, weight, bias, kept, own0),
        scratch=(pads,),
    )
    first1 = lax.ppermute(own1, "ctx", ring)
    early = permuted(early, {0: 2, 2: 0})
    raw_queries, table, known, scale, decay, entry, gain = call(
        prepare_kernel,
        (
            sds((count, GROUPED), bf16),
            sds((7, 16, WIDE), f32),
            sds((16, WIDE), f32),
            sds((8, VALUES), f32),
            sds((HEADS, count, count), f32),
            sds((count, VALUES), f32),
            sds((8, VALUES), f32),
        ),
        [VMEM] * 9,
        (100_000_000, 1_000_000),
        (own0, own1, x, weight, bias, cumulative, step, skip, gates),
        scratch=(pads,),
    )
    sent0, edge = call(
        combine_first_kernel,
        (sds((ROWS + 16, WIDE), bf16), sds((8, channels), f32)),
        [VMEM] * 6,
        (1_000_000, 1_000_000),
        (own0, first0, table, known, gates, scale),
    )
    second0 = permuted(sent0, onward)
    sent1 = call(
        combine_later_kernel,
        sds((ROWS, WIDE), bf16),
        [VMEM] * 4,
        (1_000_000, 1_000_000),
        (own1, first1, scale, edge),
    )
    second1 = permuted(sent1, onward)
    diagonal, queries, known, scale = call(
        diagonal_kernel,
        (
            sds((count, VALUES), f32),
            sds((count, GROUPED), bf16),
            sds((16, WIDE), f32),
            sds((8, VALUES), f32),
        ),
        [VMEM] * 12,
        (400_000_000, 4_000_000),
        (conv0, conv1, key0, key1, raw_queries, edge, decay, gain, first0, first1, table, gates),
    )
    out0, base = call(
        finish_first_kernel,
        (sds((count, HALF), bf16), sds((ROWS, WIDE), f32)),
        [VMEM] * 11,
        (50_000_000, 2_000_000),
        (first0, first1, second0, early, table, known, gates, scale, diagonal, queries, entry),
    )
    return call(
        finish_later_kernel,
        sds((1, count, VALUES), bf16),
        [VMEM] * 9,
        (50_000_000, 2_000_000),
        (second1, early, base, gates, scale, diagonal, queries, entry, out0),
        out_specs=HBM,
        scratch=(pltpu.VMEM((count, HALF), bf16), pltpu.SemaphoreType.DMA((PER_CHUNK + 1,))),
    )


def shifted(value, axis, steps):
    count = lax.axis_size(axis)
    first, last = (max(0, -steps), min(count, count - steps))
    return lax.ppermute(value, axis, [(source, source + steps) for source in range(first, last)])


def carried_in(array, axis, combine, identity):
    length, index = (lax.axis_size(axis), lax.axis_index(axis))
    everything = jax.tree.map(
        lambda part, kind: lax.all_gather(part.astype(kind), axis),
        array,
        (jnp.bfloat16, jnp.bfloat16),
    )
    start = jax.tree.map(
        lambda part, zero: jnp.broadcast_to(jnp.asarray(zero, part.dtype), part.shape),
        array,
        identity,
    )

    def step(k, before):
        reached = k < index
        new = combine(
            before, jax.tree.map(lambda part, own: part[k].astype(own.dtype), everything, array)
        )
        return jax.tree.map(lambda a, b: jnp.where(reached, a, b), new, before)

    return lax.fori_loop(0, length, step, start)


def convolve(padded, conv_weight, conv_bias, count_rows):
    total = conv_bias.astype(jnp.float32)[None, :]
    for offset in range(conv_weight.shape[0]):
        total = (
            total
            + padded[offset : offset + count_rows].astype(jnp.float32)
            * conv_weight[offset].astype(jnp.float32)[None, :]
        )
    return jax.nn.silu(total).astype(jnp.bfloat16)


def group_terms(values, keys_in, queries, decay_rate, step_rows):
    heads_group = step_rows.shape[0]
    count_rows = step_rows.shape[1]
    values = values.reshape(count_rows, heads_group, -1)
    cumulative = jnp.cumsum(-step_rows * decay_rate[:, None], axis=1)
    scores = jnp.einsum("tn,sn->ts", queries, keys_in, preferred_element_type=jnp.float32)
    later = lax.broadcasted_iota(jnp.int32, (count_rows, count_rows), 0)
    earlier = lax.broadcasted_iota(jnp.int32, (count_rows, count_rows), 1)
    spread = jnp.where(
        (later >= earlier)[None], cumulative[:, :, None] - cumulative[:, None, :], -1e30
    )
    weights = (jnp.exp(spread) * scores[None]).astype(jnp.bfloat16)
    scaled = (values * step_rows.T[:, :, None]).astype(jnp.bfloat16)
    diagonal_part = jnp.einsum("hts,shp->thp", weights, scaled, preferred_element_type=jnp.float32)
    tail_weight = jnp.exp(cumulative[:, -1:] - cumulative)
    written = (values * (step_rows * tail_weight).T[:, :, None]).astype(jnp.bfloat16)
    local_state = jnp.einsum("tn,thp->hpn", keys_in, written, preferred_element_type=jnp.float32)
    return (diagonal_part, local_state, jnp.exp(cumulative[:, -1]), jnp.exp(cumulative), values)


def finish_group(diagonal_part, entry_decay, queries, incoming, values, skip_gain):
    incoming_rounded = incoming.astype(jnp.bfloat16)
    carried_part = jnp.einsum(
        "tn,hpn->thp", queries, incoming_rounded, preferred_element_type=jnp.float32
    )
    carried_part = carried_part * entry_decay.T[:, :, None]
    return diagonal_part + carried_part + skip_gain[None, :, None] * values.astype(jnp.float32)


def combine(earlier, later):
    return (earlier[0] * later[0], later[0][:, None, None] * earlier[1] + later[1])


def shard_far(pre_conv, step_size, lengths, conv_weight, conv_bias, decay_rate, skip_gain):
    count_rows = pre_conv.shape[1]
    kernel_len = conv_weight.shape[0]
    heads_group = HEADS // BC_GROUPS
    position = lax.axis_index("ctx")
    sizes_row = lengths[0]
    starts = jnp.cumsum(sizes_row) - sizes_row
    fresh = jnp.any(starts == position)
    retain = jnp.where(fresh, 0.0, 1.0).astype(jnp.float32)
    own_rows = pre_conv[0]
    previous = shifted(own_rows[count_rows - kernel_len + 1 :], "ctx", 1)
    previous = jnp.where(fresh, jnp.zeros_like(previous), previous)
    convolved = convolve(
        jnp.concatenate([previous, own_rows], axis=0), conv_weight, conv_bias, count_rows
    )
    values = convolved[:, : HEADS * HEAD_DIM]
    keys_all = convolved[:, HEADS * HEAD_DIM : HEADS * HEAD_DIM + BC_GROUPS * STATE]
    queries_all = convolved[:, HEADS * HEAD_DIM + BC_GROUPS * STATE :]
    step_rows = step_size[0]
    results = []
    pieces = []
    for bc_group in range(BC_GROUPS):
        low = bc_group * heads_group
        high = low + heads_group
        pieces.append(
            group_terms(
                values[:, low * HEAD_DIM : high * HEAD_DIM],
                keys_all[:, bc_group * STATE : (bc_group + 1) * STATE],
                queries_all[:, bc_group * STATE : (bc_group + 1) * STATE],
                decay_rate[low:high],
                step_rows[low:high],
            )
        )
    decays = jnp.concatenate([piece[2] for piece in pieces], axis=0) * retain
    states = jnp.concatenate([piece[1] for piece in pieces], axis=0)
    identity = (jnp.ones_like(decays), jnp.zeros_like(states))
    totals = carried_in((decays, states), "ctx", combine, identity)
    incoming = totals[1] * retain
    for bc_group in range(BC_GROUPS):
        low = bc_group * heads_group
        high = low + heads_group
        piece = pieces[bc_group]
        results.append(
            finish_group(
                piece[0],
                piece[3],
                queries_all[:, bc_group * STATE : (bc_group + 1) * STATE],
                incoming[low:high],
                piece[4],
                skip_gain[low:high],
            )
        )
    output = (
        jnp.concatenate(results, axis=1).reshape(count_rows, HEADS * HEAD_DIM).astype(jnp.bfloat16)
    )
    return output[None]


def solution(mesh):
    in_specs = (
        P(("groups", "lane"), "ctx", None),
        P(("groups", "lane"), None, "ctx"),
        P(("groups", "lane"), None),
        P(),
        P(),
        P(),
        P(),
    )
    out_specs = P(("groups", "lane"), "ctx", None)
    shards = shard_near if mesh.shape["ctx"] <= 8 else shard_far
    return jax.shard_map(shards, mesh=mesh, in_specs=in_specs, out_specs=out_specs, check_vma=False)
```

```python
import jax
import jax.numpy as jnp
from jax import lax
from jax.experimental import pallas as pl
from jax.experimental.pallas import tpu as pltpu
from jax.sharding import PartitionSpec as P

HEADS = 64
HEAD_DIM = 32
EDGE = 3
STATE = 64
BC_GROUPS = 4
HEADS_GROUP = HEADS // BC_GROUPS
VALUES = HEADS * HEAD_DIM
WIDE = HEADS_GROUP * HEAD_DIM
GROUPED = BC_GROUPS * STATE
CHUNKS = 2
PADS = 4
ORDER = (0, 1, 2, 5, 3, 4, 6)
PER_CHUNK = BC_GROUPS // CHUNKS
HALF = PER_CHUNK * WIDE
ROWS = PER_CHUNK * STATE
TAIL_AT = ROWS
HEAD_AT = ROWS
SENT = ROWS + 16
LOG2E = 1.4426950408889634
VMEM = pl.BlockSpec(memory_space=pltpu.VMEM)
HBM = pl.BlockSpec(memory_space=pltpu.HBM)
f32 = jnp.float32
bf16 = jnp.bfloat16


def iota(shape, dim):
    return lax.broadcasted_iota(jnp.int32, shape, dim)


def dot(a, b, contract=((1,), (0,))):
    return lax.dot_general(a, b, (contract, ((), ())), preferred_element_type=f32)


def is_fresh(lengths_ref, position):
    found = jnp.int32(0)
    start = jnp.int32(0)
    for k in range(lengths_ref.shape[1]):
        found = jnp.where(start == position, jnp.int32(1), found)
        start = start + lengths_ref[0, k]
    return found


def halves(value):
    high = value.astype(bf16)
    return high, (value - high.astype(f32)).astype(bf16)


def cumulative_of(step, rate_row):
    eye = iota((HEADS, HEADS), 0) == iota((HEADS, HEADS), 1)
    rate = jnp.sum(jnp.where(eye, rate_row, 0.0), axis=1, keepdims=True)
    tokens = step.shape[1]
    upto = iota((tokens, tokens), 0) <= iota((tokens, tokens), 1)
    upto = upto.astype(bf16)
    rest = -step * rate
    total = jnp.zeros_like(rest)
    for _ in range(3):
        part = rest.astype(bf16)
        rest = rest - part.astype(f32)
        total = total + dot(part, upto)
    return total


def spread_matrix():
    rows, lanes = 2 * HEADS_GROUP, WIDE
    return (iota((rows, lanes), 0) % HEADS_GROUP == iota((rows, lanes), 1) // HEAD_DIM).astype(bf16)


def spread(per_head, group, matrix):
    part = per_head[group * HEADS_GROUP : (group + 1) * HEADS_GROUP]
    return dot(jnp.concatenate(halves(part), axis=0), matrix, ((0,), (0,)))


def half_silu(half):
    return half + half * jnp.tanh(half)


def to_rows(strip, first):
    rows = iota((8, WIDE), 0)
    top = jnp.zeros((8, WIDE), f32)
    low = jnp.zeros((8, WIDE), f32)
    for k in range(strip.shape[1] // WIDE):
        moved = pltpu.roll(strip[:, k * WIDE : (k + 1) * WIDE], (3 * k - first) % 8, 0)
        if 3 * k < 8:
            top = jnp.where((rows >= 3 * k) & (rows < 3 * k + 3), moved, top)
        if 3 * k + 2 >= 8:
            low = jnp.where((rows >= 3 * k - 8) & (rows < 3 * k - 5), moved, low)
    return jnp.concatenate([top, low], axis=0)


def conv_rows(x, weight, bias, pad_ref):
    count = x.shape[0]
    pad_ref[8 : 8 + count, :] = x
    total = bias + x * weight[3:4]
    for back in range(1, 4):
        total = total + pad_ref[8 - back : 8 - back + count, :] * weight[3 - back : 4 - back]
    return half_silu(total)


def clear(pads_ref):
    for slot in range(PADS):
        pads_ref[slot, :8, :] = jnp.zeros((8, 128), f32)


def half_taps(weight_ref, bias_ref):
    return weight_ref[...].astype(f32) * 0.5, bias_ref[...].astype(f32) * 0.5


def chunk_states(chunk, x_ref, weight, bias, kept, conv_ref, key_ref, sent_ref, pads_ref):
    matrix = spread_matrix()
    clear(pads_ref)

    def conv_tile(j):
        cols = slice(j * 128, (j + 1) * 128)
        return conv_rows(x_ref[:, cols].astype(f32), weight[:, cols], bias[j : j + 1], pads_ref.at[j % PADS])

    key = conv_tile(VALUES // 128 + chunk).astype(bf16)
    key_ref[...] = key
    for index in range(PER_CHUNK):
        group = chunk * PER_CHUNK + index
        scale = spread(kept, group, matrix)
        parts = []
        for i in range(WIDE // 128):
            local = index * WIDE + i * 128
            tile = conv_tile((chunk * HALF + local) // 128)
            conv_ref[:, local : local + 128] = tile.astype(bf16)
            parts.append((tile * scale[:, i * 128 : (i + 1) * 128]).astype(bf16))
        state = dot(
            key[:, index * STATE : (index + 1) * STATE], jnp.concatenate(parts, axis=1), ((0,), (0,))
        )
        sent_ref[index * STATE : (index + 1) * STATE, :] = state.astype(bf16)


def kept_weights(step, cumulative, goes_on):
    count = step.shape[1]
    last = cumulative[:, count - 1 :]
    tail = step * jnp.exp(last - cumulative)
    lanes = iota((HEADS, count), 1)
    kept = jnp.where((lanes >= EDGE) | (goes_on < 0.5), tail, 0.0)
    return kept, jnp.where(lanes == EDGE, jnp.exp(last), tail)


def first_kernel(
    lengths_hbm, x_hbm, step_hbm, weight_hbm, bias_hbm, rate_hbm, skip_hbm,
    conv_ref, key_ref, cumulative_ref, sent_ref, x_ref, weight_ref, bias_ref, step_ref, skip_ref, gates_ref,
    lengths_ref, rate_ref, pads_ref, sems,
):
    count = x_ref.shape[0]
    pairs = [
        (step_hbm.at[0], step_ref),
        (rate_hbm, rate_ref),
        (lengths_hbm, lengths_ref),
        (weight_hbm, weight_ref),
        (bias_hbm, bias_ref),
        (x_hbm.at[0], x_ref),
        (skip_hbm, skip_ref),
    ]
    copies = [pltpu.make_async_copy(a, b, sems.at[i]) for i, (a, b) in enumerate(pairs)]
    for i in ORDER:
        copies[i].start()
    for copy in copies[:3]:
        copy.wait()
    position = lax.axis_index("ctx")
    fresh = is_fresh(lengths_ref, position)
    goes_on = (1 - fresh).astype(f32)
    both = goes_on * (1 - is_fresh(lengths_ref, position - 1)).astype(f32)
    third = jnp.where(position == 2, 1.0, 0.0).astype(f32)
    rows = iota((8, WIDE), 0)
    gates_ref[...] = jnp.where(rows == 0, goes_on, jnp.where(rows == 1, both, third))
    step = step_ref[...]
    cumulative = cumulative_of(step, rate_ref[...])
    cumulative_ref[...] = cumulative
    kept = kept_weights(step, cumulative, goes_on)[0]
    for copy in copies[3:6]:
        copy.wait()
    weight, bias = half_taps(weight_ref, bias_ref)
    chunk_states(
        0,
        x_ref, weight, bias, kept, conv_ref, key_ref, sent_ref, pads_ref,
    )
    tail_rows = to_rows(x_ref[count - 16 :, :].astype(f32)[8:], 5)
    sent_ref[TAIL_AT : TAIL_AT + 16, :] = tail_rows.astype(bf16)
    copies[6].wait()


def later_kernel(
    x_ref, weight_ref, bias_ref, step_ref, cumulative_ref, gates_ref, before_ref,
    conv_ref, key_ref, sent_ref, early_ref, pads_ref,
):
    weight, bias = half_taps(weight_ref, bias_ref)
    kept, scales = kept_weights(step_ref[...], cumulative_ref[...], gates_ref[:1, :1])
    chunk_states(1, x_ref, weight, bias, kept, conv_ref, key_ref, sent_ref, pads_ref)
    high, low = halves(scales)
    place = iota((HEADS, 128), 1) - iota((HEADS, 128), 0)
    picked = dot(high, (place == 0).astype(bf16), ((0,), (0,)))
    picked = picked + dot(low, (place == HEADS).astype(bf16), ((0,), (0,)))
    line = jnp.concatenate([picked[k : k + 1] for k in range(4)], axis=1)
    head_rows = to_rows(x_ref[:16, :].astype(f32)[:8], 0)
    head_rows = jnp.where(iota((16, WIDE), 0) == 15, line, head_rows)
    sent_ref[HEAD_AT : HEAD_AT + 16, :] = head_rows.astype(bf16)
    early_ref[:ROWS, :] = before_ref[:ROWS, :]
    early_ref[ROWS : 2 * ROWS, :] = sent_ref[:ROWS, :]
    early_ref[2 * ROWS :, :] = before_ref[TAIL_AT : TAIL_AT + 16, :]


def known_part(head_block, table_ref):
    return (
        table_ref[0]
        + head_block * table_ref[1]
        + pltpu.roll(head_block, 1, 0) * table_ref[2]
        + pltpu.roll(head_block, 2, 0) * table_ref[3]
    )


def edge_rows(tail_block, known, table_ref):
    block = half_silu(
        known
        + tail_block * table_ref[4]
        + pltpu.roll(tail_block, 15, 0) * table_ref[5]
        + pltpu.roll(tail_block, 14, 0) * table_ref[6]
    )
    return [pltpu.roll(block, (16 - 3 * k) % 16, 0)[:8] for k in range(5)]


def head_lanes(rows):
    lanes = iota((128, VALUES), 1) // HEAD_DIM
    matrix = (iota((128, VALUES), 0) % HEADS == lanes).astype(bf16)
    return dot(rows, matrix)[:8]


def edge_scales(head_rows):
    line = head_rows[15:16].astype(f32)
    rows = [line[:, k * 128 : (k + 1) * 128] for k in range(4)]
    return head_lanes(jnp.concatenate(rows + [jnp.zeros((12, 128), f32)], axis=0).astype(bf16))


def prepare_kernel(
    later_ref, x_ref, weight_ref, bias_ref, cumulative_ref, step_ref, skip_ref, gates_ref,
    queries_ref, table_ref, known_ref, scale_ref, decay_ref, entry_ref, gain_ref, pads_ref,
):
    clear(pads_ref)
    weight, bias = half_taps(weight_ref, bias_ref)
    rows = iota((16, WIDE), 0)
    third = rows % 3
    chunk = rows // 3

    def blocked(lines):
        out = jnp.zeros((16, WIDE), f32)
        for k in range(5):
            out = jnp.where(chunk == k, lines[k], out)
        return out

    taps = [
        blocked([weight[tap : tap + 1, k * WIDE : (k + 1) * WIDE] for k in range(5)])
        for tap in range(4)
    ]
    table_ref[0] = blocked(
        [
            jnp.concatenate([bias[4 * k + i : 4 * k + i + 1, :] for i in range(4)], axis=1)
            for k in range(5)
        ]
    )
    table_ref[1] = taps[3]
    table_ref[2] = jnp.where(third == 0, 0.0, taps[2])
    table_ref[3] = jnp.where(third == 2, taps[1], 0.0)
    table_ref[4] = taps[0]
    table_ref[5] = jnp.where(third == 2, 0.0, taps[1])
    table_ref[6] = jnp.where(third == 0, taps[2], 0.0)
    known_ref[...] = known_part(later_ref[HEAD_AT : HEAD_AT + 16, :].astype(f32), table_ref)
    scale_ref[...] = edge_scales(later_ref[HEAD_AT : HEAD_AT + 16, :]) * gates_ref[:1, :1]
    cumulative = cumulative_ref[...] * LOG2E
    across = cumulative - jnp.log2(step_ref[...])
    down = cumulative.T
    count = down.shape[0]
    causal = iota((count, count), 0) >= iota((count, count), 1)
    for at in range(HEADS):
        gap = down[:, at : at + 1] - across[at : at + 1, :]
        decay_ref[at] = jnp.exp2(jnp.where(causal, gap, -1e30))
    matrix = spread_matrix()
    entry = jnp.exp2(cumulative)
    for group in range(BC_GROUPS):
        entry_ref[:, group * WIDE : (group + 1) * WIDE] = spread(entry, group, matrix)
    gain_ref[...] = head_lanes(
        jnp.concatenate(halves(skip_ref[...] + jnp.zeros((16, HEADS), f32)), axis=1)
    )
    first = VALUES + GROUPED
    for i in range(2):
        cols = slice(first + i * 128, first + (i + 1) * 128)
        j = first // 128 + i
        tile = conv_rows(
            x_ref[:, cols].astype(f32), weight[:, cols], bias[j : j + 1, :], pads_ref.at[i]
        )
        queries_ref[:, i * 128 : (i + 1) * 128] = tile.astype(bf16)


def edge_state(values_rows, keys_rows, scale, group):
    rows = iota((8, WIDE), 0)
    written = jnp.where(rows < EDGE, values_rows * scale, 0.0)
    tile = keys_rows[:, (group // 2) * 128 : (group // 2 + 1) * 128].astype(bf16)
    return dot(tile[:, (group % 2) * STATE : (group % 2 + 1) * STATE], written.astype(bf16), ((0,), (0,)))


def combine_chunk(own_ref, got_ref, decays, extras, sent_ref):
    for index in range(PER_CHUNK):
        at = slice(index * STATE, (index + 1) * STATE)
        total = own_ref[at, :].astype(f32) + extras[index] + decays[index] * got_ref[at, :].astype(f32)
        sent_ref[at, :] = total.astype(bf16)


def group_cols(group):
    return slice(group * WIDE, (group + 1) * WIDE)


def combine_first_kernel(own_ref, got_ref, table_ref, known_ref, gates_ref, scale_ref, sent_ref, edge_ref):
    tail_block = got_ref[TAIL_AT : TAIL_AT + 16, :].astype(f32) * gates_ref[:1, :]
    chunks = edge_rows(tail_block, known_ref[...], table_ref)
    scales = [scale_ref[:, group_cols(group)] for group in range(PER_CHUNK)]
    extras = [edge_state(chunks[g], chunks[BC_GROUPS], scales[g], g) for g in range(PER_CHUNK)]
    decays = [scale[EDGE : EDGE + 1] for scale in scales]
    combine_chunk(own_ref, got_ref, decays, extras, sent_ref)
    sent_ref[ROWS:, :] = own_ref[TAIL_AT : TAIL_AT + 16, :]
    for k in range(5):
        edge_ref[:, k * WIDE : (k + 1) * WIDE] = chunks[k]


def combine_later_kernel(own_ref, got_ref, scale_ref, extra_ref, sent_ref):
    groups = range(PER_CHUNK, BC_GROUPS)
    decays = [scale_ref[EDGE : EDGE + 1, group_cols(group)] for group in groups]
    extras = [extra_ref[index * STATE : (index + 1) * STATE, :] for index in range(PER_CHUNK)]
    combine_chunk(own_ref, got_ref, decays, extras, sent_ref)


def diagonal_chunk(chunk, conv_ref, key_ref, raw_queries_ref, edge_ref, decay_ref, gain_ref, diagonal_ref, queries_ref):
    count = conv_ref.shape[0]
    edge_row = iota((count, 128), 0) < EDGE
    lane_head = iota((count, 128), 1) // HEAD_DIM

    def patched(tile, j):
        rows = jnp.concatenate(
            [edge_ref[:, j * 128 : (j + 1) * 128], jnp.zeros((count - 8, 128), f32)], axis=0
        )
        return jnp.where(edge_row, rows, tile.astype(f32))

    keys = patched(key_ref[...], VALUES // 128 + chunk).astype(bf16)
    j = (VALUES + GROUPED) // 128 + chunk
    queries = patched(raw_queries_ref[:, chunk * 128 : (chunk + 1) * 128], j).astype(bf16)
    queries_ref[...] = queries
    for index in range(PER_CHUNK):
        part = slice(index * STATE, (index + 1) * STATE)
        scores = dot(queries[:, part], keys[:, part], ((1,), (1,)))
        for i in range(WIDE // 128):
            at = index * WIDE + i * 128
            j = (chunk * HALF + at) // 128
            values = patched(conv_ref[:, at : at + 128], j)
            weights, parts = [], []
            for k in range(4):
                weights.append((decay_ref[4 * j + k] * scores).astype(bf16))
                parts.append(jnp.where(lane_head == k, values, 0.0).astype(bf16))
            total = dot(jnp.concatenate(weights, axis=1), jnp.concatenate(parts, axis=0))
            diagonal_ref[:, at : at + 128] = total + gain_ref[:1, j * 128 : (j + 1) * 128] * values


def diagonal_first_kernel(
    conv_ref, key_ref, raw_queries_ref, edge_ref, decay_ref, gain_ref, own_scale_ref,
    diagonal_ref, queries_ref, extra_ref,
):
    keys = edge_ref[:, BC_GROUPS * WIDE :]
    for index in range(PER_CHUNK):
        group = PER_CHUNK + index
        cols = group_cols(group)
        extra_ref[index * STATE : (index + 1) * STATE, :] = edge_state(
            edge_ref[:, cols], keys, own_scale_ref[:, cols], group
        )
    diagonal_chunk(0, conv_ref, key_ref, raw_queries_ref, edge_ref, decay_ref, gain_ref, diagonal_ref, queries_ref)


def diagonal_later_kernel(
    conv_ref, key_ref, raw_queries_ref, edge_ref, decay_ref, gain_ref, later_ref, table_ref, gates_ref,
    diagonal_ref, queries_ref, known_ref, scale_ref,
):
    head_rows = later_ref[HEAD_AT : HEAD_AT + 16, :]
    known_ref[...] = known_part(head_rows.astype(f32), table_ref)
    scale_ref[...] = edge_scales(head_rows) * gates_ref[1:2, :1]
    diagonal_chunk(1, conv_ref, key_ref, raw_queries_ref, edge_ref, decay_ref, gain_ref, diagonal_ref, queries_ref)


def group_out(group, total, diagonal_ref, queries_ref, entry_ref):
    index = group % PER_CHUNK
    here = slice(index * WIDE, (index + 1) * WIDE)
    carried = dot(queries_ref[:, index * STATE : (index + 1) * STATE], total.astype(bf16))
    return (diagonal_ref[:, here] + entry_ref[:, group_cols(group)] * carried).astype(bf16)


def finish_first_kernel(
    first0_ref, first1_ref, second_ref, early_ref, table_ref, known_ref, gates_ref, scale_ref, diagonal_ref,
    queries_ref, entry_ref,
    out_ref, base_ref, decay_ref,
):
    third = gates_ref[2:3, :] > 0.5
    kept = gates_ref[:1, :]

    def second_of(at, early_at, rows):
        a = second_ref[at : at + rows, :].astype(f32)
        return jnp.where(third, early_ref[early_at : early_at + rows, :].astype(f32), a)

    chunks = edge_rows(second_of(ROWS, 2 * ROWS, 16), known_ref[...], table_ref)
    for group in range(BC_GROUPS):
        chunk, index = divmod(group, PER_CHUNK)
        at = slice(index * STATE, (index + 1) * STATE)
        scale = scale_ref[:, group_cols(group)]
        decay = scale[EDGE : EDGE + 1]
        first = (first0_ref, first1_ref)[chunk][at, :].astype(f32)
        total = first * kept + edge_state(chunks[group], chunks[BC_GROUPS], scale, group)
        if chunk == 0:
            total = total + decay * second_of(index * STATE, index * STATE, STATE)
            out_ref[:, group_cols(group)] = group_out(group, total, diagonal_ref, queries_ref, entry_ref)
        else:
            early = early_ref[ROWS + index * STATE : ROWS + (index + 1) * STATE, :].astype(f32)
            base_ref[at, :] = jnp.where(third, total + decay * early, total)
            decay_ref[index * 8 : (index + 1) * 8, :] = jnp.where(third, 0.0, decay) + jnp.zeros((8, WIDE), f32)


def finish_later_kernel(
    second_ref, base_ref, decay_ref, diagonal_ref, queries_ref, entry_ref, before_ref, out_hbm, out_ref, sems
):
    copies = [
        pltpu.make_async_copy(before_ref, out_hbm.at[0, :, pl.ds(0, HALF)], sems.at[PER_CHUNK])
    ]
    copies[0].start()
    for index in range(PER_CHUNK):
        group = PER_CHUNK + index
        at = slice(index * STATE, (index + 1) * STATE)
        decay = decay_ref[index * 8 : index * 8 + 1, :]
        total = base_ref[at, :] + decay * second_ref[at, :].astype(f32)
        here = pl.ds(index * WIDE, WIDE)
        out_ref[:, here] = group_out(group, total, diagonal_ref, queries_ref, entry_ref)
        copy = pltpu.make_async_copy(
            out_ref.at[:, here], out_hbm.at[0, :, pl.ds(group * WIDE, WIDE)], sems.at[index]
        )
        copy.start()
        copies.append(copy)
    for copy in copies:
        copy.wait()


def call(kernel, outs, in_specs, cost, args, out_specs=None, scratch=()):
    return pl.pallas_call(
        kernel,
        out_shape=outs,
        in_specs=in_specs,
        out_specs=out_specs or jax.tree.map(lambda _: VMEM, outs),
        scratch_shapes=scratch,
        compiler_params=pltpu.CompilerParams(vmem_limit_bytes=24 * 1024 * 1024),
        cost_estimate=pl.CostEstimate(flops=cost[0], bytes_accessed=cost[1], transcendentals=0),
    )(*args)


def permuted(array, edges):
    size, lanes = lax.axis_size("ctx"), lax.axis_size("lane")
    table = []
    for source in range(size):
        for lane in range(lanes):
            if source in edges:
                target = edges[source] * lanes + lane
            else:
                target = source * lanes + (lane + 1) % lanes
            table.append((source * lanes + lane, target))
    return lax.ppermute(array, ("ctx", "lane"), table)


def shard_near(pre_conv, step_size, lengths, conv_weight, conv_bias, decay_rate, skip_gain):
    count, channels = pre_conv.shape[1:]
    size = lax.axis_size("ctx")
    ring = [(i, (i + 1) % size) for i in range(size)]
    onward = {i: i + 2 for i in range(1, size - 2)}
    onward[size - 2] = 2
    onward[size - 1] = 1
    arguments = tuple(
        pltpu.with_memory_space_constraint(array, pltpu.HBM)
        for array in (
            lengths,
            pre_conv,
            step_size,
            conv_weight,
            conv_bias.reshape(-1, 128),
            decay_rate.reshape(1, -1),
            skip_gain.reshape(1, -1),
        )
    )
    sds = jax.ShapeDtypeStruct
    pads = pltpu.VMEM((PADS, count + 8, 128), f32)
    conv0, key0, cumulative, own0, x, weight, bias, step, skip, gates = call(
        first_kernel,
        (
            sds((count, HALF), bf16),
            sds((count, 128), bf16),
            sds((HEADS, count), f32),
            sds((SENT, WIDE), bf16),
            sds((count, channels), bf16),
            sds(conv_weight.shape, bf16),
            sds((channels // 128, 128), bf16),
            sds((HEADS, count), f32),
            sds((1, HEADS), f32),
            sds((8, WIDE), f32),
        ),
        [HBM] * 7,
        (40_000_000, 2_000_000),
        arguments,
        scratch=(
            pltpu.SMEM(lengths.shape, jnp.int32),
            pltpu.VMEM((1, HEADS), f32),
            pads,
            pltpu.SemaphoreType.DMA((7,)),
        ),
    )
    first0 = lax.ppermute(own0, "ctx", ring)
    conv1, key1, own1, early = call(
        later_kernel,
        (
            sds((count, HALF), bf16),
            sds((count, 128), bf16),
            sds((SENT, WIDE), bf16),
            sds((2 * ROWS + 16, WIDE), bf16),
        ),
        [VMEM] * 7,
        (40_000_000, 2_000_000),
        (x, weight, bias, step, cumulative, gates, own0),
        scratch=(pads,),
    )
    first1 = lax.ppermute(own1, "ctx", ring)
    early = permuted(early, {0: 2, 2: 0})
    raw_queries, table, known, scale, decay, entry, gain = call(
        prepare_kernel,
        (
            sds((count, GROUPED), bf16),
            sds((7, 16, WIDE), f32),
            sds((16, WIDE), f32),
            sds((8, VALUES), f32),
            sds((HEADS, count, count), f32),
            sds((count, VALUES), f32),
            sds((8, VALUES), f32),
        ),
        [VMEM] * 8,
        (100_000_000, 1_000_000),
        (own1, x, weight, bias, cumulative, step, skip, gates),
        scratch=(pads,),
    )
    sent0, edge = call(
        combine_first_kernel,
        (sds((ROWS + 16, WIDE), bf16), sds((8, channels), f32)),
        [VMEM] * 6,
        (1_000_000, 1_000_000),
        (own0, first0, table, known, gates, scale),
    )
    second0 = permuted(sent0, onward)
    diagonal_outs = (sds((count, HALF), f32), sds((count, 128), bf16))
    diagonal0, queries0, extra = call(
        diagonal_first_kernel,
        diagonal_outs + (sds((ROWS, WIDE), f32),),
        [VMEM] * 7,
        (200_000_000, 2_000_000),
        (conv0, key0, raw_queries, edge, decay, gain, scale),
    )
    sent1 = call(
        combine_later_kernel,
        sds((ROWS, WIDE), bf16),
        [VMEM] * 4,
        (1_000_000, 1_000_000),
        (own1, first1, scale, extra),
    )
    second1 = permuted(sent1, onward)
    diagonal1, queries1, known, scale = call(
        diagonal_later_kernel,
        diagonal_outs + (sds((16, WIDE), f32), sds((8, VALUES), f32)),
        [VMEM] * 9,
        (200_000_000, 2_000_000),
        (conv1, key1, raw_queries, edge, decay, gain, first1, table, gates),
    )
    out0, base, decay = call(
        finish_first_kernel,
        (sds((count, HALF), bf16), sds((ROWS, WIDE), f32), sds((8 * PER_CHUNK, WIDE), f32)),
        [VMEM] * 11,
        (50_000_000, 2_000_000),
        (first0, first1, second0, early, table, known, gates, scale, diagonal0, queries0, entry),
    )
    return call(
        finish_later_kernel,
        sds((1, count, VALUES), bf16),
        [VMEM] * 7,
        (50_000_000, 2_000_000),
        (second1, base, decay, diagonal1, queries1, entry, out0),
        out_specs=HBM,
        scratch=(pltpu.VMEM((count, HALF), bf16), pltpu.SemaphoreType.DMA((PER_CHUNK + 1,))),
    )


def shifted(value, axis, steps):
    count = lax.axis_size(axis)
    first, last = (max(0, -steps), min(count, count - steps))
    return lax.ppermute(value, axis, [(source, source + steps) for source in range(first, last)])


def carried_in(array, axis, combine, identity):
    length, index = (lax.axis_size(axis), lax.axis_index(axis))
    everything = jax.tree.map(
        lambda part, kind: lax.all_gather(part.astype(kind), axis),
        array,
        (jnp.bfloat16, jnp.bfloat16),
    )
    start = jax.tree.map(
        lambda part, zero: jnp.broadcast_to(jnp.asarray(zero, part.dtype), part.shape),
        array,
        identity,
    )

    def step(k, before):
        reached = k < index
        new = combine(
            before, jax.tree.map(lambda part, own: part[k].astype(own.dtype), everything, array)
        )
        return jax.tree.map(lambda a, b: jnp.where(reached, a, b), new, before)

    return lax.fori_loop(0, length, step, start)


def convolve(padded, conv_weight, conv_bias, count_rows):
    total = conv_bias.astype(jnp.float32)[None, :]
    for offset in range(conv_weight.shape[0]):
        total = (
            total
            + padded[offset : offset + count_rows].astype(jnp.float32)
            * conv_weight[offset].astype(jnp.float32)[None, :]
        )
    return jax.nn.silu(total).astype(jnp.bfloat16)


def group_terms(values, keys_in, queries, decay_rate, step_rows):
    heads_group = step_rows.shape[0]
    count_rows = step_rows.shape[1]
    values = values.reshape(count_rows, heads_group, -1)
    cumulative = jnp.cumsum(-step_rows * decay_rate[:, None], axis=1)
    scores = jnp.einsum("tn,sn->ts", queries, keys_in, preferred_element_type=jnp.float32)
    later = lax.broadcasted_iota(jnp.int32, (count_rows, count_rows), 0)
    earlier = lax.broadcasted_iota(jnp.int32, (count_rows, count_rows), 1)
    spread = jnp.where(
        (later >= earlier)[None], cumulative[:, :, None] - cumulative[:, None, :], -1e30
    )
    weights = (jnp.exp(spread) * scores[None]).astype(jnp.bfloat16)
    scaled = (values * step_rows.T[:, :, None]).astype(jnp.bfloat16)
    diagonal_part = jnp.einsum("hts,shp->thp", weights, scaled, preferred_element_type=jnp.float32)
    tail_weight = jnp.exp(cumulative[:, -1:] - cumulative)
    written = (values * (step_rows * tail_weight).T[:, :, None]).astype(jnp.bfloat16)
    local_state = jnp.einsum("tn,thp->hpn", keys_in, written, preferred_element_type=jnp.float32)
    return (diagonal_part, local_state, jnp.exp(cumulative[:, -1]), jnp.exp(cumulative), values)


def finish_group(diagonal_part, entry_decay, queries, incoming, values, skip_gain):
    incoming_rounded = incoming.astype(jnp.bfloat16)
    carried_part = jnp.einsum(
        "tn,hpn->thp", queries, incoming_rounded, preferred_element_type=jnp.float32
    )
    carried_part = carried_part * entry_decay.T[:, :, None]
    return diagonal_part + carried_part + skip_gain[None, :, None] * values.astype(jnp.float32)


def combine(earlier, later):
    return (earlier[0] * later[0], later[0][:, None, None] * earlier[1] + later[1])


def shard_far(pre_conv, step_size, lengths, conv_weight, conv_bias, decay_rate, skip_gain):
    count_rows = pre_conv.shape[1]
    kernel_len = conv_weight.shape[0]
    heads_group = HEADS // BC_GROUPS
    position = lax.axis_index("ctx")
    sizes_row = lengths[0]
    starts = jnp.cumsum(sizes_row) - sizes_row
    fresh = jnp.any(starts == position)
    retain = jnp.where(fresh, 0.0, 1.0).astype(jnp.float32)
    own_rows = pre_conv[0]
    previous = shifted(own_rows[count_rows - kernel_len + 1 :], "ctx", 1)
    previous = jnp.where(fresh, jnp.zeros_like(previous), previous)
    convolved = convolve(
        jnp.concatenate([previous, own_rows], axis=0), conv_weight, conv_bias, count_rows
    )
    values = convolved[:, : HEADS * HEAD_DIM]
    keys_all = convolved[:, HEADS * HEAD_DIM : HEADS * HEAD_DIM + BC_GROUPS * STATE]
    queries_all = convolved[:, HEADS * HEAD_DIM + BC_GROUPS * STATE :]
    step_rows = step_size[0]
    results = []
    pieces = []
    for bc_group in range(BC_GROUPS):
        low = bc_group * heads_group
        high = low + heads_group
        pieces.append(
            group_terms(
                values[:, low * HEAD_DIM : high * HEAD_DIM],
                keys_all[:, bc_group * STATE : (bc_group + 1) * STATE],
                queries_all[:, bc_group * STATE : (bc_group + 1) * STATE],
                decay_rate[low:high],
                step_rows[low:high],
            )
        )
    decays = jnp.concatenate([piece[2] for piece in pieces], axis=0) * retain
    states = jnp.concatenate([piece[1] for piece in pieces], axis=0)
    identity = (jnp.ones_like(decays), jnp.zeros_like(states))
    totals = carried_in((decays, states), "ctx", combine, identity)
    incoming = totals[1] * retain
    for bc_group in range(BC_GROUPS):
        low = bc_group * heads_group
        high = low + heads_group
        piece = pieces[bc_group]
        results.append(
            finish_group(
                piece[0],
                piece[3],
                queries_all[:, bc_group * STATE : (bc_group + 1) * STATE],
                incoming[low:high],
                piece[4],
                skip_gain[low:high],
            )
        )
    output = (
        jnp.concatenate(results, axis=1).reshape(count_rows, HEADS * HEAD_DIM).astype(jnp.bfloat16)
    )
    return output[None]


def solution(mesh):
    in_specs = (
        P(("groups", "lane"), "ctx", None),
        P(("groups", "lane"), None, "ctx"),
        P(("groups", "lane"), None),
        P(),
        P(),
        P(),
        P(),
    )
    out_specs = P(("groups", "lane"), "ctx", None)
    shards = shard_near if mesh.shape["ctx"] <= 8 else shard_far
    return jax.shard_map(shards, mesh=mesh, in_specs=in_specs, out_specs=out_specs, check_vma=False)
```

```python
import jax
import jax.numpy as jnp
from jax import lax
from jax.experimental import pallas as pl
from jax.experimental.pallas import tpu as pltpu
from jax.sharding import PartitionSpec as P

HEADS = 64
HEAD_DIM = 32
EDGE = 3
STATE = 64
BC_GROUPS = 4
HEADS_GROUP = HEADS // BC_GROUPS
VALUES = HEADS * HEAD_DIM
WIDE = HEADS_GROUP * HEAD_DIM
GROUPED = BC_GROUPS * STATE
CHUNKS = 2
PADS = 4
ORDER = (0, 1, 2, 5, 3, 4, 6)
PER_CHUNK = BC_GROUPS // CHUNKS
HALF = PER_CHUNK * WIDE
ROWS = PER_CHUNK * STATE
TAIL_AT = ROWS
HEAD_AT = ROWS
SENT = ROWS + 16
LAST_LOW = 2
LOG2E = 1.4426950408889634
VMEM = pl.BlockSpec(memory_space=pltpu.VMEM)
HBM = pl.BlockSpec(memory_space=pltpu.HBM)
f32 = jnp.float32
bf16 = jnp.bfloat16


def iota(shape, dim):
    return lax.broadcasted_iota(jnp.int32, shape, dim)


def dot(a, b, contract=((1,), (0,))):
    return lax.dot_general(a, b, (contract, ((), ())), preferred_element_type=f32)


def is_fresh(lengths_ref, position):
    found = jnp.int32(0)
    start = jnp.int32(0)
    for k in range(lengths_ref.shape[1]):
        found = jnp.where(start == position, jnp.int32(1), found)
        start = start + lengths_ref[0, k]
    return found


def halves(value):
    high = value.astype(bf16)
    return high, (value - high.astype(f32)).astype(bf16)


def cumulative_of(step, rate_row):
    eye = iota((HEADS, HEADS), 0) == iota((HEADS, HEADS), 1)
    rate = jnp.sum(jnp.where(eye, rate_row, 0.0), axis=1, keepdims=True)
    tokens = step.shape[1]
    upto = iota((tokens, tokens), 0) <= iota((tokens, tokens), 1)
    upto = upto.astype(bf16)
    rest = -step * rate
    total = jnp.zeros_like(rest)
    for _ in range(3):
        part = rest.astype(bf16)
        rest = rest - part.astype(f32)
        total = total + dot(part, upto)
    return total


def spread_matrix():
    rows, lanes = 2 * HEADS_GROUP, WIDE
    return (iota((rows, lanes), 0) % HEADS_GROUP == iota((rows, lanes), 1) // HEAD_DIM).astype(bf16)


def spread(per_head, group, matrix):
    part = per_head[group * HEADS_GROUP : (group + 1) * HEADS_GROUP]
    return dot(jnp.concatenate(halves(part), axis=0), matrix, ((0,), (0,)))


def half_silu(half):
    return half + half * jnp.tanh(half)


def to_rows(strip, first):
    rows = iota((8, WIDE), 0)
    top = jnp.zeros((8, WIDE), f32)
    low = jnp.zeros((8, WIDE), f32)
    for k in range(strip.shape[1] // WIDE):
        moved = pltpu.roll(strip[:, k * WIDE : (k + 1) * WIDE], (3 * k - first) % 8, 0)
        if 3 * k < 8:
            top = jnp.where((rows >= 3 * k) & (rows < 3 * k + 3), moved, top)
        if 3 * k + 2 >= 8:
            low = jnp.where((rows >= 3 * k - 8) & (rows < 3 * k - 5), moved, low)
    return jnp.concatenate([top, low], axis=0)


def conv_rows(x, weight, bias, pad_ref):
    count = x.shape[0]
    pad_ref[8 : 8 + count, :] = x
    total = bias + x * weight[3:4]
    for back in range(1, 4):
        total = total + pad_ref[8 - back : 8 - back + count, :] * weight[3 - back : 4 - back]
    return half_silu(total)


def clear(pads_ref):
    for slot in range(PADS):
        pads_ref[slot, :8, :] = jnp.zeros((8, 128), f32)


def half_taps(weight_ref, bias_ref):
    return weight_ref[...].astype(f32) * 0.5, bias_ref[...].astype(f32) * 0.5


def chunk_states(chunk, x_ref, weight, bias, kept, conv_ref, key_ref, sent_ref, pads_ref):
    matrix = spread_matrix()
    clear(pads_ref)

    def conv_tile(j):
        cols = slice(j * 128, (j + 1) * 128)
        return conv_rows(x_ref[:, cols].astype(f32), weight[:, cols], bias[j : j + 1], pads_ref.at[j % PADS])

    key = conv_tile(VALUES // 128 + chunk).astype(bf16)
    key_ref[...] = key
    for index in range(PER_CHUNK):
        group = chunk * PER_CHUNK + index
        scale = spread(kept, group, matrix)
        parts = []
        for i in range(WIDE // 128):
            local = index * WIDE + i * 128
            tile = conv_tile((chunk * HALF + local) // 128)
            conv_ref[:, local : local + 128] = tile.astype(bf16)
            parts.append((tile * scale[:, i * 128 : (i + 1) * 128]).astype(bf16))
        state = dot(
            key[:, index * STATE : (index + 1) * STATE], jnp.concatenate(parts, axis=1), ((0,), (0,))
        )
        sent_ref[index * STATE : (index + 1) * STATE, :] = state.astype(bf16)


def kept_weights(step, cumulative, goes_on):
    count = step.shape[1]
    last = cumulative[:, count - 1 :]
    tail = step * jnp.exp(last - cumulative)
    lanes = iota((HEADS, count), 1)
    kept = jnp.where((lanes >= EDGE) | (goes_on < 0.5), tail, 0.0)
    return kept, jnp.where(lanes == EDGE, jnp.exp(last), tail)


def first_kernel(
    lengths_hbm, x_hbm, step_hbm, weight_hbm, bias_hbm, rate_hbm, skip_hbm,
    conv_ref, key_ref, cumulative_ref, sent_ref, x_ref, weight_ref, bias_ref, step_ref, skip_ref, gates_ref,
    lengths_ref, rate_ref, pads_ref, sems,
):
    count = x_ref.shape[0]
    pairs = [
        (step_hbm.at[0], step_ref),
        (rate_hbm, rate_ref),
        (lengths_hbm, lengths_ref),
        (weight_hbm, weight_ref),
        (bias_hbm, bias_ref),
        (x_hbm.at[0], x_ref),
        (skip_hbm, skip_ref),
    ]
    copies = [pltpu.make_async_copy(a, b, sems.at[i]) for i, (a, b) in enumerate(pairs)]
    for i in ORDER:
        copies[i].start()
    for copy in copies[:3]:
        copy.wait()
    position = lax.axis_index("ctx")
    fresh = is_fresh(lengths_ref, position)
    goes_on = (1 - fresh).astype(f32)
    both = goes_on * (1 - is_fresh(lengths_ref, position - 1)).astype(f32)
    third = jnp.where(position == 2, 1.0, 0.0).astype(f32)
    rows = iota((8, WIDE), 0)
    gates_ref[...] = jnp.where(rows == 0, goes_on, jnp.where(rows == 1, both, third))
    step = step_ref[...]
    cumulative = cumulative_of(step, rate_ref[...])
    cumulative_ref[...] = cumulative
    kept = kept_weights(step, cumulative, goes_on)[0]
    for copy in copies[3:6]:
        copy.wait()
    weight, bias = half_taps(weight_ref, bias_ref)
    chunk_states(
        0,
        x_ref, weight, bias, kept, conv_ref, key_ref, sent_ref, pads_ref,
    )
    tail_rows = to_rows(x_ref[count - 16 :, :].astype(f32)[8:], 5)
    sent_ref[TAIL_AT : TAIL_AT + 16, :] = tail_rows.astype(bf16)
    copies[6].wait()


def later_kernel(
    x_ref, weight_ref, bias_ref, step_ref, cumulative_ref, gates_ref, before_ref,
    conv_ref, key_ref, sent_ref, early_ref, pads_ref,
):
    weight, bias = half_taps(weight_ref, bias_ref)
    kept, scales = kept_weights(step_ref[...], cumulative_ref[...], gates_ref[:1, :1])
    chunk_states(1, x_ref, weight, bias, kept, conv_ref, key_ref, sent_ref, pads_ref)
    high, low = halves(scales)
    place = iota((HEADS, 128), 1) - iota((HEADS, 128), 0)
    picked = dot(high, (place == 0).astype(bf16), ((0,), (0,)))
    picked = picked + dot(low, (place == HEADS).astype(bf16), ((0,), (0,)))
    line = jnp.concatenate([picked[k : k + 1] for k in range(4)], axis=1)
    head_rows = to_rows(x_ref[:16, :].astype(f32)[:8], 0)
    head_rows = jnp.where(iota((16, WIDE), 0) == 15, line, head_rows)
    sent_ref[HEAD_AT : HEAD_AT + 16, :] = head_rows.astype(bf16)
    early_ref[:ROWS, :] = before_ref[:ROWS, :]
    early_ref[ROWS : 2 * ROWS, :] = sent_ref[:ROWS, :]
    early_ref[2 * ROWS :, :] = before_ref[TAIL_AT : TAIL_AT + 16, :]


def known_part(head_block, table_ref):
    return (
        table_ref[0]
        + head_block * table_ref[1]
        + pltpu.roll(head_block, 1, 0) * table_ref[2]
        + pltpu.roll(head_block, 2, 0) * table_ref[3]
    )


def edge_rows(tail_block, known, table_ref):
    block = half_silu(
        known
        + tail_block * table_ref[4]
        + pltpu.roll(tail_block, 15, 0) * table_ref[5]
        + pltpu.roll(tail_block, 14, 0) * table_ref[6]
    )
    return [pltpu.roll(block, (16 - 3 * k) % 16, 0)[:8] for k in range(5)]


def head_lanes(rows):
    lanes = iota((128, VALUES), 1) // HEAD_DIM
    matrix = (iota((128, VALUES), 0) % HEADS == lanes).astype(bf16)
    return dot(rows, matrix)[:8]


def edge_scales(head_rows):
    line = head_rows[15:16].astype(f32)
    rows = [line[:, k * 128 : (k + 1) * 128] for k in range(4)]
    return head_lanes(jnp.concatenate(rows + [jnp.zeros((12, 128), f32)], axis=0).astype(bf16))


def prepare_kernel(
    later_ref, x_ref, weight_ref, bias_ref, cumulative_ref, step_ref, skip_ref, gates_ref,
    queries_ref, table_ref, known_ref, scale_ref, decay_ref, entry_ref, gain_ref, pads_ref,
):
    clear(pads_ref)
    weight, bias = half_taps(weight_ref, bias_ref)
    rows = iota((16, WIDE), 0)
    third = rows % 3
    chunk = rows // 3

    def blocked(lines):
        out = jnp.zeros((16, WIDE), f32)
        for k in range(5):
            out = jnp.where(chunk == k, lines[k], out)
        return out

    taps = [
        blocked([weight[tap : tap + 1, k * WIDE : (k + 1) * WIDE] for k in range(5)])
        for tap in range(4)
    ]
    table_ref[0] = blocked(
        [
            jnp.concatenate([bias[4 * k + i : 4 * k + i + 1, :] for i in range(4)], axis=1)
            for k in range(5)
        ]
    )
    table_ref[1] = taps[3]
    table_ref[2] = jnp.where(third == 0, 0.0, taps[2])
    table_ref[3] = jnp.where(third == 2, taps[1], 0.0)
    table_ref[4] = taps[0]
    table_ref[5] = jnp.where(third == 2, 0.0, taps[1])
    table_ref[6] = jnp.where(third == 0, taps[2], 0.0)
    known_ref[...] = known_part(later_ref[HEAD_AT : HEAD_AT + 16, :].astype(f32), table_ref)
    scale_ref[...] = edge_scales(later_ref[HEAD_AT : HEAD_AT + 16, :]) * gates_ref[:1, :1]
    cumulative = cumulative_ref[...] * LOG2E
    across = cumulative - jnp.log2(step_ref[...])
    down = cumulative.T
    count = down.shape[0]
    causal = iota((count, count), 0) >= iota((count, count), 1)
    for at in range(HEADS):
        gap = down[:, at : at + 1] - across[at : at + 1, :]
        decay_ref[at] = jnp.exp2(jnp.where(causal, gap, -1e30))
    matrix = spread_matrix()
    entry = jnp.exp2(cumulative)
    for group in range(BC_GROUPS):
        entry_ref[:, group * WIDE : (group + 1) * WIDE] = spread(entry, group, matrix)
    gain_ref[...] = head_lanes(
        jnp.concatenate(halves(skip_ref[...] + jnp.zeros((16, HEADS), f32)), axis=1)
    )
    first = VALUES + GROUPED
    for i in range(2):
        cols = slice(first + i * 128, first + (i + 1) * 128)
        j = first // 128 + i
        tile = conv_rows(
            x_ref[:, cols].astype(f32), weight[:, cols], bias[j : j + 1, :], pads_ref.at[i]
        )
        queries_ref[:, i * 128 : (i + 1) * 128] = tile.astype(bf16)


def edge_state(values_rows, keys_rows, scale, group):
    rows = iota((8, WIDE), 0)
    written = jnp.where(rows < EDGE, values_rows * scale, 0.0)
    tile = keys_rows[:, (group // 2) * 128 : (group // 2 + 1) * 128].astype(bf16)
    return dot(tile[:, (group % 2) * STATE : (group % 2 + 1) * STATE], written.astype(bf16), ((0,), (0,)))


def combine_chunk(own_ref, got_ref, decays, extras, sent_ref):
    for index in range(PER_CHUNK):
        at = slice(index * STATE, (index + 1) * STATE)
        total = own_ref[at, :].astype(f32) + extras[index] + decays[index] * got_ref[at, :].astype(f32)
        sent_ref[at, :] = total.astype(bf16)


def group_cols(group):
    return slice(group * WIDE, (group + 1) * WIDE)


def combine_first_kernel(own_ref, got_ref, table_ref, known_ref, gates_ref, scale_ref, sent_ref, edge_ref):
    tail_block = got_ref[TAIL_AT : TAIL_AT + 16, :].astype(f32) * gates_ref[:1, :]
    chunks = edge_rows(tail_block, known_ref[...], table_ref)
    scales = [scale_ref[:, group_cols(group)] for group in range(PER_CHUNK)]
    extras = [edge_state(chunks[g], chunks[BC_GROUPS], scales[g], g) for g in range(PER_CHUNK)]
    decays = [scale[EDGE : EDGE + 1] for scale in scales]
    combine_chunk(own_ref, got_ref, decays, extras, sent_ref)
    sent_ref[ROWS:, :] = own_ref[TAIL_AT : TAIL_AT + 16, :]
    for k in range(5):
        edge_ref[:, k * WIDE : (k + 1) * WIDE] = chunks[k]


def combine_later_kernel(own_ref, got_ref, scale_ref, extra_ref, sent_ref):
    groups = range(PER_CHUNK, BC_GROUPS)
    decays = [scale_ref[EDGE : EDGE + 1, group_cols(group)] for group in groups]
    extras = [extra_ref[index * STATE : (index + 1) * STATE, :] for index in range(PER_CHUNK)]
    combine_chunk(own_ref, got_ref, decays, extras, sent_ref)


def diagonal_chunk(chunk, conv_ref, key_ref, raw_queries_ref, edge_ref, decay_ref, gain_ref, diagonal_ref, queries_ref):
    count = conv_ref.shape[0]
    edge_row = iota((count, 128), 0) < EDGE
    lane_head = iota((count, 128), 1) // HEAD_DIM

    def patched(tile, j):
        rows = jnp.concatenate(
            [edge_ref[:, j * 128 : (j + 1) * 128], jnp.zeros((count - 8, 128), f32)], axis=0
        )
        return jnp.where(edge_row, rows, tile.astype(f32))

    keys = patched(key_ref[...], VALUES // 128 + chunk).astype(bf16)
    j = (VALUES + GROUPED) // 128 + chunk
    queries = patched(raw_queries_ref[:, chunk * 128 : (chunk + 1) * 128], j).astype(bf16)
    queries_ref[...] = queries
    for index in range(PER_CHUNK):
        part = slice(index * STATE, (index + 1) * STATE)
        scores = dot(queries[:, part], keys[:, part], ((1,), (1,)))
        for i in range(WIDE // 128):
            at = index * WIDE + i * 128
            j = (chunk * HALF + at) // 128
            values = patched(conv_ref[:, at : at + 128], j)
            weights, parts = [], []
            for k in range(4):
                weights.append((decay_ref[4 * j + k] * scores).astype(bf16))
                parts.append(jnp.where(lane_head == k, values, 0.0).astype(bf16))
            total = dot(jnp.concatenate(weights, axis=1), jnp.concatenate(parts, axis=0))
            diagonal_ref[:, at : at + 128] = total + gain_ref[:1, j * 128 : (j + 1) * 128] * values


def diagonal_first_kernel(
    conv_ref, key_ref, raw_queries_ref, edge_ref, decay_ref, gain_ref, own_scale_ref,
    diagonal_ref, queries_ref, extra_ref,
):
    keys = edge_ref[:, BC_GROUPS * WIDE :]
    for index in range(PER_CHUNK):
        group = PER_CHUNK + index
        cols = group_cols(group)
        extra_ref[index * STATE : (index + 1) * STATE, :] = edge_state(
            edge_ref[:, cols], keys, own_scale_ref[:, cols], group
        )
    diagonal_chunk(0, conv_ref, key_ref, raw_queries_ref, edge_ref, decay_ref, gain_ref, diagonal_ref, queries_ref)


def diagonal_later_kernel(
    conv_ref, key_ref, raw_queries_ref, edge_ref, decay_ref, gain_ref, later_ref, table_ref, gates_ref, before_ref,
    diagonal_ref, queries_ref, known_ref, scale_ref, out_hbm, out_ref, sems,
):
    head_rows = later_ref[HEAD_AT : HEAD_AT + 16, :]
    known_ref[...] = known_part(head_rows.astype(f32), table_ref)
    scale_ref[...] = edge_scales(head_rows) * gates_ref[1:2, :1]
    diagonal_chunk(1, conv_ref, key_ref, raw_queries_ref, edge_ref, decay_ref, gain_ref, diagonal_ref, queries_ref)

    @pl.when(lax.axis_index("ctx") == 0)
    def _():
        copies = []
        for chunk, ref in enumerate((before_ref, diagonal_ref)):
            here = pl.ds(chunk * HALF, HALF)
            out_ref[:, here] = ref[...].astype(bf16)
            copies.append(pltpu.make_async_copy(out_ref.at[:, here], out_hbm.at[0, :, here], sems.at[chunk]))
            copies[-1].start()
        for copy in copies:
            copy.wait()


def group_out(group, total, diagonal_ref, queries_ref, entry_ref):
    index = group % PER_CHUNK
    here = slice(index * WIDE, (index + 1) * WIDE)
    carried = dot(queries_ref[:, index * STATE : (index + 1) * STATE], total.astype(bf16))
    return (diagonal_ref[:, here] + entry_ref[:, group_cols(group)] * carried).astype(bf16)


def finish_first_kernel(
    first0_ref, first1_ref, second_ref, early_ref, table_ref, known_ref, gates_ref, scale_ref, diagonal_ref,
    queries_ref, later_diagonal_ref, later_queries_ref, entry_ref, done_hbm,
    out_hbm, out_ref, base_ref, decay_ref, later_ref, sems,
):
    position = lax.axis_index("ctx")

    @pl.when(position > 0)
    def _():
        third = gates_ref[2:3, :] > 0.5
        kept = gates_ref[:1, :]

        def second_of(at, early_at, rows):
            a = second_ref[at : at + rows, :].astype(f32)
            return jnp.where(third, early_ref[early_at : early_at + rows, :].astype(f32), a)

        chunks = edge_rows(second_of(ROWS, 2 * ROWS, 16), known_ref[...], table_ref)
        for group in range(BC_GROUPS):
            chunk, index = divmod(group, PER_CHUNK)
            at = slice(index * STATE, (index + 1) * STATE)
            scale = scale_ref[:, group_cols(group)]
            decay = scale[EDGE : EDGE + 1]
            first = (first0_ref, first1_ref)[chunk][at, :].astype(f32)
            total = first * kept + edge_state(chunks[group], chunks[BC_GROUPS], scale, group)
            if chunk == 0:
                total = total + decay * second_of(index * STATE, index * STATE, STATE)
                out_ref[:, group_cols(group)] = group_out(group, total, diagonal_ref, queries_ref, entry_ref)
            else:
                early = early_ref[ROWS + index * STATE : ROWS + (index + 1) * STATE, :].astype(f32)
                base_ref[at, :] = jnp.where(third, total + decay * early, total)
                decay_ref[index * 8 : (index + 1) * 8, :] = jnp.where(third, 0.0, decay) + jnp.zeros((8, WIDE), f32)

    @pl.when((position > 0) & (position <= LAST_LOW))
    def _():
        copies = [
            pltpu.make_async_copy(out_ref, out_hbm.at[0, :, pl.ds(0, HALF)], sems.at[0]),
            pltpu.make_async_copy(later_ref, out_hbm.at[0, :, pl.ds(HALF, HALF)], sems.at[1]),
        ]
        copies[0].start()
        for index in range(PER_CHUNK):
            at = slice(index * STATE, (index + 1) * STATE)
            later_ref[:, index * WIDE : (index + 1) * WIDE] = group_out(
                PER_CHUNK + index, base_ref[at, :], later_diagonal_ref, later_queries_ref, entry_ref
            )
        copies[1].start()
        for copy in copies:
            copy.wait()


def finish_later_kernel(
    second_ref, base_ref, decay_ref, diagonal_ref, queries_ref, entry_ref, before_ref, done_hbm, out_hbm, out_ref, sems
):
    @pl.when(lax.axis_index("ctx") > LAST_LOW)
    def _():
        copies = [
            pltpu.make_async_copy(before_ref, out_hbm.at[0, :, pl.ds(0, HALF)], sems.at[PER_CHUNK])
        ]
        copies[0].start()
        for index in range(PER_CHUNK):
            group = PER_CHUNK + index
            at = slice(index * STATE, (index + 1) * STATE)
            decay = decay_ref[index * 8 : index * 8 + 1, :]
            total = base_ref[at, :] + decay * second_ref[at, :].astype(f32)
            here = pl.ds(index * WIDE, WIDE)
            out_ref[:, here] = group_out(group, total, diagonal_ref, queries_ref, entry_ref)
            copy = pltpu.make_async_copy(
                out_ref.at[:, here], out_hbm.at[0, :, pl.ds(group * WIDE, WIDE)], sems.at[index]
            )
            copy.start()
            copies.append(copy)
        for copy in copies:
            copy.wait()


def call(kernel, outs, in_specs, cost, args, out_specs=None, scratch=(), aliases={}):
    return pl.pallas_call(
        kernel,
        out_shape=outs,
        in_specs=in_specs,
        out_specs=out_specs or jax.tree.map(lambda _: VMEM, outs),
        scratch_shapes=scratch,
        input_output_aliases=aliases,
        compiler_params=pltpu.CompilerParams(vmem_limit_bytes=24 * 1024 * 1024),
        cost_estimate=pl.CostEstimate(flops=cost[0], bytes_accessed=cost[1], transcendentals=0),
    )(*args)


def permuted(array, edges):
    size, lanes = lax.axis_size("ctx"), lax.axis_size("lane")
    table = []
    for source in range(size):
        for lane in range(lanes):
            if source in edges:
                target = edges[source] * lanes + lane
            else:
                target = source * lanes + (lane + 1) % lanes
            table.append((source * lanes + lane, target))
    return lax.ppermute(array, ("ctx", "lane"), table)


def shard_near(pre_conv, step_size, lengths, conv_weight, conv_bias, decay_rate, skip_gain):
    count, channels = pre_conv.shape[1:]
    size = lax.axis_size("ctx")
    ring = [(i, (i + 1) % size) for i in range(size)]
    onward = {i: i + 2 for i in range(1, size - 2)}
    onward[size - 2] = 2
    onward[size - 1] = 1
    arguments = tuple(
        pltpu.with_memory_space_constraint(array, pltpu.HBM)
        for array in (
            lengths,
            pre_conv,
            step_size,
            conv_weight,
            conv_bias.reshape(-1, 128),
            decay_rate.reshape(1, -1),
            skip_gain.reshape(1, -1),
        )
    )
    sds = jax.ShapeDtypeStruct
    pads = pltpu.VMEM((PADS, count + 8, 128), f32)
    conv0, key0, cumulative, own0, x, weight, bias, step, skip, gates = call(
        first_kernel,
        (
            sds((count, HALF), bf16),
            sds((count, 128), bf16),
            sds((HEADS, count), f32),
            sds((SENT, WIDE), bf16),
            sds((count, channels), bf16),
            sds(conv_weight.shape, bf16),
            sds((channels // 128, 128), bf16),
            sds((HEADS, count), f32),
            sds((1, HEADS), f32),
            sds((8, WIDE), f32),
        ),
        [HBM] * 7,
        (40_000_000, 2_000_000),
        arguments,
        scratch=(
            pltpu.SMEM(lengths.shape, jnp.int32),
            pltpu.VMEM((1, HEADS), f32),
            pads,
            pltpu.SemaphoreType.DMA((7,)),
        ),
    )
    first0 = lax.ppermute(own0, "ctx", ring)
    conv1, key1, own1, early = call(
        later_kernel,
        (
            sds((count, HALF), bf16),
            sds((count, 128), bf16),
            sds((SENT, WIDE), bf16),
            sds((2 * ROWS + 16, WIDE), bf16),
        ),
        [VMEM] * 7,
        (40_000_000, 2_000_000),
        (x, weight, bias, step, cumulative, gates, own0),
        scratch=(pads,),
    )
    first1 = lax.ppermute(own1, "ctx", ring)
    early = permuted(early, {0: 2, 2: 0})
    raw_queries, table, known, scale, decay, entry, gain = call(
        prepare_kernel,
        (
            sds((count, GROUPED), bf16),
            sds((7, 16, WIDE), f32),
            sds((16, WIDE), f32),
            sds((8, VALUES), f32),
            sds((HEADS, count, count), f32),
            sds((count, VALUES), f32),
            sds((8, VALUES), f32),
        ),
        [VMEM] * 8,
        (100_000_000, 1_000_000),
        (own1, x, weight, bias, cumulative, step, skip, gates),
        scratch=(pads,),
    )
    sent0, edge = call(
        combine_first_kernel,
        (sds((ROWS + 16, WIDE), bf16), sds((8, channels), f32)),
        [VMEM] * 6,
        (1_000_000, 1_000_000),
        (own0, first0, table, known, gates, scale),
    )
    second0 = permuted(sent0, onward)
    diagonal_outs = (sds((count, HALF), f32), sds((count, 128), bf16))
    diagonal0, queries0, extra = call(
        diagonal_first_kernel,
        diagonal_outs + (sds((ROWS, WIDE), f32),),
        [VMEM] * 7,
        (200_000_000, 2_000_000),
        (conv0, key0, raw_queries, edge, decay, gain, scale),
    )
    sent1 = call(
        combine_later_kernel,
        sds((ROWS, WIDE), bf16),
        [VMEM] * 4,
        (1_000_000, 1_000_000),
        (own1, first1, scale, extra),
    )
    second1 = permuted(sent1, onward)
    out_shape = sds((1, count, VALUES), bf16)
    diagonal1, queries1, known, scale, out = call(
        diagonal_later_kernel,
        diagonal_outs + (sds((16, WIDE), f32), sds((8, VALUES), f32), out_shape),
        [VMEM] * 10,
        (200_000_000, 2_000_000),
        (conv1, key1, raw_queries, edge, decay, gain, first1, table, gates, diagonal0),
        out_specs=(VMEM, VMEM, VMEM, VMEM, HBM),
        scratch=(pltpu.VMEM((count, VALUES), bf16), pltpu.SemaphoreType.DMA((CHUNKS,))),
    )
    out, out0, base, decay = call(
        finish_first_kernel,
        (
            out_shape,
            sds((count, HALF), bf16),
            sds((ROWS, WIDE), f32),
            sds((8 * PER_CHUNK, WIDE), f32),
        ),
        [VMEM] * 13 + [HBM],
        (50_000_000, 2_000_000),
        (
            first0, first1, second0, early, table, known, gates, scale,
            diagonal0, queries0, diagonal1, queries1, entry, out,
        ),
        out_specs=(HBM, VMEM, VMEM, VMEM),
        scratch=(pltpu.VMEM((count, HALF), bf16), pltpu.SemaphoreType.DMA((2,))),
        aliases={13: 0},
    )
    return call(
        finish_later_kernel,
        out_shape,
        [VMEM] * 7 + [HBM],
        (50_000_000, 2_000_000),
        (second1, base, decay, diagonal1, queries1, entry, out0, out),
        out_specs=HBM,
        scratch=(pltpu.VMEM((count, HALF), bf16), pltpu.SemaphoreType.DMA((PER_CHUNK + 1,))),
        aliases={7: 0},
    )


def shifted(value, axis, steps):
    count = lax.axis_size(axis)
    first, last = (max(0, -steps), min(count, count - steps))
    return lax.ppermute(value, axis, [(source, source + steps) for source in range(first, last)])


def carried_in(array, axis, combine, identity):
    length, index = (lax.axis_size(axis), lax.axis_index(axis))
    everything = jax.tree.map(
        lambda part, kind: lax.all_gather(part.astype(kind), axis),
        array,
        (jnp.bfloat16, jnp.bfloat16),
    )
    start = jax.tree.map(
        lambda part, zero: jnp.broadcast_to(jnp.asarray(zero, part.dtype), part.shape),
        array,
        identity,
    )

    def step(k, before):
        reached = k < index
        new = combine(
            before, jax.tree.map(lambda part, own: part[k].astype(own.dtype), everything, array)
        )
        return jax.tree.map(lambda a, b: jnp.where(reached, a, b), new, before)

    return lax.fori_loop(0, length, step, start)


def convolve(padded, conv_weight, conv_bias, count_rows):
    total = conv_bias.astype(jnp.float32)[None, :]
    for offset in range(conv_weight.shape[0]):
        total = (
            total
            + padded[offset : offset + count_rows].astype(jnp.float32)
            * conv_weight[offset].astype(jnp.float32)[None, :]
        )
    return jax.nn.silu(total).astype(jnp.bfloat16)


def group_terms(values, keys_in, queries, decay_rate, step_rows):
    heads_group = step_rows.shape[0]
    count_rows = step_rows.shape[1]
    values = values.reshape(count_rows, heads_group, -1)
    cumulative = jnp.cumsum(-step_rows * decay_rate[:, None], axis=1)
    scores = jnp.einsum("tn,sn->ts", queries, keys_in, preferred_element_type=jnp.float32)
    later = lax.broadcasted_iota(jnp.int32, (count_rows, count_rows), 0)
    earlier = lax.broadcasted_iota(jnp.int32, (count_rows, count_rows), 1)
    spread = jnp.where(
        (later >= earlier)[None], cumulative[:, :, None] - cumulative[:, None, :], -1e30
    )
    weights = (jnp.exp(spread) * scores[None]).astype(jnp.bfloat16)
    scaled = (values * step_rows.T[:, :, None]).astype(jnp.bfloat16)
    diagonal_part = jnp.einsum("hts,shp->thp", weights, scaled, preferred_element_type=jnp.float32)
    tail_weight = jnp.exp(cumulative[:, -1:] - cumulative)
    written = (values * (step_rows * tail_weight).T[:, :, None]).astype(jnp.bfloat16)
    local_state = jnp.einsum("tn,thp->hpn", keys_in, written, preferred_element_type=jnp.float32)
    return (diagonal_part, local_state, jnp.exp(cumulative[:, -1]), jnp.exp(cumulative), values)


def finish_group(diagonal_part, entry_decay, queries, incoming, values, skip_gain):
    incoming_rounded = incoming.astype(jnp.bfloat16)
    carried_part = jnp.einsum(
        "tn,hpn->thp", queries, incoming_rounded, preferred_element_type=jnp.float32
    )
    carried_part = carried_part * entry_decay.T[:, :, None]
    return diagonal_part + carried_part + skip_gain[None, :, None] * values.astype(jnp.float32)


def combine(earlier, later):
    return (earlier[0] * later[0], later[0][:, None, None] * earlier[1] + later[1])


def shard_far(pre_conv, step_size, lengths, conv_weight, conv_bias, decay_rate, skip_gain):
    count_rows = pre_conv.shape[1]
    kernel_len = conv_weight.shape[0]
    heads_group = HEADS // BC_GROUPS
    position = lax.axis_index("ctx")
    sizes_row = lengths[0]
    starts = jnp.cumsum(sizes_row) - sizes_row
    fresh = jnp.any(starts == position)
    retain = jnp.where(fresh, 0.0, 1.0).astype(jnp.float32)
    own_rows = pre_conv[0]
    previous = shifted(own_rows[count_rows - kernel_len + 1 :], "ctx", 1)
    previous = jnp.where(fresh, jnp.zeros_like(previous), previous)
    convolved = convolve(
        jnp.concatenate([previous, own_rows], axis=0), conv_weight, conv_bias, count_rows
    )
    values = convolved[:, : HEADS * HEAD_DIM]
    keys_all = convolved[:, HEADS * HEAD_DIM : HEADS * HEAD_DIM + BC_GROUPS * STATE]
    queries_all = convolved[:, HEADS * HEAD_DIM + BC_GROUPS * STATE :]
    step_rows = step_size[0]
    results = []
    pieces = []
    for bc_group in range(BC_GROUPS):
        low = bc_group * heads_group
        high = low + heads_group
        pieces.append(
            group_terms(
                values[:, low * HEAD_DIM : high * HEAD_DIM],
                keys_all[:, bc_group * STATE : (bc_group + 1) * STATE],
                queries_all[:, bc_group * STATE : (bc_group + 1) * STATE],
                decay_rate[low:high],
                step_rows[low:high],
            )
        )
    decays = jnp.concatenate([piece[2] for piece in pieces], axis=0) * retain
    states = jnp.concatenate([piece[1] for piece in pieces], axis=0)
    identity = (jnp.ones_like(decays), jnp.zeros_like(states))
    totals = carried_in((decays, states), "ctx", combine, identity)
    incoming = totals[1] * retain
    for bc_group in range(BC_GROUPS):
        low = bc_group * heads_group
        high = low + heads_group
        piece = pieces[bc_group]
        results.append(
            finish_group(
                piece[0],
                piece[3],
                queries_all[:, bc_group * STATE : (bc_group + 1) * STATE],
                incoming[low:high],
                piece[4],
                skip_gain[low:high],
            )
        )
    output = (
        jnp.concatenate(results, axis=1).reshape(count_rows, HEADS * HEAD_DIM).astype(jnp.bfloat16)
    )
    return output[None]


def solution(mesh):
    in_specs = (
        P(("groups", "lane"), "ctx", None),
        P(("groups", "lane"), None, "ctx"),
        P(("groups", "lane"), None),
        P(),
        P(),
        P(),
        P(),
    )
    out_specs = P(("groups", "lane"), "ctx", None)
    shards = shard_near if mesh.shape["ctx"] <= 8 else shard_far
    return jax.shard_map(shards, mesh=mesh, in_specs=in_specs, out_specs=out_specs, check_vma=False)
```

```python
import jax
import jax.numpy as jnp
from jax import lax
from jax.experimental import pallas as pl
from jax.experimental.pallas import tpu as pltpu
from jax.sharding import PartitionSpec as P

HEADS = 64
HEAD_DIM = 32
EDGE = 3
STATE = 64
BC_GROUPS = 4
HEADS_GROUP = HEADS // BC_GROUPS
VALUES = HEADS * HEAD_DIM
WIDE = HEADS_GROUP * HEAD_DIM
GROUPED = BC_GROUPS * STATE
CHUNKS = 2
PADS = 4
ORDER = (0, 1, 2, 5, 3, 4, 6)
PER_CHUNK = BC_GROUPS // CHUNKS
HALF = PER_CHUNK * WIDE
ROWS = PER_CHUNK * STATE
TAIL_AT = ROWS
HEAD_AT = ROWS
SENT = ROWS + 16
LAST_LOW = 2
LOG2E = 1.4426950408889634
VMEM = pl.BlockSpec(memory_space=pltpu.VMEM)
HBM = pl.BlockSpec(memory_space=pltpu.HBM)
f32 = jnp.float32
bf16 = jnp.bfloat16


def iota(shape, dim):
    return lax.broadcasted_iota(jnp.int32, shape, dim)


def dot(a, b, contract=((1,), (0,))):
    return lax.dot_general(a, b, (contract, ((), ())), preferred_element_type=f32)


def is_fresh(lengths_ref, position):
    found = jnp.int32(0)
    start = jnp.int32(0)
    for k in range(lengths_ref.shape[1]):
        found = jnp.where(start == position, jnp.int32(1), found)
        start = start + lengths_ref[0, k]
    return found


def halves(value):
    high = value.astype(bf16)
    return high, (value - high.astype(f32)).astype(bf16)


def cumulative_of(step, rate_row):
    eye = iota((HEADS, HEADS), 0) == iota((HEADS, HEADS), 1)
    rate = jnp.sum(jnp.where(eye, rate_row, 0.0), axis=1, keepdims=True)
    tokens = step.shape[1]
    upto = iota((tokens, tokens), 0) <= iota((tokens, tokens), 1)
    upto = upto.astype(bf16)
    rest = -step * rate
    total = jnp.zeros_like(rest)
    for _ in range(3):
        part = rest.astype(bf16)
        rest = rest - part.astype(f32)
        total = total + dot(part, upto)
    return total


def spread_matrix():
    rows, lanes = 2 * HEADS_GROUP, WIDE
    return (iota((rows, lanes), 0) % HEADS_GROUP == iota((rows, lanes), 1) // HEAD_DIM).astype(bf16)


def spread(per_head, group, matrix):
    part = per_head[group * HEADS_GROUP : (group + 1) * HEADS_GROUP]
    return dot(jnp.concatenate(halves(part), axis=0), matrix, ((0,), (0,)))


def half_silu(half):
    return half + half * jnp.tanh(half)


def to_rows(strip, first):
    rows = iota((8, WIDE), 0)
    top = jnp.zeros((8, WIDE), f32)
    low = jnp.zeros((8, WIDE), f32)
    for k in range(strip.shape[1] // WIDE):
        moved = pltpu.roll(strip[:, k * WIDE : (k + 1) * WIDE], (3 * k - first) % 8, 0)
        if 3 * k < 8:
            top = jnp.where((rows >= 3 * k) & (rows < 3 * k + 3), moved, top)
        if 3 * k + 2 >= 8:
            low = jnp.where((rows >= 3 * k - 8) & (rows < 3 * k - 5), moved, low)
    return jnp.concatenate([top, low], axis=0)


def conv_rows(x, weight, bias, pad_ref):
    count = x.shape[0]
    pad_ref[8 : 8 + count, :] = x
    total = bias + x * weight[3:4]
    for back in range(1, 4):
        total = total + pad_ref[8 - back : 8 - back + count, :] * weight[3 - back : 4 - back]
    return half_silu(total)


def clear(pads_ref):
    for slot in range(PADS):
        pads_ref[slot, :8, :] = jnp.zeros((8, 128), f32)


def half_taps(weight_ref, bias_ref):
    return weight_ref[...].astype(f32) * 0.5, bias_ref[...].astype(f32) * 0.5


def chunk_states(chunk, x_ref, weight, bias, kept, conv_ref, key_ref, sent_ref, pads_ref):
    matrix = spread_matrix()
    clear(pads_ref)

    def conv_tile(j):
        cols = slice(j * 128, (j + 1) * 128)
        return conv_rows(x_ref[:, cols].astype(f32), weight[:, cols], bias[j : j + 1], pads_ref.at[j % PADS])

    key = conv_tile(VALUES // 128 + chunk).astype(bf16)
    key_ref[...] = key
    for index in range(PER_CHUNK):
        group = chunk * PER_CHUNK + index
        scale = spread(kept, group, matrix)
        parts = []
        for i in range(WIDE // 128):
            local = index * WIDE + i * 128
            tile = conv_tile((chunk * HALF + local) // 128)
            conv_ref[:, local : local + 128] = tile.astype(bf16)
            parts.append((tile * scale[:, i * 128 : (i + 1) * 128]).astype(bf16))
        state = dot(
            key[:, index * STATE : (index + 1) * STATE], jnp.concatenate(parts, axis=1), ((0,), (0,))
        )
        sent_ref[index * STATE : (index + 1) * STATE, :] = state.astype(bf16)


def kept_weights(step, cumulative, goes_on):
    count = step.shape[1]
    last = cumulative[:, count - 1 :]
    tail = step * jnp.exp(last - cumulative)
    lanes = iota((HEADS, count), 1)
    kept = jnp.where((lanes >= EDGE) | (goes_on < 0.5), tail, 0.0)
    return kept, jnp.where(lanes == EDGE, jnp.exp(last), tail)


def first_kernel(
    lengths_hbm, x_hbm, step_hbm, weight_hbm, bias_hbm, rate_hbm, skip_hbm,
    conv_ref, key_ref, cumulative_ref, sent_ref, x_ref, weight_ref, bias_ref, step_ref, skip_ref, gates_ref,
    lengths_ref, rate_ref, pads_ref, sems,
):
    count = x_ref.shape[0]
    pairs = [
        (step_hbm.at[0], step_ref),
        (rate_hbm, rate_ref),
        (lengths_hbm, lengths_ref),
        (weight_hbm, weight_ref),
        (bias_hbm, bias_ref),
        (x_hbm.at[0], x_ref),
        (skip_hbm, skip_ref),
    ]
    copies = [pltpu.make_async_copy(a, b, sems.at[i]) for i, (a, b) in enumerate(pairs)]
    for i in ORDER:
        copies[i].start()
    for copy in copies[:3]:
        copy.wait()
    position = lax.axis_index("ctx")
    fresh = is_fresh(lengths_ref, position)
    goes_on = (1 - fresh).astype(f32)
    both = goes_on * (1 - is_fresh(lengths_ref, position - 1)).astype(f32)
    third = jnp.where(position == 2, 1.0, 0.0).astype(f32)
    rows = iota((8, WIDE), 0)
    gates_ref[...] = jnp.where(rows == 0, goes_on, jnp.where(rows == 1, both, third))
    step = step_ref[...]
    cumulative = cumulative_of(step, rate_ref[...])
    cumulative_ref[...] = cumulative
    kept = kept_weights(step, cumulative, goes_on)[0]
    for copy in copies[3:6]:
        copy.wait()
    weight, bias = half_taps(weight_ref, bias_ref)
    chunk_states(
        0,
        x_ref, weight, bias, kept, conv_ref, key_ref, sent_ref, pads_ref,
    )
    tail_rows = to_rows(x_ref[count - 16 :, :].astype(f32)[8:], 5)
    sent_ref[TAIL_AT : TAIL_AT + 16, :] = tail_rows.astype(bf16)
    copies[6].wait()


def later_kernel(
    x_ref, weight_ref, bias_ref, step_ref, cumulative_ref, gates_ref, before_ref,
    conv_ref, key_ref, sent_ref, early_ref, pads_ref,
):
    weight, bias = half_taps(weight_ref, bias_ref)
    kept, scales = kept_weights(step_ref[...], cumulative_ref[...], gates_ref[:1, :1])
    chunk_states(1, x_ref, weight, bias, kept, conv_ref, key_ref, sent_ref, pads_ref)
    high, low = halves(scales)
    place = iota((HEADS, 128), 1) - iota((HEADS, 128), 0)
    picked = dot(high, (place == 0).astype(bf16), ((0,), (0,)))
    picked = picked + dot(low, (place == HEADS).astype(bf16), ((0,), (0,)))
    line = jnp.concatenate([picked[k : k + 1] for k in range(4)], axis=1)
    head_rows = to_rows(x_ref[:16, :].astype(f32)[:8], 0)
    head_rows = jnp.where(iota((16, WIDE), 0) == 15, line, head_rows)
    sent_ref[HEAD_AT : HEAD_AT + 16, :] = head_rows.astype(bf16)
    early_ref[:ROWS, :] = before_ref[:ROWS, :]
    early_ref[ROWS : 2 * ROWS, :] = sent_ref[:ROWS, :]
    early_ref[2 * ROWS :, :] = before_ref[TAIL_AT : TAIL_AT + 16, :]


def known_part(head_block, table_ref):
    return (
        table_ref[0]
        + head_block * table_ref[1]
        + pltpu.roll(head_block, 1, 0) * table_ref[2]
        + pltpu.roll(head_block, 2, 0) * table_ref[3]
    )


def edge_rows(tail_block, known, table_ref):
    block = half_silu(
        known
        + tail_block * table_ref[4]
        + pltpu.roll(tail_block, 15, 0) * table_ref[5]
        + pltpu.roll(tail_block, 14, 0) * table_ref[6]
    )
    return [pltpu.roll(block, (16 - 3 * k) % 16, 0)[:8] for k in range(5)]


def head_lanes(rows):
    lanes = iota((128, VALUES), 1) // HEAD_DIM
    matrix = (iota((128, VALUES), 0) % HEADS == lanes).astype(bf16)
    return dot(rows, matrix)[:8]


def edge_scales(head_rows):
    line = head_rows[15:16].astype(f32)
    rows = [line[:, k * 128 : (k + 1) * 128] for k in range(4)]
    return head_lanes(jnp.concatenate(rows + [jnp.zeros((12, 128), f32)], axis=0).astype(bf16))


def causal_mask(count):
    return iota((count, count), 0) >= iota((count, count), 1)


def token_decay(at, across_ref, down_ref, causal):
    gap = down_ref[:, at : at + 1] - across_ref[at : at + 1, :]
    return jnp.exp2(jnp.where(causal, gap, -1e30))


def prepare_kernel(
    later_ref, x_ref, weight_ref, bias_ref, cumulative_ref, step_ref, skip_ref, gates_ref,
    queries_ref, table_ref, known_ref, scale_ref, decay_ref, across_ref, down_ref, entry_ref, gain_ref, pads_ref,
):
    clear(pads_ref)
    weight, bias = half_taps(weight_ref, bias_ref)
    rows = iota((16, WIDE), 0)
    third = rows % 3
    chunk = rows // 3

    def blocked(lines):
        out = jnp.zeros((16, WIDE), f32)
        for k in range(5):
            out = jnp.where(chunk == k, lines[k], out)
        return out

    taps = [
        blocked([weight[tap : tap + 1, k * WIDE : (k + 1) * WIDE] for k in range(5)])
        for tap in range(4)
    ]
    table_ref[0] = blocked(
        [
            jnp.concatenate([bias[4 * k + i : 4 * k + i + 1, :] for i in range(4)], axis=1)
            for k in range(5)
        ]
    )
    table_ref[1] = taps[3]
    table_ref[2] = jnp.where(third == 0, 0.0, taps[2])
    table_ref[3] = jnp.where(third == 2, taps[1], 0.0)
    table_ref[4] = taps[0]
    table_ref[5] = jnp.where(third == 2, 0.0, taps[1])
    table_ref[6] = jnp.where(third == 0, taps[2], 0.0)
    known_ref[...] = known_part(later_ref[HEAD_AT : HEAD_AT + 16, :].astype(f32), table_ref)
    scale_ref[...] = edge_scales(later_ref[HEAD_AT : HEAD_AT + 16, :]) * gates_ref[:1, :1]
    cumulative = cumulative_ref[...] * LOG2E
    across_ref[...] = cumulative - jnp.log2(step_ref[...])
    down_ref[...] = cumulative.T
    causal = causal_mask(across_ref.shape[1])
    for at in range(HEADS // CHUNKS):
        decay_ref[at] = token_decay(at, across_ref, down_ref, causal)
    matrix = spread_matrix()
    entry = jnp.exp2(cumulative)
    for group in range(BC_GROUPS):
        entry_ref[:, group * WIDE : (group + 1) * WIDE] = spread(entry, group, matrix)
    gain_ref[...] = head_lanes(
        jnp.concatenate(halves(skip_ref[...] + jnp.zeros((16, HEADS), f32)), axis=1)
    )
    first = VALUES + GROUPED
    for i in range(2):
        cols = slice(first + i * 128, first + (i + 1) * 128)
        j = first // 128 + i
        tile = conv_rows(
            x_ref[:, cols].astype(f32), weight[:, cols], bias[j : j + 1, :], pads_ref.at[i]
        )
        queries_ref[:, i * 128 : (i + 1) * 128] = tile.astype(bf16)


def edge_state(values_rows, keys_rows, scale, group):
    rows = iota((8, WIDE), 0)
    written = jnp.where(rows < EDGE, values_rows * scale, 0.0)
    tile = keys_rows[:, (group // 2) * 128 : (group // 2 + 1) * 128].astype(bf16)
    return dot(tile[:, (group % 2) * STATE : (group % 2 + 1) * STATE], written.astype(bf16), ((0,), (0,)))


def combine_chunk(own_ref, got_ref, decays, extras, sent_ref):
    for index in range(PER_CHUNK):
        at = slice(index * STATE, (index + 1) * STATE)
        total = own_ref[at, :].astype(f32) + extras[index] + decays[index] * got_ref[at, :].astype(f32)
        sent_ref[at, :] = total.astype(bf16)


def group_cols(group):
    return slice(group * WIDE, (group + 1) * WIDE)


def combine_first_kernel(own_ref, got_ref, table_ref, known_ref, gates_ref, scale_ref, sent_ref, edge_ref):
    tail_block = got_ref[TAIL_AT : TAIL_AT + 16, :].astype(f32) * gates_ref[:1, :]
    chunks = edge_rows(tail_block, known_ref[...], table_ref)
    scales = [scale_ref[:, group_cols(group)] for group in range(PER_CHUNK)]
    extras = [edge_state(chunks[g], chunks[BC_GROUPS], scales[g], g) for g in range(PER_CHUNK)]
    decays = [scale[EDGE : EDGE + 1] for scale in scales]
    combine_chunk(own_ref, got_ref, decays, extras, sent_ref)
    sent_ref[ROWS:, :] = own_ref[TAIL_AT : TAIL_AT + 16, :]
    for k in range(5):
        edge_ref[:, k * WIDE : (k + 1) * WIDE] = chunks[k]


def combine_later_kernel(own_ref, got_ref, scale_ref, extra_ref, sent_ref):
    groups = range(PER_CHUNK, BC_GROUPS)
    decays = [scale_ref[EDGE : EDGE + 1, group_cols(group)] for group in groups]
    extras = [extra_ref[index * STATE : (index + 1) * STATE, :] for index in range(PER_CHUNK)]
    combine_chunk(own_ref, got_ref, decays, extras, sent_ref)


def diagonal_chunk(chunk, conv_ref, key_ref, raw_queries_ref, edge_ref, decay_of, gain_ref, diagonal_ref, queries_ref):
    count = conv_ref.shape[0]
    edge_row = iota((count, 128), 0) < EDGE
    lane_head = iota((count, 128), 1) // HEAD_DIM

    def patched(tile, j):
        rows = jnp.concatenate(
            [edge_ref[:, j * 128 : (j + 1) * 128], jnp.zeros((count - 8, 128), f32)], axis=0
        )
        return jnp.where(edge_row, rows, tile.astype(f32))

    keys = patched(key_ref[...], VALUES // 128 + chunk).astype(bf16)
    j = (VALUES + GROUPED) // 128 + chunk
    queries = patched(raw_queries_ref[:, chunk * 128 : (chunk + 1) * 128], j).astype(bf16)
    queries_ref[...] = queries
    for index in range(PER_CHUNK):
        part = slice(index * STATE, (index + 1) * STATE)
        scores = dot(queries[:, part], keys[:, part], ((1,), (1,)))
        for i in range(WIDE // 128):
            at = index * WIDE + i * 128
            j = (chunk * HALF + at) // 128
            values = patched(conv_ref[:, at : at + 128], j)
            weights, parts = [], []
            for k in range(4):
                weights.append((decay_of(4 * j + k) * scores).astype(bf16))
                parts.append(jnp.where(lane_head == k, values, 0.0).astype(bf16))
            total = dot(jnp.concatenate(weights, axis=1), jnp.concatenate(parts, axis=0))
            diagonal_ref[:, at : at + 128] = total + gain_ref[:1, j * 128 : (j + 1) * 128] * values


def diagonal_first_kernel(
    conv_ref, key_ref, raw_queries_ref, edge_ref, decay_ref, gain_ref, own_scale_ref,
    diagonal_ref, queries_ref, extra_ref,
):
    keys = edge_ref[:, BC_GROUPS * WIDE :]
    for index in range(PER_CHUNK):
        group = PER_CHUNK + index
        cols = group_cols(group)
        extra_ref[index * STATE : (index + 1) * STATE, :] = edge_state(
            edge_ref[:, cols], keys, own_scale_ref[:, cols], group
        )
    diagonal_chunk(
        0, conv_ref, key_ref, raw_queries_ref, edge_ref, lambda at: decay_ref[at], gain_ref, diagonal_ref, queries_ref
    )


def diagonal_later_kernel(
    conv_ref, key_ref, raw_queries_ref, edge_ref, across_ref, down_ref, gain_ref, later_ref, table_ref, gates_ref,
    before_ref,
    diagonal_ref, queries_ref, known_ref, scale_ref, out_hbm, out_ref, sems,
):
    head_rows = later_ref[HEAD_AT : HEAD_AT + 16, :]
    known_ref[...] = known_part(head_rows.astype(f32), table_ref)
    scale_ref[...] = edge_scales(head_rows) * gates_ref[1:2, :1]
    causal = causal_mask(conv_ref.shape[0])
    diagonal_chunk(
        1, conv_ref, key_ref, raw_queries_ref, edge_ref,
        lambda at: token_decay(at, across_ref, down_ref, causal),
        gain_ref, diagonal_ref, queries_ref,
    )

    @pl.when(lax.axis_index("ctx") == 0)
    def _():
        copies = []
        for chunk, ref in enumerate((before_ref, diagonal_ref)):
            here = pl.ds(chunk * HALF, HALF)
            out_ref[:, here] = ref[...].astype(bf16)
            copies.append(pltpu.make_async_copy(out_ref.at[:, here], out_hbm.at[0, :, here], sems.at[chunk]))
            copies[-1].start()
        for copy in copies:
            copy.wait()


def group_out(group, total, diagonal_ref, queries_ref, entry_ref):
    index = group % PER_CHUNK
    here = slice(index * WIDE, (index + 1) * WIDE)
    carried = dot(queries_ref[:, index * STATE : (index + 1) * STATE], total.astype(bf16))
    return (diagonal_ref[:, here] + entry_ref[:, group_cols(group)] * carried).astype(bf16)


def finish_first_kernel(
    first0_ref, first1_ref, second_ref, early_ref, table_ref, known_ref, gates_ref, scale_ref, diagonal_ref,
    queries_ref, later_diagonal_ref, later_queries_ref, entry_ref, done_hbm,
    out_hbm, out_ref, base_ref, decay_ref, later_ref, sems,
):
    position = lax.axis_index("ctx")

    @pl.when(position > 0)
    def _():
        third = gates_ref[2:3, :] > 0.5
        kept = gates_ref[:1, :]

        def second_of(at, early_at, rows):
            a = second_ref[at : at + rows, :].astype(f32)
            return jnp.where(third, early_ref[early_at : early_at + rows, :].astype(f32), a)

        chunks = edge_rows(second_of(ROWS, 2 * ROWS, 16), known_ref[...], table_ref)
        for group in range(BC_GROUPS):
            chunk, index = divmod(group, PER_CHUNK)
            at = slice(index * STATE, (index + 1) * STATE)
            scale = scale_ref[:, group_cols(group)]
            decay = scale[EDGE : EDGE + 1]
            first = (first0_ref, first1_ref)[chunk][at, :].astype(f32)
            total = first * kept + edge_state(chunks[group], chunks[BC_GROUPS], scale, group)
            if chunk == 0:
                total = total + decay * second_of(index * STATE, index * STATE, STATE)
                out_ref[:, group_cols(group)] = group_out(group, total, diagonal_ref, queries_ref, entry_ref)
            else:
                early = early_ref[ROWS + index * STATE : ROWS + (index + 1) * STATE, :].astype(f32)
                base_ref[at, :] = jnp.where(third, total + decay * early, total)
                decay_ref[index * 8 : (index + 1) * 8, :] = jnp.where(third, 0.0, decay) + jnp.zeros((8, WIDE), f32)

    @pl.when((position > 0) & (position <= LAST_LOW))
    def _():
        copies = [
            pltpu.make_async_copy(out_ref, out_hbm.at[0, :, pl.ds(0, HALF)], sems.at[0]),
            pltpu.make_async_copy(later_ref, out_hbm.at[0, :, pl.ds(HALF, HALF)], sems.at[1]),
        ]
        copies[0].start()
        for index in range(PER_CHUNK):
            at = slice(index * STATE, (index + 1) * STATE)
            later_ref[:, index * WIDE : (index + 1) * WIDE] = group_out(
                PER_CHUNK + index, base_ref[at, :], later_diagonal_ref, later_queries_ref, entry_ref
            )
        copies[1].start()
        for copy in copies:
            copy.wait()


def finish_later_kernel(
    second_ref, base_ref, decay_ref, diagonal_ref, queries_ref, entry_ref, before_ref, done_hbm, out_hbm, out_ref, sems
):
    @pl.when(lax.axis_index("ctx") > LAST_LOW)
    def _():
        copies = [
            pltpu.make_async_copy(before_ref, out_hbm.at[0, :, pl.ds(0, HALF)], sems.at[PER_CHUNK])
        ]
        copies[0].start()
        for index in range(PER_CHUNK):
            group = PER_CHUNK + index
            at = slice(index * STATE, (index + 1) * STATE)
            decay = decay_ref[index * 8 : index * 8 + 1, :]
            total = base_ref[at, :] + decay * second_ref[at, :].astype(f32)
            here = pl.ds(index * WIDE, WIDE)
            out_ref[:, here] = group_out(group, total, diagonal_ref, queries_ref, entry_ref)
            copy = pltpu.make_async_copy(
                out_ref.at[:, here], out_hbm.at[0, :, pl.ds(group * WIDE, WIDE)], sems.at[index]
            )
            copy.start()
            copies.append(copy)
        for copy in copies:
            copy.wait()


def call(kernel, outs, in_specs, cost, args, out_specs=None, scratch=(), aliases={}):
    return pl.pallas_call(
        kernel,
        out_shape=outs,
        in_specs=in_specs,
        out_specs=out_specs or jax.tree.map(lambda _: VMEM, outs),
        scratch_shapes=scratch,
        input_output_aliases=aliases,
        compiler_params=pltpu.CompilerParams(vmem_limit_bytes=24 * 1024 * 1024),
        cost_estimate=pl.CostEstimate(flops=cost[0], bytes_accessed=cost[1], transcendentals=0),
    )(*args)


def permuted(array, edges):
    size, lanes = lax.axis_size("ctx"), lax.axis_size("lane")
    table = []
    for source in range(size):
        for lane in range(lanes):
            if source in edges:
                target = edges[source] * lanes + lane
            else:
                target = source * lanes + (lane + 1) % lanes
            table.append((source * lanes + lane, target))
    return lax.ppermute(array, ("ctx", "lane"), table)


def shard_near(pre_conv, step_size, lengths, conv_weight, conv_bias, decay_rate, skip_gain):
    count, channels = pre_conv.shape[1:]
    size = lax.axis_size("ctx")
    ring = [(i, (i + 1) % size) for i in range(size)]
    onward = {i: i + 2 for i in range(1, size - 2)}
    onward[size - 2] = 2
    onward[size - 1] = 1
    arguments = tuple(
        pltpu.with_memory_space_constraint(array, pltpu.HBM)
        for array in (
            lengths,
            pre_conv,
            step_size,
            conv_weight,
            conv_bias.reshape(-1, 128),
            decay_rate.reshape(1, -1),
            skip_gain.reshape(1, -1),
        )
    )
    sds = jax.ShapeDtypeStruct
    pads = pltpu.VMEM((PADS, count + 8, 128), f32)
    conv0, key0, cumulative, own0, x, weight, bias, step, skip, gates = call(
        first_kernel,
        (
            sds((count, HALF), bf16),
            sds((count, 128), bf16),
            sds((HEADS, count), f32),
            sds((SENT, WIDE), bf16),
            sds((count, channels), bf16),
            sds(conv_weight.shape, bf16),
            sds((channels // 128, 128), bf16),
            sds((HEADS, count), f32),
            sds((1, HEADS), f32),
            sds((8, WIDE), f32),
        ),
        [HBM] * 7,
        (40_000_000, 2_000_000),
        arguments,
        scratch=(
            pltpu.SMEM(lengths.shape, jnp.int32),
            pltpu.VMEM((1, HEADS), f32),
            pads,
            pltpu.SemaphoreType.DMA((7,)),
        ),
    )
    first0 = lax.ppermute(own0, "ctx", ring)
    conv1, key1, own1, early = call(
        later_kernel,
        (
            sds((count, HALF), bf16),
            sds((count, 128), bf16),
            sds((SENT, WIDE), bf16),
            sds((2 * ROWS + 16, WIDE), bf16),
        ),
        [VMEM] * 7,
        (40_000_000, 2_000_000),
        (x, weight, bias, step, cumulative, gates, own0),
        scratch=(pads,),
    )
    first1 = lax.ppermute(own1, "ctx", ring)
    early = permuted(early, {0: 2, 2: 0})
    raw_queries, table, known, scale, decay, across, down, entry, gain = call(
        prepare_kernel,
        (
            sds((count, GROUPED), bf16),
            sds((7, 16, WIDE), f32),
            sds((16, WIDE), f32),
            sds((8, VALUES), f32),
            sds((HEADS // CHUNKS, count, count), f32),
            sds((HEADS, count), f32),
            sds((count, HEADS), f32),
            sds((count, VALUES), f32),
            sds((8, VALUES), f32),
        ),
        [VMEM] * 8,
        (100_000_000, 1_000_000),
        (own1, x, weight, bias, cumulative, step, skip, gates),
        scratch=(pads,),
    )
    sent0, edge = call(
        combine_first_kernel,
        (sds((ROWS + 16, WIDE), bf16), sds((8, channels), f32)),
        [VMEM] * 6,
        (1_000_000, 1_000_000),
        (own0, first0, table, known, gates, scale),
    )
    second0 = permuted(sent0, onward)
    diagonal_outs = (sds((count, HALF), f32), sds((count, 128), bf16))
    diagonal0, queries0, extra = call(
        diagonal_first_kernel,
        diagonal_outs + (sds((ROWS, WIDE), f32),),
        [VMEM] * 7,
        (200_000_000, 2_000_000),
        (conv0, key0, raw_queries, edge, decay, gain, scale),
    )
    sent1 = call(
        combine_later_kernel,
        sds((ROWS, WIDE), bf16),
        [VMEM] * 4,
        (1_000_000, 1_000_000),
        (own1, first1, scale, extra),
    )
    second1 = permuted(sent1, onward)
    out_shape = sds((1, count, VALUES), bf16)
    diagonal1, queries1, known, scale, out = call(
        diagonal_later_kernel,
        diagonal_outs + (sds((16, WIDE), f32), sds((8, VALUES), f32), out_shape),
        [VMEM] * 11,
        (200_000_000, 2_000_000),
        (conv1, key1, raw_queries, edge, across, down, gain, first1, table, gates, diagonal0),
        out_specs=(VMEM, VMEM, VMEM, VMEM, HBM),
        scratch=(pltpu.VMEM((count, VALUES), bf16), pltpu.SemaphoreType.DMA((CHUNKS,))),
    )
    out, out0, base, decay = call(
        finish_first_kernel,
        (
            out_shape,
            sds((count, HALF), bf16),
            sds((ROWS, WIDE), f32),
            sds((8 * PER_CHUNK, WIDE), f32),
        ),
        [VMEM] * 13 + [HBM],
        (50_000_000, 2_000_000),
        (
            first0, first1, second0, early, table, known, gates, scale,
            diagonal0, queries0, diagonal1, queries1, entry, out,
        ),
        out_specs=(HBM, VMEM, VMEM, VMEM),
        scratch=(pltpu.VMEM((count, HALF), bf16), pltpu.SemaphoreType.DMA((2,))),
        aliases={13: 0},
    )
    return call(
        finish_later_kernel,
        out_shape,
        [VMEM] * 7 + [HBM],
        (50_000_000, 2_000_000),
        (second1, base, decay, diagonal1, queries1, entry, out0, out),
        out_specs=HBM,
        scratch=(pltpu.VMEM((count, HALF), bf16), pltpu.SemaphoreType.DMA((PER_CHUNK + 1,))),
        aliases={7: 0},
    )


def shifted(value, axis, steps):
    count = lax.axis_size(axis)
    first, last = (max(0, -steps), min(count, count - steps))
    return lax.ppermute(value, axis, [(source, source + steps) for source in range(first, last)])


def carried_in(array, axis, combine, identity):
    length, index = (lax.axis_size(axis), lax.axis_index(axis))
    everything = jax.tree.map(
        lambda part, kind: lax.all_gather(part.astype(kind), axis),
        array,
        (jnp.bfloat16, jnp.bfloat16),
    )
    start = jax.tree.map(
        lambda part, zero: jnp.broadcast_to(jnp.asarray(zero, part.dtype), part.shape),
        array,
        identity,
    )

    def step(k, before):
        reached = k < index
        new = combine(
            before, jax.tree.map(lambda part, own: part[k].astype(own.dtype), everything, array)
        )
        return jax.tree.map(lambda a, b: jnp.where(reached, a, b), new, before)

    return lax.fori_loop(0, length, step, start)


def convolve(padded, conv_weight, conv_bias, count_rows):
    total = conv_bias.astype(jnp.float32)[None, :]
    for offset in range(conv_weight.shape[0]):
        total = (
            total
            + padded[offset : offset + count_rows].astype(jnp.float32)
            * conv_weight[offset].astype(jnp.float32)[None, :]
        )
    return jax.nn.silu(total).astype(jnp.bfloat16)


def group_terms(values, keys_in, queries, decay_rate, step_rows):
    heads_group = step_rows.shape[0]
    count_rows = step_rows.shape[1]
    values = values.reshape(count_rows, heads_group, -1)
    cumulative = jnp.cumsum(-step_rows * decay_rate[:, None], axis=1)
    scores = jnp.einsum("tn,sn->ts", queries, keys_in, preferred_element_type=jnp.float32)
    later = lax.broadcasted_iota(jnp.int32, (count_rows, count_rows), 0)
    earlier = lax.broadcasted_iota(jnp.int32, (count_rows, count_rows), 1)
    spread = jnp.where(
        (later >= earlier)[None], cumulative[:, :, None] - cumulative[:, None, :], -1e30
    )
    weights = (jnp.exp(spread) * scores[None]).astype(jnp.bfloat16)
    scaled = (values * step_rows.T[:, :, None]).astype(jnp.bfloat16)
    diagonal_part = jnp.einsum("hts,shp->thp", weights, scaled, preferred_element_type=jnp.float32)
    tail_weight = jnp.exp(cumulative[:, -1:] - cumulative)
    written = (values * (step_rows * tail_weight).T[:, :, None]).astype(jnp.bfloat16)
    local_state = jnp.einsum("tn,thp->hpn", keys_in, written, preferred_element_type=jnp.float32)
    return (diagonal_part, local_state, jnp.exp(cumulative[:, -1]), jnp.exp(cumulative), values)


def finish_group(diagonal_part, entry_decay, queries, incoming, values, skip_gain):
    incoming_rounded = incoming.astype(jnp.bfloat16)
    carried_part = jnp.einsum(
        "tn,hpn->thp", queries, incoming_rounded, preferred_element_type=jnp.float32
    )
    carried_part = carried_part * entry_decay.T[:, :, None]
    return diagonal_part + carried_part + skip_gain[None, :, None] * values.astype(jnp.float32)


def combine(earlier, later):
    return (earlier[0] * later[0], later[0][:, None, None] * earlier[1] + later[1])


def shard_far(pre_conv, step_size, lengths, conv_weight, conv_bias, decay_rate, skip_gain):
    count_rows = pre_conv.shape[1]
    kernel_len = conv_weight.shape[0]
    heads_group = HEADS // BC_GROUPS
    position = lax.axis_index("ctx")
    sizes_row = lengths[0]
    starts = jnp.cumsum(sizes_row) - sizes_row
    fresh = jnp.any(starts == position)
    retain = jnp.where(fresh, 0.0, 1.0).astype(jnp.float32)
    own_rows = pre_conv[0]
    previous = shifted(own_rows[count_rows - kernel_len + 1 :], "ctx", 1)
    previous = jnp.where(fresh, jnp.zeros_like(previous), previous)
    convolved = convolve(
        jnp.concatenate([previous, own_rows], axis=0), conv_weight, conv_bias, count_rows
    )
    values = convolved[:, : HEADS * HEAD_DIM]
    keys_all = convolved[:, HEADS * HEAD_DIM : HEADS * HEAD_DIM + BC_GROUPS * STATE]
    queries_all = convolved[:, HEADS * HEAD_DIM + BC_GROUPS * STATE :]
    step_rows = step_size[0]
    results = []
    pieces = []
    for bc_group in range(BC_GROUPS):
        low = bc_group * heads_group
        high = low + heads_group
        pieces.append(
            group_terms(
                values[:, low * HEAD_DIM : high * HEAD_DIM],
                keys_all[:, bc_group * STATE : (bc_group + 1) * STATE],
                queries_all[:, bc_group * STATE : (bc_group + 1) * STATE],
                decay_rate[low:high],
                step_rows[low:high],
            )
        )
    decays = jnp.concatenate([piece[2] for piece in pieces], axis=0) * retain
    states = jnp.concatenate([piece[1] for piece in pieces], axis=0)
    identity = (jnp.ones_like(decays), jnp.zeros_like(states))
    totals = carried_in((decays, states), "ctx", combine, identity)
    incoming = totals[1] * retain
    for bc_group in range(BC_GROUPS):
        low = bc_group * heads_group
        high = low + heads_group
        piece = pieces[bc_group]
        results.append(
            finish_group(
                piece[0],
                piece[3],
                queries_all[:, bc_group * STATE : (bc_group + 1) * STATE],
                incoming[low:high],
                piece[4],
                skip_gain[low:high],
            )
        )
    output = (
        jnp.concatenate(results, axis=1).reshape(count_rows, HEADS * HEAD_DIM).astype(jnp.bfloat16)
    )
    return output[None]


def solution(mesh):
    in_specs = (
        P(("groups", "lane"), "ctx", None),
        P(("groups", "lane"), None, "ctx"),
        P(("groups", "lane"), None),
        P(),
        P(),
        P(),
        P(),
    )
    out_specs = P(("groups", "lane"), "ctx", None)
    shards = shard_near if mesh.shape["ctx"] <= 8 else shard_far
    return jax.shard_map(shards, mesh=mesh, in_specs=in_specs, out_specs=out_specs, check_vma=False)
```

```python
import jax
import jax.numpy as jnp
from jax import lax
from jax.experimental import pallas as pl
from jax.experimental.pallas import tpu as pltpu
from jax.sharding import PartitionSpec as P

HEADS = 64
HEAD_DIM = 32
EDGE = 3
STATE = 64
BC_GROUPS = 4
HEADS_GROUP = HEADS // BC_GROUPS
VALUES = HEADS * HEAD_DIM
WIDE = HEADS_GROUP * HEAD_DIM
GROUPED = BC_GROUPS * STATE
CHUNKS = 2
PADS = 4
ORDER = (0, 1, 2, 5, 3, 4, 6)
PER_CHUNK = BC_GROUPS // CHUNKS
HALF = PER_CHUNK * WIDE
ROWS = PER_CHUNK * STATE
TAIL_AT = ROWS
HEAD_AT = ROWS
SENT = ROWS + 16
LAST_LOW = 2
LOG2E = 1.4426950408889634
VMEM = pl.BlockSpec(memory_space=pltpu.VMEM)
HBM = pl.BlockSpec(memory_space=pltpu.HBM)
f32 = jnp.float32
bf16 = jnp.bfloat16


def iota(shape, dim):
    return lax.broadcasted_iota(jnp.int32, shape, dim)


def dot(a, b, contract=((1,), (0,))):
    return lax.dot_general(a, b, (contract, ((), ())), preferred_element_type=f32)


def is_fresh(lengths_ref, position):
    found = jnp.int32(0)
    start = jnp.int32(0)
    for k in range(lengths_ref.shape[1]):
        found = jnp.where(start == position, jnp.int32(1), found)
        start = start + lengths_ref[0, k]
    return found


def halves(value):
    high = value.astype(bf16)
    return high, (value - high.astype(f32)).astype(bf16)


def cumulative_of(step, rate_row):
    eye = iota((HEADS, HEADS), 0) == iota((HEADS, HEADS), 1)
    rate = jnp.sum(jnp.where(eye, rate_row, 0.0), axis=1, keepdims=True)
    tokens = step.shape[1]
    upto = iota((tokens, tokens), 0) <= iota((tokens, tokens), 1)
    upto = upto.astype(bf16)
    rest = -step * rate
    total = jnp.zeros_like(rest)
    for _ in range(3):
        part = rest.astype(bf16)
        rest = rest - part.astype(f32)
        total = total + dot(part, upto)
    return total


def spread_matrix():
    rows, lanes = 2 * HEADS_GROUP, WIDE
    return (iota((rows, lanes), 0) % HEADS_GROUP == iota((rows, lanes), 1) // HEAD_DIM).astype(bf16)


def spread(per_head, group, matrix):
    part = per_head[group * HEADS_GROUP : (group + 1) * HEADS_GROUP]
    return dot(jnp.concatenate(halves(part), axis=0), matrix, ((0,), (0,)))


def half_silu(half):
    return half + half * jnp.tanh(half)


def to_rows(strip, first):
    rows = iota((8, WIDE), 0)
    top = jnp.zeros((8, WIDE), f32)
    low = jnp.zeros((8, WIDE), f32)
    for k in range(strip.shape[1] // WIDE):
        moved = pltpu.roll(strip[:, k * WIDE : (k + 1) * WIDE], (3 * k - first) % 8, 0)
        if 3 * k < 8:
            top = jnp.where((rows >= 3 * k) & (rows < 3 * k + 3), moved, top)
        if 3 * k + 2 >= 8:
            low = jnp.where((rows >= 3 * k - 8) & (rows < 3 * k - 5), moved, low)
    return jnp.concatenate([top, low], axis=0)


def conv_rows(x, weight, bias, pad_ref):
    count = x.shape[0]
    pad_ref[8 : 8 + count, :] = x
    total = bias + x * weight[3:4]
    for back in range(1, 4):
        total = total + pad_ref[8 - back : 8 - back + count, :] * weight[3 - back : 4 - back]
    return half_silu(total)


def clear(pads_ref):
    for slot in range(PADS):
        pads_ref[slot, :8, :] = jnp.zeros((8, 128), f32)


def half_taps(weight_ref, bias_ref):
    return weight_ref[...].astype(f32) * 0.5, bias_ref[...].astype(f32) * 0.5


def chunk_states(chunk, x_ref, weight, bias, kept, conv_ref, key_ref, sent_ref, pads_ref):
    matrix = spread_matrix()
    clear(pads_ref)

    def conv_tile(j):
        cols = slice(j * 128, (j + 1) * 128)
        return conv_rows(x_ref[:, cols].astype(f32), weight[:, cols], bias[j : j + 1], pads_ref.at[j % PADS])

    key = conv_tile(VALUES // 128 + chunk).astype(bf16)
    key_ref[...] = key
    for index in range(PER_CHUNK):
        group = chunk * PER_CHUNK + index
        scale = spread(kept, group, matrix)
        parts = []
        for i in range(WIDE // 128):
            local = index * WIDE + i * 128
            tile = conv_tile((chunk * HALF + local) // 128)
            conv_ref[:, local : local + 128] = tile.astype(bf16)
            parts.append((tile * scale[:, i * 128 : (i + 1) * 128]).astype(bf16))
        state = dot(
            key[:, index * STATE : (index + 1) * STATE], jnp.concatenate(parts, axis=1), ((0,), (0,))
        )
        sent_ref[index * STATE : (index + 1) * STATE, :] = state.astype(bf16)


def kept_weights(step, cumulative, goes_on):
    count = step.shape[1]
    last = cumulative[:, count - 1 :]
    tail = step * jnp.exp(last - cumulative)
    lanes = iota((HEADS, count), 1)
    kept = jnp.where((lanes >= EDGE) | (goes_on < 0.5), tail, 0.0)
    return kept, jnp.where(lanes == EDGE, jnp.exp(last), tail)


def first_kernel(
    lengths_hbm, x_hbm, step_hbm, weight_hbm, bias_hbm, rate_hbm, skip_hbm,
    conv_ref, key_ref, cumulative_ref, sent_ref, x_ref, weight_ref, bias_ref, step_ref, skip_ref, gates_ref,
    lengths_ref, rate_ref, pads_ref, sems,
):
    count = x_ref.shape[0]
    pairs = [
        (step_hbm.at[0], step_ref),
        (rate_hbm, rate_ref),
        (lengths_hbm, lengths_ref),
        (weight_hbm, weight_ref),
        (bias_hbm, bias_ref),
        (x_hbm.at[0], x_ref),
        (skip_hbm, skip_ref),
    ]
    copies = [pltpu.make_async_copy(a, b, sems.at[i]) for i, (a, b) in enumerate(pairs)]
    for i in ORDER:
        copies[i].start()
    for copy in copies[:3]:
        copy.wait()
    position = lax.axis_index("ctx")
    fresh = is_fresh(lengths_ref, position)
    goes_on = (1 - fresh).astype(f32)
    both = goes_on * (1 - is_fresh(lengths_ref, position - 1)).astype(f32)
    third = jnp.where(position == 2, 1.0, 0.0).astype(f32)
    rows = iota((8, WIDE), 0)
    gates_ref[...] = jnp.where(rows == 0, goes_on, jnp.where(rows == 1, both, third))
    step = step_ref[...]
    cumulative = cumulative_of(step, rate_ref[...])
    cumulative_ref[...] = cumulative
    kept = kept_weights(step, cumulative, goes_on)[0]
    for copy in copies[3:6]:
        copy.wait()
    weight, bias = half_taps(weight_ref, bias_ref)
    chunk_states(
        0,
        x_ref, weight, bias, kept, conv_ref, key_ref, sent_ref, pads_ref,
    )
    tail_rows = to_rows(x_ref[count - 16 :, :].astype(f32)[8:], 5)
    sent_ref[TAIL_AT : TAIL_AT + 16, :] = tail_rows.astype(bf16)
    copies[6].wait()


def later_kernel(
    x_ref, weight_ref, bias_ref, step_ref, cumulative_ref, gates_ref, before_ref,
    conv_ref, key_ref, sent_ref, early_ref, pads_ref,
):
    weight, bias = half_taps(weight_ref, bias_ref)
    kept, scales = kept_weights(step_ref[...], cumulative_ref[...], gates_ref[:1, :1])
    chunk_states(1, x_ref, weight, bias, kept, conv_ref, key_ref, sent_ref, pads_ref)
    high, low = halves(scales)
    place = iota((HEADS, 128), 1) - iota((HEADS, 128), 0)
    picked = dot(high, (place == 0).astype(bf16), ((0,), (0,)))
    picked = picked + dot(low, (place == HEADS).astype(bf16), ((0,), (0,)))
    line = jnp.concatenate([picked[k : k + 1] for k in range(4)], axis=1)
    head_rows = to_rows(x_ref[:16, :].astype(f32)[:8], 0)
    head_rows = jnp.where(iota((16, WIDE), 0) == 15, line, head_rows)
    sent_ref[HEAD_AT : HEAD_AT + 16, :] = head_rows.astype(bf16)
    early_ref[:ROWS, :] = before_ref[:ROWS, :]
    early_ref[ROWS : 2 * ROWS, :] = sent_ref[:ROWS, :]
    early_ref[2 * ROWS :, :] = before_ref[TAIL_AT : TAIL_AT + 16, :]


def known_part(head_block, table_ref):
    return (
        table_ref[0]
        + head_block * table_ref[1]
        + pltpu.roll(head_block, 1, 0) * table_ref[2]
        + pltpu.roll(head_block, 2, 0) * table_ref[3]
    )


def edge_rows(tail_block, known, table_ref):
    block = half_silu(
        known
        + tail_block * table_ref[4]
        + pltpu.roll(tail_block, 15, 0) * table_ref[5]
        + pltpu.roll(tail_block, 14, 0) * table_ref[6]
    )
    return [pltpu.roll(block, (16 - 3 * k) % 16, 0)[:8] for k in range(5)]


def head_lanes(rows):
    lanes = iota((128, VALUES), 1) // HEAD_DIM
    matrix = (iota((128, VALUES), 0) % HEADS == lanes).astype(bf16)
    return dot(rows, matrix)[:8]


def edge_scales(head_rows):
    line = head_rows[15:16].astype(f32)
    rows = [line[:, k * 128 : (k + 1) * 128] for k in range(4)]
    return head_lanes(jnp.concatenate(rows + [jnp.zeros((12, 128), f32)], axis=0).astype(bf16))


def causal_mask(count):
    return iota((count, count), 0) >= iota((count, count), 1)


def token_decay(at, across_ref, down_ref, causal):
    gap = down_ref[:, at : at + 1] - across_ref[at : at + 1, :]
    return jnp.exp2(jnp.where(causal, gap, -1e30))


def prepare_kernel(
    later_ref, x_ref, weight_ref, bias_ref, cumulative_ref, step_ref, skip_ref, gates_ref,
    queries_ref, table_ref, known_ref, scale_ref, across_ref, down_ref, entry_ref, gain_ref, pads_ref,
):
    clear(pads_ref)
    weight, bias = half_taps(weight_ref, bias_ref)
    rows = iota((16, WIDE), 0)
    third = rows % 3
    chunk = rows // 3

    def blocked(lines):
        out = jnp.zeros((16, WIDE), f32)
        for k in range(5):
            out = jnp.where(chunk == k, lines[k], out)
        return out

    taps = [
        blocked([weight[tap : tap + 1, k * WIDE : (k + 1) * WIDE] for k in range(5)])
        for tap in range(4)
    ]
    table_ref[0] = blocked(
        [
            jnp.concatenate([bias[4 * k + i : 4 * k + i + 1, :] for i in range(4)], axis=1)
            for k in range(5)
        ]
    )
    table_ref[1] = taps[3]
    table_ref[2] = jnp.where(third == 0, 0.0, taps[2])
    table_ref[3] = jnp.where(third == 2, taps[1], 0.0)
    table_ref[4] = taps[0]
    table_ref[5] = jnp.where(third == 2, 0.0, taps[1])
    table_ref[6] = jnp.where(third == 0, taps[2], 0.0)
    known_ref[...] = known_part(later_ref[HEAD_AT : HEAD_AT + 16, :].astype(f32), table_ref)
    scale_ref[...] = edge_scales(later_ref[HEAD_AT : HEAD_AT + 16, :]) * gates_ref[:1, :1]
    cumulative = cumulative_ref[...] * LOG2E
    across_ref[...] = cumulative - jnp.log2(step_ref[...])
    down_ref[...] = cumulative.T
    matrix = spread_matrix()
    entry = jnp.exp2(cumulative)
    for group in range(BC_GROUPS):
        entry_ref[:, group * WIDE : (group + 1) * WIDE] = spread(entry, group, matrix)
    gain_ref[...] = head_lanes(
        jnp.concatenate(halves(skip_ref[...] + jnp.zeros((16, HEADS), f32)), axis=1)
    )
    first = VALUES + GROUPED
    for i in range(2):
        cols = slice(first + i * 128, first + (i + 1) * 128)
        j = first // 128 + i
        tile = conv_rows(
            x_ref[:, cols].astype(f32), weight[:, cols], bias[j : j + 1, :], pads_ref.at[i]
        )
        queries_ref[:, i * 128 : (i + 1) * 128] = tile.astype(bf16)


def edge_state(values_rows, keys_rows, scale, group):
    rows = iota((8, WIDE), 0)
    written = jnp.where(rows < EDGE, values_rows * scale, 0.0)
    tile = keys_rows[:, (group // 2) * 128 : (group // 2 + 1) * 128].astype(bf16)
    return dot(tile[:, (group % 2) * STATE : (group % 2 + 1) * STATE], written.astype(bf16), ((0,), (0,)))


def combine_chunk(own_ref, got_ref, decays, extras, sent_ref):
    for index in range(PER_CHUNK):
        at = slice(index * STATE, (index + 1) * STATE)
        total = own_ref[at, :].astype(f32) + extras[index] + decays[index] * got_ref[at, :].astype(f32)
        sent_ref[at, :] = total.astype(bf16)


def group_cols(group):
    return slice(group * WIDE, (group + 1) * WIDE)


def combine_first_kernel(own_ref, got_ref, table_ref, known_ref, gates_ref, scale_ref, sent_ref, edge_ref):
    tail_block = got_ref[TAIL_AT : TAIL_AT + 16, :].astype(f32) * gates_ref[:1, :]
    chunks = edge_rows(tail_block, known_ref[...], table_ref)
    scales = [scale_ref[:, group_cols(group)] for group in range(PER_CHUNK)]
    extras = [edge_state(chunks[g], chunks[BC_GROUPS], scales[g], g) for g in range(PER_CHUNK)]
    decays = [scale[EDGE : EDGE + 1] for scale in scales]
    combine_chunk(own_ref, got_ref, decays, extras, sent_ref)
    sent_ref[ROWS:, :] = own_ref[TAIL_AT : TAIL_AT + 16, :]
    for k in range(5):
        edge_ref[:, k * WIDE : (k + 1) * WIDE] = chunks[k]


def combine_later_kernel(own_ref, got_ref, scale_ref, extra_ref, sent_ref):
    groups = range(PER_CHUNK, BC_GROUPS)
    decays = [scale_ref[EDGE : EDGE + 1, group_cols(group)] for group in groups]
    extras = [extra_ref[index * STATE : (index + 1) * STATE, :] for index in range(PER_CHUNK)]
    combine_chunk(own_ref, got_ref, decays, extras, sent_ref)


def diagonal_chunk(chunk, conv_ref, key_ref, raw_queries_ref, edge_ref, decay_of, gain_ref, diagonal_ref, queries_ref):
    count = conv_ref.shape[0]
    edge_row = iota((count, 128), 0) < EDGE
    lane_head = iota((count, 128), 1) // HEAD_DIM

    def patched(tile, j):
        rows = jnp.concatenate(
            [edge_ref[:, j * 128 : (j + 1) * 128], jnp.zeros((count - 8, 128), f32)], axis=0
        )
        return jnp.where(edge_row, rows, tile.astype(f32))

    keys = patched(key_ref[...], VALUES // 128 + chunk).astype(bf16)
    j = (VALUES + GROUPED) // 128 + chunk
    queries = patched(raw_queries_ref[:, chunk * 128 : (chunk + 1) * 128], j).astype(bf16)
    queries_ref[...] = queries
    for index in range(PER_CHUNK):
        part = slice(index * STATE, (index + 1) * STATE)
        scores = dot(queries[:, part], keys[:, part], ((1,), (1,)))
        for i in range(WIDE // 128):
            at = index * WIDE + i * 128
            j = (chunk * HALF + at) // 128
            values = patched(conv_ref[:, at : at + 128], j)
            weights, parts = [], []
            for k in range(4):
                weights.append((decay_of(4 * j + k) * scores).astype(bf16))
                parts.append(jnp.where(lane_head == k, values, 0.0).astype(bf16))
            total = dot(jnp.concatenate(weights, axis=1), jnp.concatenate(parts, axis=0))
            diagonal_ref[:, at : at + 128] = total + gain_ref[:1, j * 128 : (j + 1) * 128] * values


def diagonal_first_kernel(
    conv_ref, key_ref, raw_queries_ref, edge_ref, across_ref, down_ref, gain_ref, own_scale_ref,
    diagonal_ref, queries_ref, extra_ref,
):
    keys = edge_ref[:, BC_GROUPS * WIDE :]
    for index in range(PER_CHUNK):
        group = PER_CHUNK + index
        cols = group_cols(group)
        extra_ref[index * STATE : (index + 1) * STATE, :] = edge_state(
            edge_ref[:, cols], keys, own_scale_ref[:, cols], group
        )
    causal = causal_mask(conv_ref.shape[0])
    diagonal_chunk(
        0, conv_ref, key_ref, raw_queries_ref, edge_ref,
        lambda at: token_decay(at, across_ref, down_ref, causal),
        gain_ref, diagonal_ref, queries_ref,
    )


def diagonal_later_kernel(
    conv_ref, key_ref, raw_queries_ref, edge_ref, across_ref, down_ref, gain_ref, later_ref, table_ref, gates_ref,
    before_ref,
    diagonal_ref, queries_ref, known_ref, scale_ref, out_hbm, out_ref, sems,
):
    head_rows = later_ref[HEAD_AT : HEAD_AT + 16, :]
    known_ref[...] = known_part(head_rows.astype(f32), table_ref)
    scale_ref[...] = edge_scales(head_rows) * gates_ref[1:2, :1]
    causal = causal_mask(conv_ref.shape[0])
    diagonal_chunk(
        1, conv_ref, key_ref, raw_queries_ref, edge_ref,
        lambda at: token_decay(at, across_ref, down_ref, causal),
        gain_ref, diagonal_ref, queries_ref,
    )

    @pl.when(lax.axis_index("ctx") == 0)
    def _():
        copies = []
        for chunk, ref in enumerate((before_ref, diagonal_ref)):
            here = pl.ds(chunk * HALF, HALF)
            out_ref[:, here] = ref[...].astype(bf16)
            copies.append(pltpu.make_async_copy(out_ref.at[:, here], out_hbm.at[0, :, here], sems.at[chunk]))
            copies[-1].start()
        for copy in copies:
            copy.wait()


def group_out(group, total, diagonal_ref, queries_ref, entry_ref):
    index = group % PER_CHUNK
    here = slice(index * WIDE, (index + 1) * WIDE)
    carried = dot(queries_ref[:, index * STATE : (index + 1) * STATE], total.astype(bf16))
    return (diagonal_ref[:, here] + entry_ref[:, group_cols(group)] * carried).astype(bf16)


def finish_first_kernel(
    first0_ref, first1_ref, second_ref, early_ref, table_ref, known_ref, gates_ref, scale_ref, diagonal_ref,
    queries_ref, later_diagonal_ref, later_queries_ref, entry_ref, done_hbm,
    out_hbm, out_ref, base_ref, decay_ref, later_ref, sems,
):
    position = lax.axis_index("ctx")

    @pl.when(position > 0)
    def _():
        third = gates_ref[2:3, :] > 0.5
        kept = gates_ref[:1, :]

        def second_of(at, early_at, rows):
            a = second_ref[at : at + rows, :].astype(f32)
            return jnp.where(third, early_ref[early_at : early_at + rows, :].astype(f32), a)

        chunks = edge_rows(second_of(ROWS, 2 * ROWS, 16), known_ref[...], table_ref)
        for group in range(BC_GROUPS):
            chunk, index = divmod(group, PER_CHUNK)
            at = slice(index * STATE, (index + 1) * STATE)
            scale = scale_ref[:, group_cols(group)]
            decay = scale[EDGE : EDGE + 1]
            first = (first0_ref, first1_ref)[chunk][at, :].astype(f32)
            total = first * kept + edge_state(chunks[group], chunks[BC_GROUPS], scale, group)
            if chunk == 0:
                total = total + decay * second_of(index * STATE, index * STATE, STATE)
                out_ref[:, group_cols(group)] = group_out(group, total, diagonal_ref, queries_ref, entry_ref)
            else:
                early = early_ref[ROWS + index * STATE : ROWS + (index + 1) * STATE, :].astype(f32)
                base_ref[at, :] = jnp.where(third, total + decay * early, total)
                decay_ref[index * 8 : (index + 1) * 8, :] = jnp.where(third, 0.0, decay) + jnp.zeros((8, WIDE), f32)

    @pl.when((position > 0) & (position <= LAST_LOW))
    def _():
        copies = [
            pltpu.make_async_copy(out_ref, out_hbm.at[0, :, pl.ds(0, HALF)], sems.at[0]),
            pltpu.make_async_copy(later_ref, out_hbm.at[0, :, pl.ds(HALF, HALF)], sems.at[1]),
        ]
        copies[0].start()
        for index in range(PER_CHUNK):
            at = slice(index * STATE, (index + 1) * STATE)
            later_ref[:, index * WIDE : (index + 1) * WIDE] = group_out(
                PER_CHUNK + index, base_ref[at, :], later_diagonal_ref, later_queries_ref, entry_ref
            )
        copies[1].start()
        for copy in copies:
            copy.wait()


def finish_later_kernel(
    second_ref, base_ref, decay_ref, diagonal_ref, queries_ref, entry_ref, before_ref, done_hbm, out_hbm, out_ref, sems
):
    @pl.when(lax.axis_index("ctx") > LAST_LOW)
    def _():
        copies = [
            pltpu.make_async_copy(before_ref, out_hbm.at[0, :, pl.ds(0, HALF)], sems.at[PER_CHUNK])
        ]
        copies[0].start()
        for index in range(PER_CHUNK):
            group = PER_CHUNK + index
            at = slice(index * STATE, (index + 1) * STATE)
            decay = decay_ref[index * 8 : index * 8 + 1, :]
            total = base_ref[at, :] + decay * second_ref[at, :].astype(f32)
            here = pl.ds(index * WIDE, WIDE)
            out_ref[:, here] = group_out(group, total, diagonal_ref, queries_ref, entry_ref)
            copy = pltpu.make_async_copy(
                out_ref.at[:, here], out_hbm.at[0, :, pl.ds(group * WIDE, WIDE)], sems.at[index]
            )
            copy.start()
            copies.append(copy)
        for copy in copies:
            copy.wait()


def call(kernel, outs, in_specs, cost, args, out_specs=None, scratch=(), aliases={}):
    return pl.pallas_call(
        kernel,
        out_shape=outs,
        in_specs=in_specs,
        out_specs=out_specs or jax.tree.map(lambda _: VMEM, outs),
        scratch_shapes=scratch,
        input_output_aliases=aliases,
        compiler_params=pltpu.CompilerParams(vmem_limit_bytes=24 * 1024 * 1024),
        cost_estimate=pl.CostEstimate(flops=cost[0], bytes_accessed=cost[1], transcendentals=0),
    )(*args)


def permuted(array, edges):
    size, lanes = lax.axis_size("ctx"), lax.axis_size("lane")
    table = []
    for source in range(size):
        for lane in range(lanes):
            if source in edges:
                target = edges[source] * lanes + lane
            else:
                target = source * lanes + (lane + 1) % lanes
            table.append((source * lanes + lane, target))
    return lax.ppermute(array, ("ctx", "lane"), table)


def shard_near(pre_conv, step_size, lengths, conv_weight, conv_bias, decay_rate, skip_gain):
    count, channels = pre_conv.shape[1:]
    size = lax.axis_size("ctx")
    ring = [(i, (i + 1) % size) for i in range(size)]
    onward = {i: i + 2 for i in range(1, size - 2)}
    onward[size - 2] = 2
    onward[size - 1] = 1
    arguments = tuple(
        pltpu.with_memory_space_constraint(array, pltpu.HBM)
        for array in (
            lengths,
            pre_conv,
            step_size,
            conv_weight,
            conv_bias.reshape(-1, 128),
            decay_rate.reshape(1, -1),
            skip_gain.reshape(1, -1),
        )
    )
    sds = jax.ShapeDtypeStruct
    pads = pltpu.VMEM((PADS, count + 8, 128), f32)
    conv0, key0, cumulative, own0, x, weight, bias, step, skip, gates = call(
        first_kernel,
        (
            sds((count, HALF), bf16),
            sds((count, 128), bf16),
            sds((HEADS, count), f32),
            sds((SENT, WIDE), bf16),
            sds((count, channels), bf16),
            sds(conv_weight.shape, bf16),
            sds((channels // 128, 128), bf16),
            sds((HEADS, count), f32),
            sds((1, HEADS), f32),
            sds((8, WIDE), f32),
        ),
        [HBM] * 7,
        (40_000_000, 2_000_000),
        arguments,
        scratch=(
            pltpu.SMEM(lengths.shape, jnp.int32),
            pltpu.VMEM((1, HEADS), f32),
            pads,
            pltpu.SemaphoreType.DMA((7,)),
        ),
    )
    first0 = lax.ppermute(own0, "ctx", ring)
    conv1, key1, own1, early = call(
        later_kernel,
        (
            sds((count, HALF), bf16),
            sds((count, 128), bf16),
            sds((SENT, WIDE), bf16),
            sds((2 * ROWS + 16, WIDE), bf16),
        ),
        [VMEM] * 7,
        (40_000_000, 2_000_000),
        (x, weight, bias, step, cumulative, gates, own0),
        scratch=(pads,),
    )
    first1 = lax.ppermute(own1, "ctx", ring)
    early = permuted(early, {0: 2, 2: 0})
    raw_queries, table, known, scale, across, down, entry, gain = call(
        prepare_kernel,
        (
            sds((count, GROUPED), bf16),
            sds((7, 16, WIDE), f32),
            sds((16, WIDE), f32),
            sds((8, VALUES), f32),
            sds((HEADS, count), f32),
            sds((count, HEADS), f32),
            sds((count, VALUES), f32),
            sds((8, VALUES), f32),
        ),
        [VMEM] * 8,
        (100_000_000, 1_000_000),
        (own1, x, weight, bias, cumulative, step, skip, gates),
        scratch=(pads,),
    )
    sent0, edge = call(
        combine_first_kernel,
        (sds((ROWS + 16, WIDE), bf16), sds((8, channels), f32)),
        [VMEM] * 6,
        (1_000_000, 1_000_000),
        (own0, first0, table, known, gates, scale),
    )
    second0 = permuted(sent0, onward)
    diagonal_outs = (sds((count, HALF), f32), sds((count, 128), bf16))
    diagonal0, queries0, extra = call(
        diagonal_first_kernel,
        diagonal_outs + (sds((ROWS, WIDE), f32),),
        [VMEM] * 8,
        (200_000_000, 2_000_000),
        (conv0, key0, raw_queries, edge, across, down, gain, scale),
    )
    sent1 = call(
        combine_later_kernel,
        sds((ROWS, WIDE), bf16),
        [VMEM] * 4,
        (1_000_000, 1_000_000),
        (own1, first1, scale, extra),
    )
    second1 = permuted(sent1, onward)
    out_shape = sds((1, count, VALUES), bf16)
    diagonal1, queries1, known, scale, out = call(
        diagonal_later_kernel,
        diagonal_outs + (sds((16, WIDE), f32), sds((8, VALUES), f32), out_shape),
        [VMEM] * 11,
        (200_000_000, 2_000_000),
        (conv1, key1, raw_queries, edge, across, down, gain, first1, table, gates, diagonal0),
        out_specs=(VMEM, VMEM, VMEM, VMEM, HBM),
        scratch=(pltpu.VMEM((count, VALUES), bf16), pltpu.SemaphoreType.DMA((CHUNKS,))),
    )
    out, out0, base, decay = call(
        finish_first_kernel,
        (
            out_shape,
            sds((count, HALF), bf16),
            sds((ROWS, WIDE), f32),
            sds((8 * PER_CHUNK, WIDE), f32),
        ),
        [VMEM] * 13 + [HBM],
        (50_000_000, 2_000_000),
        (
            first0, first1, second0, early, table, known, gates, scale,
            diagonal0, queries0, diagonal1, queries1, entry, out,
        ),
        out_specs=(HBM, VMEM, VMEM, VMEM),
        scratch=(pltpu.VMEM((count, HALF), bf16), pltpu.SemaphoreType.DMA((2,))),
        aliases={13: 0},
    )
    return call(
        finish_later_kernel,
        out_shape,
        [VMEM] * 7 + [HBM],
        (50_000_000, 2_000_000),
        (second1, base, decay, diagonal1, queries1, entry, out0, out),
        out_specs=HBM,
        scratch=(pltpu.VMEM((count, HALF), bf16), pltpu.SemaphoreType.DMA((PER_CHUNK + 1,))),
        aliases={7: 0},
    )


def shifted(value, axis, steps):
    count = lax.axis_size(axis)
    first, last = (max(0, -steps), min(count, count - steps))
    return lax.ppermute(value, axis, [(source, source + steps) for source in range(first, last)])


def carried_in(array, axis, combine, identity):
    length, index = (lax.axis_size(axis), lax.axis_index(axis))
    everything = jax.tree.map(
        lambda part, kind: lax.all_gather(part.astype(kind), axis),
        array,
        (jnp.bfloat16, jnp.bfloat16),
    )
    start = jax.tree.map(
        lambda part, zero: jnp.broadcast_to(jnp.asarray(zero, part.dtype), part.shape),
        array,
        identity,
    )

    def step(k, before):
        reached = k < index
        new = combine(
            before, jax.tree.map(lambda part, own: part[k].astype(own.dtype), everything, array)
        )
        return jax.tree.map(lambda a, b: jnp.where(reached, a, b), new, before)

    return lax.fori_loop(0, length, step, start)


def convolve(padded, conv_weight, conv_bias, count_rows):
    total = conv_bias.astype(jnp.float32)[None, :]
    for offset in range(conv_weight.shape[0]):
        total = (
            total
            + padded[offset : offset + count_rows].astype(jnp.float32)
            * conv_weight[offset].astype(jnp.float32)[None, :]
        )
    return jax.nn.silu(total).astype(jnp.bfloat16)


def group_terms(values, keys_in, queries, decay_rate, step_rows):
    heads_group = step_rows.shape[0]
    count_rows = step_rows.shape[1]
    values = values.reshape(count_rows, heads_group, -1)
    cumulative = jnp.cumsum(-step_rows * decay_rate[:, None], axis=1)
    scores = jnp.einsum("tn,sn->ts", queries, keys_in, preferred_element_type=jnp.float32)
    later = lax.broadcasted_iota(jnp.int32, (count_rows, count_rows), 0)
    earlier = lax.broadcasted_iota(jnp.int32, (count_rows, count_rows), 1)
    spread = jnp.where(
        (later >= earlier)[None], cumulative[:, :, None] - cumulative[:, None, :], -1e30
    )
    weights = (jnp.exp(spread) * scores[None]).astype(jnp.bfloat16)
    scaled = (values * step_rows.T[:, :, None]).astype(jnp.bfloat16)
    diagonal_part = jnp.einsum("hts,shp->thp", weights, scaled, preferred_element_type=jnp.float32)
    tail_weight = jnp.exp(cumulative[:, -1:] - cumulative)
    written = (values * (step_rows * tail_weight).T[:, :, None]).astype(jnp.bfloat16)
    local_state = jnp.einsum("tn,thp->hpn", keys_in, written, preferred_element_type=jnp.float32)
    return (diagonal_part, local_state, jnp.exp(cumulative[:, -1]), jnp.exp(cumulative), values)


def finish_group(diagonal_part, entry_decay, queries, incoming, values, skip_gain):
    incoming_rounded = incoming.astype(jnp.bfloat16)
    carried_part = jnp.einsum(
        "tn,hpn->thp", queries, incoming_rounded, preferred_element_type=jnp.float32
    )
    carried_part = carried_part * entry_decay.T[:, :, None]
    return diagonal_part + carried_part + skip_gain[None, :, None] * values.astype(jnp.float32)


def combine(earlier, later):
    return (earlier[0] * later[0], later[0][:, None, None] * earlier[1] + later[1])


def shard_far(pre_conv, step_size, lengths, conv_weight, conv_bias, decay_rate, skip_gain):
    count_rows = pre_conv.shape[1]
    kernel_len = conv_weight.shape[0]
    heads_group = HEADS // BC_GROUPS
    position = lax.axis_index("ctx")
    sizes_row = lengths[0]
    starts = jnp.cumsum(sizes_row) - sizes_row
    fresh = jnp.any(starts == position)
    retain = jnp.where(fresh, 0.0, 1.0).astype(jnp.float32)
    own_rows = pre_conv[0]
    previous = shifted(own_rows[count_rows - kernel_len + 1 :], "ctx", 1)
    previous = jnp.where(fresh, jnp.zeros_like(previous), previous)
    convolved = convolve(
        jnp.concatenate([previous, own_rows], axis=0), conv_weight, conv_bias, count_rows
    )
    values = convolved[:, : HEADS * HEAD_DIM]
    keys_all = convolved[:, HEADS * HEAD_DIM : HEADS * HEAD_DIM + BC_GROUPS * STATE]
    queries_all = convolved[:, HEADS * HEAD_DIM + BC_GROUPS * STATE :]
    step_rows = step_size[0]
    results = []
    pieces = []
    for bc_group in range(BC_GROUPS):
        low = bc_group * heads_group
        high = low + heads_group
        pieces.append(
            group_terms(
                values[:, low * HEAD_DIM : high * HEAD_DIM],
                keys_all[:, bc_group * STATE : (bc_group + 1) * STATE],
                queries_all[:, bc_group * STATE : (bc_group + 1) * STATE],
                decay_rate[low:high],
                step_rows[low:high],
            )
        )
    decays = jnp.concatenate([piece[2] for piece in pieces], axis=0) * retain
    states = jnp.concatenate([piece[1] for piece in pieces], axis=0)
    identity = (jnp.ones_like(decays), jnp.zeros_like(states))
    totals = carried_in((decays, states), "ctx", combine, identity)
    incoming = totals[1] * retain
    for bc_group in range(BC_GROUPS):
        low = bc_group * heads_group
        high = low + heads_group
        piece = pieces[bc_group]
        results.append(
            finish_group(
                piece[0],
                piece[3],
                queries_all[:, bc_group * STATE : (bc_group + 1) * STATE],
                incoming[low:high],
                piece[4],
                skip_gain[low:high],
            )
        )
    output = (
        jnp.concatenate(results, axis=1).reshape(count_rows, HEADS * HEAD_DIM).astype(jnp.bfloat16)
    )
    return output[None]


def solution(mesh):
    in_specs = (
        P(("groups", "lane"), "ctx", None),
        P(("groups", "lane"), None, "ctx"),
        P(("groups", "lane"), None),
        P(),
        P(),
        P(),
        P(),
    )
    out_specs = P(("groups", "lane"), "ctx", None)
    shards = shard_near if mesh.shape["ctx"] <= 8 else shard_far
    return jax.shard_map(shards, mesh=mesh, in_specs=in_specs, out_specs=out_specs, check_vma=False)
```
